32 devices in a mesh: member: 8 (over y, x, core), tile: 4 (over z).
Axes of the slice: x: 2, y: 2, z: 4, core: 2. Of those that a mesh axis runs over, the one named last changes fastest.
Arguments:
- member_concentration: float32 [16, 4, 128, 256], P('member', None, 'tile'), may hold values from -6 to 6
- courant_pairs: float32 [2, 4, 128, 256], P(None, None, 'tile'), may hold values from -0.4 to 0.4
- obs_cell: int32 [32768], replicated, may hold values from 0 to 131071, as said below
- obs_value: float32 [32768], replicated, may hold values from -6 to 6
- obs_error: float32 [32768], replicated, may hold values from 0.25 to 4
- obs_list: int32 [8, 16, 1024], P('tile', 'member'), may hold values from -1 to 32767, as said below
Outputs:
- analysis: float32 [16, 4, 128, 256], P('member', None, 'tile')
The draws below stay inside these ranges and needn't reach their ends.
Inputs may be any that keep to these rules, and one draw needn't show every extreme that they name: `obs_cell`: observation g lies in rows r * 32 to r * 32 + 31 and columns c * 32 to c * 32 + 31, with r = (g // 1024) % (4) and c = (g // 1024) // 4. `obs_list`: filled slots come first in each list; each list has 1 to 1024 filled slots and some list has exactly 1024; a filled slot names an observation whose region (as for obs_cell) is the patch's own or one of the eight around it, columns wrapping around and rows not.
All inputs are finite; a program needn't handle non-finite values.
Results may differ from the reference program's by a relative error of at most 0.0013.
Values may be sent and summed in bfloat16 or wider, within the bound.
No kernel may reach another device: no remote copies, remote signals or barrier semaphores. Data moves between devices by JAX's collectives and lax.ppermute only.
A program may use at most 128 MiB of HBM per device.

```python
import math
import jax
import jax.numpy as jnp
from jax import lax

M = 16
LEVELS = 4
SIDE = 32
PATCH = 16
LOC_LEN = 16
SLOTS = 1024
OBS_DEV = 1024
NX = 256
NY = 128
NOBS = 32768
PROWS = 8
PCOLS = 16


def draw_obs_cell(key, part):
    key = jax.random.fold_in(key, 11)
    region_rows = NY // SIDE
    number = jnp.arange(NOBS, dtype=jnp.int32)
    region = number // OBS_DEV
    column_block = region // region_rows
    row_block = region % region_rows
    streams = jax.random.split(key, 3)
    level_drawn = jax.random.randint(streams[0], (NOBS,), 0, LEVELS)
    row_drawn = row_block * SIDE + jax.random.randint(streams[1], (NOBS,), 0, SIDE)
    column_drawn = column_block * SIDE + jax.random.randint(streams[2], (NOBS,), 0, SIDE)
    cells = (level_drawn * NY + row_drawn) * NX + column_drawn
    cells = jnp.where(number == NOBS - 1, LEVELS * NY * NX - 1, cells)
    cells = jnp.where(number == 0, 0, cells)
    return cells.astype(jnp.int32)


def draw_obs_list(key, part):
    key = jax.random.fold_in(key, 23)
    region_rows = NY // SIDE
    region_columns = NX // SIDE
    patch_total = PROWS * PCOLS
    streams = jax.random.split(key, 7)
    first_draw = jax.random.randint(streams[0], (patch_total,), 0, SLOTS)
    second_draw = jax.random.randint(streams[1], (patch_total,), 0, SLOTS)
    third_draw = jax.random.randint(streams[2], (patch_total,), 0, SLOTS)
    counts = 1 + first_draw * second_draw // SLOTS * third_draw // SLOTS
    chosen = jax.random.randint(streams[3], (), 0, patch_total)
    numbers = jnp.arange(patch_total, dtype=jnp.int32)
    counts = jnp.where(numbers == chosen, SLOTS, counts)
    home_row = numbers // PCOLS * PATCH // SIDE
    home_column = numbers % PCOLS * PATCH // SIDE
    shift_row = jax.random.randint(streams[4], (patch_total, SLOTS), -1, 2)
    shift_column = jax.random.randint(streams[5], (patch_total, SLOTS), -1, 2)
    near_row = jnp.clip(home_row[:, None] + shift_row, 0, region_rows - 1)
    near_column = (home_column[:, None] + shift_column + region_columns) % region_columns
    within = jax.random.randint(streams[6], (patch_total, SLOTS), 0, OBS_DEV)
    entries = (near_column * region_rows + near_row) * OBS_DEV + within
    entries = entries.at[patch_total - 1, 0].set(NOBS - 1)
    slot_number = jnp.arange(SLOTS, dtype=jnp.int32)
    listed = jnp.where(slot_number[None, :] < counts[:, None], entries, -1)
    return listed.reshape(PROWS, PCOLS, SLOTS).astype(jnp.int32)


def block_scale(own_key, dims, pieces, low, high):
    gain = 1.0
    for position, parts in pieces:
        steps = jax.random.uniform(jax.random.fold_in(jax.random.fold_in(own_key, 6), position), (parts,), jnp.float32, low / len(pieces), high / len(pieces))
        gain = gain * jnp.repeat(jnp.exp(steps), dims[position] // parts).reshape((-1,) + (1,) * (len(dims) - 1 - position))
    return gain


def gaussian(own_key, extent, scale, most, cuts=(), kind=jnp.bfloat16):
    array = jax.random.normal(own_key, extent, jnp.float32) * scale
    if len(cuts) > 0:
        array = block_scale(own_key, extent, cuts, -0.22, 0.18) * array
    return jnp.clip(array, min=-most, max=most).astype(kind)


def setup_inputs(seed: int = 0) -> dict:
    streams_of = jax.random.split(jax.random.key(seed), 7)
    member_concentration = gaussian(streams_of[0], (M, LEVELS, NY, NX), 1.0, 6.0, ((0, 8), (2, 4)), jnp.float32)
    courant_pairs = jnp.clip(jax.random.uniform(streams_of[1], (2, LEVELS, NY, NX), jnp.float32, -0.4, 0.4) * block_scale(streams_of[1], (2, LEVELS, NY, NX), ((2, 4),), -0.4, 0.0), -0.4, 0.4)
    obs_cell = draw_obs_cell(jax.random.fold_in(streams_of[6], 71), 0)
    obs_value = gaussian(streams_of[3], (NOBS,), 1.0, 6.0, (), jnp.float32)
    obs_error = jnp.clip(jnp.exp(jax.random.uniform(streams_of[4], (NOBS,), jnp.float32, math.log(0.25), math.log(4.0))), 0.25, 4.0)
    obs_list = draw_obs_list(jax.random.fold_in(streams_of[6], 71), 0)
    return dict(member_concentration=member_concentration, courant_pairs=courant_pairs, obs_cell=obs_cell, obs_value=obs_value, obs_error=obs_error, obs_list=obs_list)


diffusion = 0.05
highest = lax.Precision.HIGHEST

def update(current, north_rows, south_rows, east_cells, west_cells, courant_pairs):
    meridional = courant_pairs[0]
    zonal_flow = courant_pairs[1]
    advection = jnp.maximum(zonal_flow, 0.0) * (current - west_cells) + jnp.minimum(zonal_flow, 0.0) * (east_cells - current) + jnp.maximum(meridional, 0.0) * (current - south_rows) + jnp.minimum(meridional, 0.0) * (north_rows - current)
    return current - advection + diffusion * (north_rows + south_rows + east_cells + west_cells - 4.0 * current)

def transport_concentration(current, courant_pairs):
    blank_row = jnp.zeros_like(current[:, :, :1, :])
    north_rows = jnp.concatenate([current[:, :, 1:, :], blank_row], axis=2)
    south_rows = jnp.concatenate([blank_row, current[:, :, :-1, :]], axis=2)
    east_cells = jnp.roll(current, -1, axis=3)
    west_cells = jnp.roll(current, 1, axis=3)
    return update(current, north_rows, south_rows, east_cells, west_cells, courant_pairs)

def localize(cells, patch_row, patch_column, variance, grid_height, grid_width):
    cell_row = cells // grid_width % grid_height
    column_of_cell = cells % grid_width
    row_gap = (cell_row - patch_row * PATCH - PATCH // 2).astype(jnp.float32) + 0.5
    column_gap = ((column_of_cell - patch_column * PATCH - PATCH // 2 + grid_width // 2) % grid_width - grid_width // 2).astype(jnp.float32) + 0.5
    return jnp.exp(-(row_gap * row_gap + column_gap * column_gap) / (2.0 * LOC_LEN * LOC_LEN)) / variance

def accumulate(spread, innovation, weight):
    scaled = spread * weight[:, None, :]
    system_terms = jnp.einsum('pms,pns->pmn', scaled, spread, precision=highest)
    forcing = jnp.einsum('pms,ps->pm', scaled, innovation, precision=highest)
    return (system_terms, forcing)

def solve_lower(factor):
    identity = jnp.eye(factor.shape[0], dtype=jnp.float32)
    return jax.scipy.linalg.solve_triangular(factor, identity, lower=True)

def transform(system_terms, forcing, ensemble_size):
    identity = jnp.eye(ensemble_size, dtype=jnp.float32)
    lower_factor = jnp.linalg.cholesky(system_terms + (ensemble_size - 1.0) * identity)
    inverse = jax.vmap(solve_lower)(lower_factor)
    inner = jnp.einsum('pij,pj->pi', inverse, forcing, precision=highest)
    mean_weight = jnp.einsum('pji,pj->pi', inverse, inner, precision=highest)
    spread_weight = jnp.sqrt(ensemble_size - 1.0) * jnp.swapaxes(inverse, 1, 2)
    return mean_weight[:, :, None] + spread_weight - identity

def reference(member_concentration, courant_pairs, obs_cell, obs_value, obs_error, obs_list):
    predicted_ensemble = member_concentration
    for repeat in range(2):
        predicted_ensemble = transport_concentration(predicted_ensemble, courant_pairs)
    common_arrays = predicted_ensemble.astype(jnp.bfloat16)
    ensemble = common_arrays.astype(jnp.float32)
    centred = ensemble - lax.optimization_barrier(jnp.mean(ensemble, axis=0))
    observed = common_arrays.reshape(M, LEVELS * NY * NX)[:, obs_cell].astype(jnp.float32)
    obs_mean = lax.optimization_barrier(jnp.mean(observed, axis=0))
    obs_spread = observed - obs_mean
    innovation = obs_value - obs_mean
    blocks = centred.reshape(M, LEVELS, PROWS, PATCH, PCOLS, PATCH)
    columns_here = jnp.arange(PCOLS, dtype=jnp.int32)[:, None]

    def one_row(inputs):
        row_number, row_lists, row_blocks = inputs
        valid = row_lists >= 0
        safe = jnp.where(valid, row_lists, 0)
        spread = jnp.moveaxis(obs_spread[:, safe], 0, 1)
        weight = jnp.where(valid, localize(obs_cell[safe], row_number, columns_here, obs_error[safe], NY, NX), 0.0)
        system_terms, forcing = accumulate(spread, innovation[safe], weight)
        trans = transform(system_terms, forcing, M)
        local = jnp.transpose(row_blocks, (3, 0, 1, 2, 4)).reshape(PCOLS, M, LEVELS * PATCH * PATCH)
        change = jnp.einsum('pjk,pjc->pkc', trans, local, precision=highest)
        return change.astype(jnp.bfloat16)
    changes = lax.map(one_row, (jnp.arange(PROWS, dtype=jnp.int32), obs_list, jnp.moveaxis(blocks, 2, 0)))
    changes = changes.reshape(PROWS, PCOLS, M, LEVELS, PATCH, PATCH)
    assimilation_correction = jnp.transpose(changes, (2, 3, 0, 4, 1, 5)).reshape(M, LEVELS, NY, NX)
    return predicted_ensemble + assimilation_correction.astype(jnp.float32)
```

```python
import functools

import jax
import jax.numpy as jnp
from jax import lax
from jax.experimental import pallas as pl
from jax.experimental.pallas import tpu as pltpu
from jax.sharding import PartitionSpec as P

PATCH = 16
LOC_LEN = 16
DIFFUSION = 0.05
LANES = 128
BLOCK = 8

f32 = jnp.float32
bf16 = jnp.bfloat16


def call(body, outs, scratch=(), flops=1_000_000, moved=1_000_000):
    return pl.pallas_call(
        body,
        out_shape=[jax.ShapeDtypeStruct(shape, kind) for shape, kind in outs],
        scratch_shapes=list(scratch),
        compiler_params=pltpu.CompilerParams(vmem_limit_bytes=48 * 1024 * 1024),
        cost_estimate=pl.CostEstimate(flops=flops, bytes_accessed=moved, transcendentals=0),
    )


def split(number, size):
    if size & (size - 1) == 0:
        return number >> (size.bit_length() - 1), number & (size - 1)
    quotient = number // size
    return quotient, number - quotient * size


def wrapped(number, size):
    if size & (size - 1) == 0:
        return number & (size - 1)
    return lax.rem(number + size, size)


def iota(shape, axis):
    return lax.broadcasted_iota(jnp.int32, shape, axis)


def pick_lanes(values, index):
    rows = [
        jnp.take_along_axis(values[r : r + BLOCK], index, axis=1, mode="promise_in_bounds")
        for r in range(0, values.shape[0], BLOCK)
    ]
    return rows[0] if len(rows) == 1 else jnp.concatenate(rows, axis=0)


def transpose_chunks(parts):
    lane = iota(parts[0].shape, 1)
    low = lane < 64
    even = (lane & 32) == 0
    parts = list(parts)
    for i in (0, 1):
        a, b = parts[i], parts[i + 2]
        parts[i] = jnp.where(low, a, pltpu.roll(b, 64, 1))
        parts[i + 2] = jnp.where(low, pltpu.roll(a, 64, 1), b)
    for i in (0, 2):
        a, b = parts[i], parts[i + 1]
        parts[i] = jnp.where(even, a, pltpu.roll(b, 32, 1))
        parts[i + 1] = jnp.where(even, pltpu.roll(a, 96, 1), b)
    return parts


def pack_edges(tracer, courant, lists, to_south, to_north):
    members, levels, side, width = tracer.shape
    for b in range(members):
        for l in range(levels):
            row = b * levels + l
            to_south[row : row + 1, :] = tracer[b, l, 0:1, :]
            to_south[8 + row : 9 + row, :] = tracer[b, l, 1:2, :]
            to_north[row : row + 1, :] = tracer[b, l, side - 1 : side, :]
            to_north[8 + row : 9 + row, :] = tracer[b, l, side - 2 : side - 1, :]
    for c in range(2):
        for l in range(levels):
            row = 16 + c * levels + l
            to_south[row : row + 1, :] = courant[c, l, 0:1, :]
            to_north[row : row + 1, :] = courant[c, l, side - 1 : side, :]
    row = 24
    for a in range(lists.shape[0]):
        for b in range(lists.shape[1]):
            for s in range(0, lists.shape[2], width):
                part = lists[a, b : b + 1, s : s + width].astype(f32)
                to_south[row : row + 1, :] = part
                to_north[row : row + 1, :] = part
                row += 1


def coefficients(meridional, zonal):
    return (
        (1.0 - 4.0 * DIFFUSION) - jnp.abs(zonal) - jnp.abs(meridional),
        DIFFUSION + jnp.maximum(zonal, 0.0),
        DIFFUSION - jnp.minimum(zonal, 0.0),
        DIFFUSION + jnp.maximum(meridional, 0.0),
        DIFFUSION - jnp.minimum(meridional, 0.0),
    )


def stencil(current, south, north, factors):
    width = current.shape[1]
    centre, from_west, from_east, from_south, from_north = factors
    west = pltpu.roll(current, 1, 1)
    east = pltpu.roll(current, width - 1, 1)
    return (
        centre * current
        + from_west * west
        + from_east * east
        + from_south * south
        + from_north * north
    )


def forecast_body(
    tracer, courant, own_south, own_north, south, north, cell, forecast, send, table, *, tiles, height
):
    members, levels, side, width = tracer.shape
    blocks = width // side
    tile = lax.axis_index("tile")
    planes = members * levels

    def edge(own, other):
        twice = lambda first: jnp.concatenate([other[first : first + levels, :]] * members, axis=0)
        return coefficients(twice(16), twice(16 + levels))

    below = stencil(
        south[0:planes, :], south[8 : 8 + planes, :], own_south[0:planes, :], edge(own_south, south)
    )
    above = stencil(
        north[0:planes, :], own_north[0:planes, :], north[8 : 8 + planes, :], edge(own_north, north)
    )
    below = jnp.where(tile == 0, 0.0, below)
    above = jnp.where(tile == tiles - 1, 0.0, above)
    row = iota((side, width), 0)
    for l in range(levels):
        factors = coefficients(courant[0, l], courant[1, l])
        for b in range(members):
            plane = b * levels + l
            current = tracer[b, l]
            for low, high in (
                (south[plane : plane + 1, :], north[plane : plane + 1, :]),
                (below[plane : plane + 1, :], above[plane : plane + 1, :]),
            ):
                lower = jnp.where(row == 0, low, pltpu.roll(current, 1, 0))
                upper = jnp.where(row == side - 1, high, pltpu.roll(current, side - 1, 0))
                current = stencil(current, lower, upper, factors)
            forecast[b, l] = current

    region_rows = planes * BLOCK
    for q in range(width // LANES):
        parts = [
            forecast[:, :, r : r + BLOCK, q * LANES : (q + 1) * LANES].reshape(region_rows, LANES)
            for r in range(0, side, BLOCK)
        ]
        for c, part in enumerate(transpose_chunks(parts)):
            rounded = part.astype(bf16)
            send[4 * q + c, 0:region_rows, :] = rounded
            table[4 * q + c] = rounded.astype(f32)

    hits = levels * BLOCK
    observed = []
    first = pl.multiple_of(tile * BLOCK, BLOCK)
    for c in range(blocks):
        cells = cell[c, pl.ds(first, BLOCK), :]
        above_row, column = split(cells, width)
        level, grid_row = split(above_row, height)
        _, local_row = split(grid_row, side)
        _, local_column = split(column, side)
        band, sub_row = split(local_row, BLOCK)
        high = level * BLOCK + sub_row
        low = band * side + local_column
        mine = [jnp.zeros((BLOCK, LANES), f32) for _ in range(members)]
        for h in range(hits):
            here = high == h
            for b in range(members):
                line = table[c, b * hits + h : b * hits + h + 1, :]
                line = jnp.broadcast_to(line, (BLOCK, LANES))
                mine[b] = jnp.where(here, pick_lanes(line, low), mine[b])
        observed.append(mine)
    for c in range(blocks):
        rows = [
            observed[(c + r - 1) % blocks][b] for b in range(members) for r in range(3)
        ]
        for i in range(0, len(rows), 2):
            at = region_rows + i * BLOCK
            send[c, at : at + 2 * BLOCK, :] = jnp.concatenate(rows[i : i + 2], axis=0).astype(bf16)


def weights_body(
    lists, south, north, cell, value, variance, weights, values, planes, *, tiles, blocks, height, width, side
):
    tile = lax.axis_index("tile")
    block = lax.axis_index("member")
    per_side = side // PATCH
    patches = per_side * per_side
    slots = lists.shape[2]
    sub = slots // LANES
    depth = 3 * BLOCK
    rows, columns, sizes = [], [], []
    for r in range(3):
        column_block = wrapped(block + (r - 1), blocks)
        first = pl.multiple_of((column_block * tiles + tile) * BLOCK, BLOCK)
        cells = cell[pl.ds(first, BLOCK), :]
        above_row, column = split(cells, width)
        _, grid_row = split(above_row, height)
        rows.append(grid_row)
        columns.append(column)
        sizes.append(variance[pl.ds(first, BLOCK), :])
        values[r * BLOCK : (r + 1) * BLOCK, :] = value[pl.ds(first, BLOCK), :]
    grid_row = jnp.concatenate(rows, axis=0)
    column = jnp.concatenate(columns, axis=0)
    size = jnp.concatenate(sizes, axis=0)

    def pieces(dt, p):
        if dt == 0:
            return [lists[p // per_side, p % per_side : p % per_side + 1, :]]
        source = south if dt < 0 else north
        each = slots // width
        return [
            source[24 + p * each + i : 25 + p * each + i, :].astype(jnp.int32) for i in range(each)
        ]

    index = 0
    for dt in (0, -1, 1):
        for p in range(patches):
            count = jnp.zeros((depth, LANES), f32)
            for part in pieces(dt, p):
                length = part.shape[1]
                region, within = split(part, BLOCK * LANES)
                region_column, region_row = split(region, tiles)
                line, lane = split(within, LANES)
                near = wrapped(region_column - block + 1, blocks)
                fits = (part >= 0) & (region_row == tile) & (near < 3)
                line = jnp.where(fits, near * BLOCK + line, -1)
                one = (iota((depth, length), 0) == line).astype(f32).astype(bf16)
                other = (iota((LANES, length), 0) == lane).astype(f32).astype(bf16)
                count += lax.dot_general(
                    one, other, (((1,), (1,)), ((), ())), preferred_element_type=f32
                )
            patch_row = (tile + dt) * per_side + p // per_side
            patch_column = block * per_side + p % per_side
            row_gap = (grid_row - patch_row * PATCH - PATCH // 2).astype(f32) + 0.5
            turned = column - patch_column * PATCH - PATCH // 2 + width // 2
            column_gap = (wrapped(turned, width) - width // 2).astype(f32) + 0.5
            near = jnp.exp(
                -(row_gap * row_gap + column_gap * column_gap) / (2.0 * LOC_LEN * LOC_LEN)
            )
            planes[index * depth : (index + 1) * depth, :] = count * (near / size)
            index += 1
    for extra in range(index, 16):
        planes[extra * depth : (extra + 1) * depth, :] = jnp.zeros((depth, LANES), f32)
    for i in range(depth):
        weights[:, i * LANES : (i + 1) * LANES] = planes[pl.ds(i, 16, stride=depth), :]


def halves(values):
    high = values.astype(bf16)
    return high, (values - high.astype(f32)).astype(bf16)


def dot_rows(left, right):
    return lax.dot_general(left, right, (((1,), (1,)), ((), ())), preferred_element_type=f32)


def systems_body(
    received, weights, values, own, to_south, to_north, planes, tall_high, tall_low, wide_high, wide_low, *, patches
):
    sources, all_rows, _ = received.shape
    depth = 3 * BLOCK
    region_rows = own_rows(received)
    members = (all_rows - region_rows) // depth
    ensemble = sources * members
    total = jnp.zeros((depth, LANES), f32)
    for s in range(sources):
        both = received[s, region_rows:all_rows, :].astype(f32)
        planes[s * members * depth : (s + 1) * members * depth, :] = both
        for b in range(members):
            total += both[b * depth : (b + 1) * depth, :]
    mean = total / ensemble
    for k in range(ensemble):
        planes[k * depth : (k + 1) * depth, :] -= mean
    planes[ensemble * depth : (ensemble + 1) * depth, :] = values[...] - mean
    for k in range(ensemble + 1, ensemble + 8):
        planes[k * depth : (k + 1) * depth, :] = jnp.zeros((depth, LANES), f32)
    for i in range(depth):
        at = slice(i * LANES, (i + 1) * LANES)
        tile = planes[pl.ds(i, ensemble + 8, stride=depth), :]
        high, low = halves(tile)
        wide_high[:, at] = high
        wide_low[:, at] = low
        spread = tile[0:ensemble, :]
        for p in range(3 * patches):
            high, low = halves(spread * weights[p : p + 1, at])
            tall_high[p * ensemble : (p + 1) * ensemble, at] = high
            tall_low[p * ensemble : (p + 1) * ensemble, at] = low
    result = (
        dot_rows(wide_high[...], tall_high[...])
        + dot_rows(wide_low[...], tall_high[...])
        + dot_rows(wide_high[...], tall_low[...])
    )
    count = patches * ensemble // 64
    for n in range(3 * count):
        target = (own, to_south, to_north)[n // count]
        at = n % count
        piece = result[:, n // 2 * LANES : (n // 2 + 1) * LANES] if n // 2 * LANES + LANES <= result.shape[1] else None
        if piece is None:
            piece = jnp.concatenate([result[:, n * 64 :], jnp.zeros((ensemble + 8, 64), f32)], axis=1)
        else:
            if n % 2:
                piece = pltpu.roll(piece, 64, 1)
            piece = jnp.where(iota(piece.shape, 1) < 64, piece, 0.0)
        target[:, at * LANES : (at + 1) * LANES] = piece


def own_rows(received):
    return 64


def analysis_body(received, own, south, north, send, centred, factors, *, patches):
    sources, all_rows, _ = received.shape
    region_rows = own_rows(received)
    members = send.shape[1] * sources // received.shape[0] // (region_rows // 2)
    ensemble = sources * members
    hits = region_rows // members
    total = jnp.zeros((hits, LANES), f32)
    for s in range(sources):
        part = received[s, 0:region_rows, :].astype(f32)
        for b in range(members):
            one = part[b * hits : (b + 1) * hits, :]
            centred[s * members + b] = one
            total += one
    mean = total / ensemble
    for k in range(ensemble):
        centred[k] -= mean

    count = patches * ensemble // 64
    group = 64 // ensemble
    row = iota((ensemble + 8, LANES), 0)
    lane = iota((ensemble + 8, LANES), 1)
    within = lane & (ensemble - 1)
    start = jnp.where(
        (row == within) & (row < ensemble), jnp.where(lane < 64, ensemble - 1.0, 1.0), 0.0
    )
    lane8 = iota((BLOCK, LANES), 1)
    group_start = (lane8 & 63) & ~(ensemble - 1)
    transforms = []
    for i in range(count):
        at = slice(i * LANES, (i + 1) * LANES)
        state = own[:, at] + south[:, at] + north[:, at] + start
        pivots = jnp.ones((ensemble, LANES), f32)
        for k in range(ensemble):
            column = pick_lanes(state, group_start + k)
            pivot = column[k : k + 1, :]
            scaled = state[k : k + 1, :] / pivot
            state = state - jnp.where(row > k, column, 0.0) * scaled
            pivots = jnp.where(row[0:ensemble] == k, pivot, pivots)
        inverse = state[0:ensemble, :] * lax.rsqrt(pivots)
        mean_weight = -state[ensemble : ensemble + 1, :]
        unit = jnp.where(row[0:ensemble] == within[0:ensemble], 1.0, 0.0)
        transforms.append(mean_weight + (ensemble - 1.0) ** 0.5 * inverse - unit)

    side_lanes = 32
    patch = (lane8 // (2 * side_lanes)) * 2 + (lane8 & (side_lanes - 1)) // PATCH
    inside = 64 + (patch & (group - 1)) * ensemble if group > 1 else 64 + 0 * patch
    which = patch // group
    for j in range(ensemble):
        chosen = pick_lanes(transforms[0], inside + j)
        for i in range(1, count):
            other = pick_lanes(transforms[i], inside + j)
            chosen = jnp.where(jnp.broadcast_to(which[0:1] == i, chosen.shape), other, chosen)
        factors[j] = chosen

    def one_destination(d, _):
        totals = [jnp.zeros((hits, LANES), f32) for _ in range(members)]
        for j in range(ensemble):
            block = centred[j]
            for b in range(members):
                totals[b] += factors[j, pl.ds(d * members + b, 1), :] * block
        send[d] = jnp.concatenate(totals, axis=0).astype(bf16)
        return 0

    lax.fori_loop(0, sources, one_destination, 0)


def output_body(forecast, received, analysis):
    members, levels, side, width = forecast.shape
    for q in range(width // LANES):
        parts = [received[4 * q + c].astype(f32) for c in range(4)]
        at = slice(q * LANES, (q + 1) * LANES)
        for r, part in enumerate(transpose_chunks(parts)):
            rows = slice(r * BLOCK, (r + 1) * BLOCK)
            analysis[:, :, rows, at] = forecast[:, :, rows, at] + part.reshape(
                members, levels, BLOCK, LANES
            )


def shards(member_concentration, courant_pairs, obs_cell, obs_value, obs_error, obs_list):
    members, levels, side, width = member_concentration.shape
    blocks = lax.axis_size("member")
    tiles = lax.axis_size("tile")
    height = side * tiles
    ensemble = members * blocks
    per_side = side // PATCH
    patches = per_side * per_side
    slots = obs_list.shape[2]
    region_rows = members * levels * BLOCK
    depth = 3 * BLOCK
    all_rows = region_rows + members * depth
    edge_rows = -(-(24 + patches * slots // width) // 8) * 8

    to_south, to_north = call(pack_edges, [((edge_rows, width), f32)] * 2)(
        member_concentration, courant_pairs, obs_list
    )
    up = [(i, i + 1) for i in range(tiles - 1)]
    down = [(i + 1, i) for i in range(tiles - 1)]
    south = lax.ppermute(to_north, "tile", up)
    north = lax.ppermute(to_south, "tile", down)

    flat = lambda array: array.reshape(-1, LANES)
    cell = flat(obs_cell)
    forecast, send = call(
        functools.partial(forecast_body, tiles=tiles, height=height),
        [(member_concentration.shape, f32), ((blocks, all_rows, LANES), bf16)],
        [pltpu.VMEM((blocks, region_rows, LANES), f32)],
    )(
        member_concentration,
        courant_pairs,
        to_south,
        to_north,
        south,
        north,
        cell.reshape(blocks, tiles * BLOCK, LANES),
    )
    received = lax.all_to_all(send, "member", split_axis=0, concat_axis=0, tiled=True)
    weights, values = call(
        functools.partial(
            weights_body, tiles=tiles, blocks=blocks, height=height, width=width, side=side
        ),
        [((16, depth * LANES), f32), ((depth, LANES), f32)],
        [pltpu.VMEM((16 * depth, LANES), f32)],
        flops=100_000_000,
    )(obs_list, south, north, cell, flat(obs_value), flat(obs_error))

    tall = 3 * patches * ensemble
    system_shape = (ensemble + 8, patches * ensemble // 64 * LANES)
    own, for_south, for_north = call(
        functools.partial(systems_body, patches=patches),
        [(system_shape, f32)] * 3,
        [
            pltpu.VMEM(((ensemble + 8) * depth, LANES), f32),
            pltpu.VMEM((tall, depth * LANES), bf16),
            pltpu.VMEM((tall, depth * LANES), bf16),
            pltpu.VMEM((ensemble + 8, depth * LANES), bf16),
            pltpu.VMEM((ensemble + 8, depth * LANES), bf16),
        ],
    )(received, weights, values)
    from_south = lax.ppermute(for_north, "tile", up)
    from_north = lax.ppermute(for_south, "tile", down)

    (change,) = call(
        functools.partial(analysis_body, patches=patches),
        [((blocks, region_rows, LANES), bf16)],
        [
            pltpu.VMEM((ensemble, levels * BLOCK, LANES), f32),
            pltpu.VMEM((ensemble, ensemble, LANES), f32),
        ],
    )(received, own, from_south, from_north)
    returned = lax.all_to_all(change, "member", split_axis=0, concat_axis=0, tiled=True)
    (analysis,) = call(output_body, [(forecast.shape, f32)])(forecast, returned)
    return analysis


def solution(mesh):
    return jax.shard_map(
        shards,
        mesh=mesh,
        in_specs=(
            P("member", None, "tile", None),
            P(None, None, "tile", None),
            P(),
            P(),
            P(),
            P("tile", "member", None),
        ),
        out_specs=P("member", None, "tile", None),
        check_vma=False,
    )
```

```python
import functools

import jax
import jax.numpy as jnp
from jax import lax
from jax.experimental import pallas as pl
from jax.experimental.pallas import tpu as pltpu
from jax.sharding import PartitionSpec as P

PATCH = 16
LOC_LEN = 16
DIFFUSION = 0.05
LANES = 128
BLOCK = 8

f32 = jnp.float32
bf16 = jnp.bfloat16


def call(body, outs, scratch=(), flops=1_000_000, moved=1_000_000, specs=None):
    specs = {} if specs is None else {"in_specs": specs}
    return pl.pallas_call(
        body,
        **specs,
        out_shape=[jax.ShapeDtypeStruct(shape, kind) for shape, kind in outs],
        scratch_shapes=list(scratch),
        compiler_params=pltpu.CompilerParams(vmem_limit_bytes=48 * 1024 * 1024),
        cost_estimate=pl.CostEstimate(flops=flops, bytes_accessed=moved, transcendentals=0),
    )


def split(number, size):
    if size & (size - 1) == 0:
        return number >> (size.bit_length() - 1), number & (size - 1)
    quotient = number // size
    return quotient, number - quotient * size


def wrapped(number, size):
    if size & (size - 1) == 0:
        return number & (size - 1)
    return lax.rem(number + size, size)


def iota(shape, axis):
    return lax.broadcasted_iota(jnp.int32, shape, axis)


def pick_lanes(values, index):
    rows = [
        jnp.take_along_axis(values[r : r + BLOCK], index, axis=1, mode="promise_in_bounds")
        for r in range(0, values.shape[0], BLOCK)
    ]
    return rows[0] if len(rows) == 1 else jnp.concatenate(rows, axis=0)


def transpose_chunks(parts):
    lane = iota(parts[0].shape, 1)
    low = lane < 64
    even = (lane & 32) == 0
    parts = list(parts)
    for i in (0, 1):
        a, b = parts[i], parts[i + 2]
        parts[i] = jnp.where(low, a, pltpu.roll(b, 64, 1))
        parts[i + 2] = jnp.where(low, pltpu.roll(a, 64, 1), b)
    for i in (0, 2):
        a, b = parts[i], parts[i + 1]
        parts[i] = jnp.where(even, a, pltpu.roll(b, 32, 1))
        parts[i + 1] = jnp.where(even, pltpu.roll(a, 96, 1), b)
    return parts


def pack_edges(tracer, courant, lists, edges, first, last, first_rates, last_rates, numbers, arrived):
    members, levels, side, width = tracer.shape
    copies = [
        pltpu.make_async_copy(source, target, arrived.at[i])
        for i, (source, target) in enumerate(
            (
                (tracer.at[:, :, 0:BLOCK, :], first),
                (tracer.at[:, :, side - BLOCK : side, :], last),
                (courant.at[:, :, 0:BLOCK, :], first_rates),
                (courant.at[:, :, side - BLOCK : side, :], last_rates),
                (lists, numbers),
            )
        )
    ]
    for copy in copies:
        copy.start()
    for copy in copies:
        copy.wait()
    for b in range(members):
        for l in range(levels):
            row = b * levels + l
            edges[row : row + 1, :] = first[b, l, 0:1, :]
            edges[8 + row : 9 + row, :] = first[b, l, 1:2, :]
            edges[24 + row : 25 + row, :] = last[b, l, BLOCK - 1 : BLOCK, :]
            edges[32 + row : 33 + row, :] = last[b, l, BLOCK - 2 : BLOCK - 1, :]
    for c in range(2):
        for l in range(levels):
            row = c * levels + l
            edges[16 + row : 17 + row, :] = first_rates[c, l, 0:1, :]
            edges[40 + row : 41 + row, :] = last_rates[c, l, BLOCK - 1 : BLOCK, :]
    row = 48
    for a in range(numbers.shape[0]):
        for b in range(numbers.shape[1]):
            for s in range(0, numbers.shape[2], width):
                edges[row : row + 1, :] = numbers[a, b : b + 1, s : s + width].astype(f32)
                row += 1


def coefficients(meridional, zonal):
    return (
        (1.0 - 4.0 * DIFFUSION) - jnp.abs(zonal) - jnp.abs(meridional),
        DIFFUSION + jnp.maximum(zonal, 0.0),
        DIFFUSION - jnp.minimum(zonal, 0.0),
        DIFFUSION + jnp.maximum(meridional, 0.0),
        DIFFUSION - jnp.minimum(meridional, 0.0),
    )


def stencil(current, south, north, factors):
    width = current.shape[1]
    centre, from_west, from_east, from_south, from_north = factors
    west = pltpu.roll(current, 1, 1)
    east = pltpu.roll(current, width - 1, 1)
    return (
        centre * current
        + from_west * west
        + from_east * east
        + from_south * south
        + from_north * north
    )


def beside(gathered, tile, tiles):
    south = gathered.at[jnp.maximum(tile - 1, 0)]
    north = gathered.at[jnp.minimum(tile + 1, tiles - 1)]
    return south, north


def forecast_body(tracer, courant, edges, cell, forecast, send, table, *, tiles, height):
    members, levels, side, width = tracer.shape
    blocks = width // side
    tile = lax.axis_index("tile")
    planes = members * levels

    south, north = beside(edges, tile, tiles)
    inside_south, inside_north = tile > 0, tile < tiles - 1
    low = jnp.where(inside_south, south[24 : 24 + planes, :], 0.0)
    lowest = south[32 : 32 + planes, :]
    high = jnp.where(inside_north, north[0:planes, :], 0.0)
    highest = north[8 : 8 + planes, :]

    def edge(source, row):
        twice = lambda first: jnp.concatenate([source[first : first + levels, :]] * members, axis=0)
        return coefficients(twice(row), twice(row + levels))

    below = stencil(low, lowest, edges[tile, 0:planes, :], edge(south, 40))
    above = stencil(high, edges[tile, 24 : 24 + planes, :], highest, edge(north, 16))
    below = jnp.where(inside_south, below, 0.0)
    above = jnp.where(inside_north, above, 0.0)
    row = iota((side, width), 0)
    for l in range(levels):
        factors = coefficients(courant[0, l], courant[1, l])
        for b in range(members):
            plane = b * levels + l
            current = tracer[b, l]
            for under, over in ((low, high), (below, above)):
                under, over = under[plane : plane + 1, :], over[plane : plane + 1, :]
                lower = jnp.where(row == 0, under, pltpu.roll(current, 1, 0))
                upper = jnp.where(row == side - 1, over, pltpu.roll(current, side - 1, 0))
                current = stencil(current, lower, upper, factors)
            forecast[b, l] = current

    region_rows = planes * BLOCK
    for q in range(width // LANES):
        parts = [
            forecast[:, :, r : r + BLOCK, q * LANES : (q + 1) * LANES].reshape(region_rows, LANES)
            for r in range(0, side, BLOCK)
        ]
        for c, part in enumerate(transpose_chunks(parts)):
            rounded = part.astype(bf16)
            send[4 * q + c, 0:region_rows, :] = rounded
            table[4 * q + c] = rounded.astype(f32)

    hits = levels * BLOCK
    observed = []
    first = pl.multiple_of(tile * BLOCK, BLOCK)
    for c in range(blocks):
        cells = cell[c, pl.ds(first, BLOCK), :]
        above_row, column = split(cells, width)
        level, grid_row = split(above_row, height)
        _, local_row = split(grid_row, side)
        _, local_column = split(column, side)
        band, sub_row = split(local_row, BLOCK)
        high = level * BLOCK + sub_row
        low = band * side + local_column
        mine = [jnp.zeros((BLOCK, LANES), f32) for _ in range(members)]
        for h in range(hits):
            here = high == h
            for b in range(members):
                line = table[c, b * hits + h : b * hits + h + 1, :]
                line = jnp.broadcast_to(line, (BLOCK, LANES))
                mine[b] = jnp.where(here, pick_lanes(line, low), mine[b])
        observed.append(mine)
    for c in range(blocks):
        rows = [
            observed[(c + r - 1) % blocks][b] for b in range(members) for r in range(3)
        ]
        for i in range(0, len(rows), 2):
            at = region_rows + i * BLOCK
            send[c, at : at + 2 * BLOCK, :] = jnp.concatenate(rows[i : i + 2], axis=0).astype(bf16)


def weights_body(
    lists, edges, cell, value, variance, weights, values, planes, *, tiles, blocks, height, width, side
):
    tile = lax.axis_index("tile")
    block = lax.axis_index("member")
    south, north = beside(edges, tile, tiles)
    per_side = side // PATCH
    patches = per_side * per_side
    slots = lists.shape[2]
    depth = 3 * BLOCK
    rows, columns, sizes = [], [], []
    for r in range(3):
        column_block = wrapped(block + (r - 1), blocks)
        first = pl.multiple_of((column_block * tiles + tile) * BLOCK, BLOCK)
        cells = cell[pl.ds(first, BLOCK), :]
        above_row, column = split(cells, width)
        _, grid_row = split(above_row, height)
        rows.append(grid_row)
        columns.append(column)
        sizes.append(variance[pl.ds(first, BLOCK), :])
        values[r * BLOCK : (r + 1) * BLOCK, :] = value[pl.ds(first, BLOCK), :]
    grid_row = jnp.concatenate(rows, axis=0)
    column = jnp.concatenate(columns, axis=0)
    size = jnp.concatenate(sizes, axis=0)

    def pieces(dt, p):
        if dt == 0:
            return [lists[p // per_side, p % per_side : p % per_side + 1, :]]
        source = south if dt < 0 else north
        each = slots // width
        return [
            source[48 + p * each + i : 49 + p * each + i, :].astype(jnp.int32) for i in range(each)
        ]

    index = 0
    for dt in (0, -1, 1):
        for p in range(patches):
            count = jnp.zeros((depth, LANES), f32)
            for part in pieces(dt, p):
                length = part.shape[1]
                region, within = split(part, BLOCK * LANES)
                region_column, region_row = split(region, tiles)
                line, lane = split(within, LANES)
                near = wrapped(region_column - block + 1, blocks)
                fits = (part >= 0) & (region_row == tile) & (near < 3)
                line = jnp.where(fits, near * BLOCK + line, -1)
                one = (iota((depth, length), 0) == line).astype(f32).astype(bf16)
                other = (iota((LANES, length), 0) == lane).astype(f32).astype(bf16)
                count += lax.dot_general(
                    one, other, (((1,), (1,)), ((), ())), preferred_element_type=f32
                )
            patch_row = (tile + dt) * per_side + p // per_side
            patch_column = block * per_side + p % per_side
            row_gap = (grid_row - patch_row * PATCH - PATCH // 2).astype(f32) + 0.5
            turned = column - patch_column * PATCH - PATCH // 2 + width // 2
            column_gap = (wrapped(turned, width) - width // 2).astype(f32) + 0.5
            near = jnp.exp(
                -(row_gap * row_gap + column_gap * column_gap) / (2.0 * LOC_LEN * LOC_LEN)
            )
            planes[index * depth : (index + 1) * depth, :] = count * (near / size)
            index += 1
    for extra in range(index, 16):
        planes[extra * depth : (extra + 1) * depth, :] = jnp.zeros((depth, LANES), f32)
    for i in range(depth):
        weights[:, i * LANES : (i + 1) * LANES] = planes[pl.ds(i, 16, stride=depth), :]


def halves(values):
    high = values.astype(bf16)
    return high, (values - high.astype(f32)).astype(bf16)


def dot_rows(left, right):
    return lax.dot_general(left, right, (((1,), (1,)), ((), ())), preferred_element_type=f32)


def systems_body(
    received, weights, values, own, others, planes, tall_high, tall_low, wide_high, wide_low, *, patches
):
    sources, all_rows, _ = received.shape
    depth = 3 * BLOCK
    region_rows = own_rows(received)
    members = (all_rows - region_rows) // depth
    ensemble = sources * members
    total = jnp.zeros((depth, LANES), f32)
    for s in range(sources):
        both = received[s, region_rows:all_rows, :].astype(f32)
        planes[s * members * depth : (s + 1) * members * depth, :] = both
        for b in range(members):
            total += both[b * depth : (b + 1) * depth, :]
    mean = total / ensemble
    for k in range(ensemble):
        planes[k * depth : (k + 1) * depth, :] -= mean
    planes[ensemble * depth : (ensemble + 1) * depth, :] = values[...] - mean
    for k in range(ensemble + 1, ensemble + 8):
        planes[k * depth : (k + 1) * depth, :] = jnp.zeros((depth, LANES), f32)
    for i in range(depth):
        at = slice(i * LANES, (i + 1) * LANES)
        tile = planes[pl.ds(i, ensemble + 8, stride=depth), :]
        high, low = halves(tile)
        wide_high[:, at] = high
        wide_low[:, at] = low
        spread = tile[0:ensemble, :]
        for p in range(3 * patches):
            high, low = halves(spread * weights[p : p + 1, at])
            tall_high[p * ensemble : (p + 1) * ensemble, at] = high
            tall_low[p * ensemble : (p + 1) * ensemble, at] = low
    result = (
        dot_rows(wide_high[...], tall_high[...])
        + dot_rows(wide_low[...], tall_high[...])
        + dot_rows(wide_high[...], tall_low[...])
    )
    count = patches * ensemble // 64
    for n in range(3 * count):
        target = (own, others.at[0], others.at[1])[n // count]
        at = n % count
        piece = result[:, n // 2 * LANES : (n // 2 + 1) * LANES] if n // 2 * LANES + LANES <= result.shape[1] else None
        if piece is None:
            piece = jnp.concatenate([result[:, n * 64 :], jnp.zeros((ensemble + 8, 64), f32)], axis=1)
        else:
            if n % 2:
                piece = pltpu.roll(piece, 64, 1)
            piece = jnp.where(iota(piece.shape, 1) < 64, piece, 0.0)
        target[:, at * LANES : (at + 1) * LANES] = piece


def own_rows(received):
    return 64


def analysis_body(received, own, others, send, centred, factors, *, patches, tiles):
    sources, all_rows, _ = received.shape
    region_rows = own_rows(received)
    members = send.shape[1] * sources // received.shape[0] // (region_rows // 2)
    ensemble = sources * members
    hits = region_rows // members
    total = jnp.zeros((hits, LANES), f32)
    for s in range(sources):
        part = received[s, 0:region_rows, :].astype(f32)
        for b in range(members):
            one = part[b * hits : (b + 1) * hits, :]
            centred[s * members + b] = one
            total += one
    mean = total / ensemble
    for k in range(ensemble):
        centred[k] -= mean

    tile = lax.axis_index("tile")
    south, north = beside(others, tile, tiles)
    south = jnp.where(tile > 0, south[1], 0.0)
    north = jnp.where(tile < tiles - 1, north[0], 0.0)
    count = patches * ensemble // 64
    group = 64 // ensemble
    row = iota((ensemble + 8, LANES), 0)
    lane = iota((ensemble + 8, LANES), 1)
    within = lane & (ensemble - 1)
    start = jnp.where(
        (row == within) & (row < ensemble), jnp.where(lane < 64, ensemble - 1.0, 1.0), 0.0
    )
    lane8 = iota((BLOCK, LANES), 1)
    group_start = (lane8 & 63) & ~(ensemble - 1)
    transforms = []
    for i in range(count):
        at = slice(i * LANES, (i + 1) * LANES)
        state = own[:, at] + south[:, at] + north[:, at] + start
        pivots = jnp.ones((ensemble, LANES), f32)
        for k in range(ensemble):
            column = pick_lanes(state, group_start + k)
            pivot = column[k : k + 1, :]
            scaled = state[k : k + 1, :] / pivot
            state = state - jnp.where(row > k, column, 0.0) * scaled
            pivots = jnp.where(row[0:ensemble] == k, pivot, pivots)
        inverse = state[0:ensemble, :] * lax.rsqrt(pivots)
        mean_weight = -state[ensemble : ensemble + 1, :]
        unit = jnp.where(row[0:ensemble] == within[0:ensemble], 1.0, 0.0)
        transforms.append(mean_weight + (ensemble - 1.0) ** 0.5 * inverse - unit)

    side_lanes = 32
    patch = (lane8 // (2 * side_lanes)) * 2 + (lane8 & (side_lanes - 1)) // PATCH
    inside = 64 + (patch & (group - 1)) * ensemble if group > 1 else 64 + 0 * patch
    which = patch // group
    for j in range(ensemble):
        chosen = pick_lanes(transforms[0], inside + j)
        for i in range(1, count):
            other = pick_lanes(transforms[i], inside + j)
            chosen = jnp.where(jnp.broadcast_to(which[0:1] == i, chosen.shape), other, chosen)
        factors[j] = chosen

    def one_destination(d, _):
        totals = [jnp.zeros((hits, LANES), f32) for _ in range(members)]
        for j in range(ensemble):
            block = centred[j]
            for b in range(members):
                totals[b] += factors[j, pl.ds(d * members + b, 1), :] * block
        send[d] = jnp.concatenate(totals, axis=0).astype(bf16)
        return 0

    lax.fori_loop(0, sources, one_destination, 0)


def output_body(forecast, received, analysis):
    members, levels, side, width = forecast.shape
    for q in range(width // LANES):
        parts = [received[4 * q + c].astype(f32) for c in range(4)]
        at = slice(q * LANES, (q + 1) * LANES)
        for r, part in enumerate(transpose_chunks(parts)):
            rows = slice(r * BLOCK, (r + 1) * BLOCK)
            analysis[:, :, rows, at] = forecast[:, :, rows, at] + part.reshape(
                members, levels, BLOCK, LANES
            )


def shards(member_concentration, courant_pairs, obs_cell, obs_value, obs_error, obs_list):
    members, levels, side, width = member_concentration.shape
    blocks = lax.axis_size("member")
    tiles = lax.axis_size("tile")
    height = side * tiles
    ensemble = members * blocks
    per_side = side // PATCH
    patches = per_side * per_side
    slots = obs_list.shape[2]
    region_rows = members * levels * BLOCK
    depth = 3 * BLOCK
    all_rows = region_rows + members * depth
    edge_rows = -(-(48 + patches * slots // width) // 8) * 8
    edge_shape = (members, levels, BLOCK, width)
    rate_shape = (2, levels, BLOCK, width)

    (own_edges,) = call(
        pack_edges,
        [((edge_rows, width), f32)],
        [
            pltpu.VMEM(edge_shape, f32),
            pltpu.VMEM(edge_shape, f32),
            pltpu.VMEM(rate_shape, f32),
            pltpu.VMEM(rate_shape, f32),
            pltpu.VMEM(obs_list.shape, jnp.int32),
            pltpu.SemaphoreType.DMA((5,)),
        ],
        specs=[pl.BlockSpec(memory_space=pltpu.HBM)] * 3,
    )(member_concentration, courant_pairs, obs_list)
    edges = lax.all_gather(own_edges, "tile", axis=0, tiled=False)

    flat = lambda array: array.reshape(-1, LANES)
    cell = flat(obs_cell)
    forecast, send = call(
        functools.partial(forecast_body, tiles=tiles, height=height),
        [(member_concentration.shape, f32), ((blocks, all_rows, LANES), bf16)],
        [pltpu.VMEM((blocks, region_rows, LANES), f32)],
    )(
        member_concentration,
        courant_pairs,
        edges,
        cell.reshape(blocks, tiles * BLOCK, LANES),
    )
    received = lax.all_to_all(send, "member", split_axis=0, concat_axis=0, tiled=True)
    weights, values = call(
        functools.partial(
            weights_body, tiles=tiles, blocks=blocks, height=height, width=width, side=side
        ),
        [((16, depth * LANES), f32), ((depth, LANES), f32)],
        [pltpu.VMEM((16 * depth, LANES), f32)],
        flops=100_000_000,
    )(obs_list, edges, cell, flat(obs_value), flat(obs_error))

    tall = 3 * patches * ensemble
    system_shape = (ensemble + 8, patches * ensemble // 64 * LANES)
    own, for_others = call(
        functools.partial(systems_body, patches=patches),
        [(system_shape, f32), ((2,) + system_shape, f32)],
        [
            pltpu.VMEM(((ensemble + 8) * depth, LANES), f32),
            pltpu.VMEM((tall, depth * LANES), bf16),
            pltpu.VMEM((tall, depth * LANES), bf16),
            pltpu.VMEM((ensemble + 8, depth * LANES), bf16),
            pltpu.VMEM((ensemble + 8, depth * LANES), bf16),
        ],
    )(received, weights, values)
    others = lax.all_gather(for_others, "tile", axis=0, tiled=False)

    (change,) = call(
        functools.partial(analysis_body, patches=patches, tiles=tiles),
        [((blocks, region_rows, LANES), bf16)],
        [
            pltpu.VMEM((ensemble, levels * BLOCK, LANES), f32),
            pltpu.VMEM((ensemble, ensemble, LANES), f32),
        ],
    )(received, own, others)
    returned = lax.all_to_all(change, "member", split_axis=0, concat_axis=0, tiled=True)
    (analysis,) = call(output_body, [(forecast.shape, f32)])(forecast, returned)
    return analysis


def solution(mesh):
    return jax.shard_map(
        shards,
        mesh=mesh,
        in_specs=(
            P("member", None, "tile", None),
            P(None, None, "tile", None),
            P(),
            P(),
            P(),
            P("tile", "member", None),
        ),
        out_specs=P("member", None, "tile", None),
        check_vma=False,
    )
```

```python
import functools

import jax
import jax.numpy as jnp
from jax import lax
from jax.experimental import pallas as pl
from jax.experimental.pallas import tpu as pltpu
from jax.sharding import PartitionSpec as P

PATCH = 16
LOC_LEN = 16
DIFFUSION = 0.05
LANES = 128
BLOCK = 8

f32 = jnp.float32
bf16 = jnp.bfloat16


def call(body, outs, scratch=(), flops=1_000_000, moved=1_000_000, specs=None, vmem=48):
    specs = {} if specs is None else {"in_specs": specs}
    return pl.pallas_call(
        body,
        **specs,
        out_shape=[jax.ShapeDtypeStruct(shape, kind) for shape, kind in outs],
        scratch_shapes=list(scratch),
        compiler_params=pltpu.CompilerParams(vmem_limit_bytes=vmem * 1024 * 1024),
        cost_estimate=pl.CostEstimate(flops=flops, bytes_accessed=moved, transcendentals=0),
    )


def split(number, size):
    if size & (size - 1) == 0:
        return number >> (size.bit_length() - 1), number & (size - 1)
    quotient = number // size
    return quotient, number - quotient * size


def wrapped(number, size):
    if size & (size - 1) == 0:
        return number & (size - 1)
    return lax.rem(number + size, size)


def iota(shape, axis):
    return lax.broadcasted_iota(jnp.int32, shape, axis)


def pick_lanes(values, index):
    rows = [
        jnp.take_along_axis(values[r : r + BLOCK], index, axis=1, mode="promise_in_bounds")
        for r in range(0, values.shape[0], BLOCK)
    ]
    return rows[0] if len(rows) == 1 else jnp.concatenate(rows, axis=0)


def transpose_chunks(parts):
    lane = iota(parts[0].shape, 1)
    low = lane < 64
    even = (lane & 32) == 0
    parts = list(parts)
    for i in (0, 1):
        a, b = parts[i], parts[i + 2]
        parts[i] = jnp.where(low, a, pltpu.roll(b, 64, 1))
        parts[i + 2] = jnp.where(low, pltpu.roll(a, 64, 1), b)
    for i in (0, 2):
        a, b = parts[i], parts[i + 1]
        parts[i] = jnp.where(even, a, pltpu.roll(b, 32, 1))
        parts[i + 1] = jnp.where(even, pltpu.roll(a, 96, 1), b)
    return parts


def pack_edges(
    tracer, courant, lists, to_first, to_second, first, last, first_rates, last_rates, numbers, arrived
):
    members, levels, side, width = tracer.shape
    copies = [
        pltpu.make_async_copy(source, target, arrived.at[i])
        for i, (source, target) in enumerate(
            (
                (tracer.at[:, :, 0:BLOCK, :], first),
                (tracer.at[:, :, side - BLOCK : side, :], last),
                (courant.at[:, :, 0:BLOCK, :], first_rates),
                (courant.at[:, :, side - BLOCK : side, :], last_rates),
                (lists, numbers),
            )
        )
    ]
    for copy in copies:
        copy.start()
    for copy in copies:
        copy.wait()
    even = lax.rem(lax.axis_index("tile"), 2) == 0

    def put(row, low, high):
        to_first[row : row + 1, :] = jnp.where(even, high, low)
        to_second[row : row + 1, :] = jnp.where(even, low, high)

    end = BLOCK - 1
    for b in range(members):
        for l in range(levels):
            row = b * levels + l
            put(row, first[b, l, 0:1, :], last[b, l, end : end + 1, :])
            put(8 + row, first[b, l, 1:2, :], last[b, l, end - 1 : end, :])
    for c in range(2):
        for l in range(levels):
            put(16 + c * levels + l, first_rates[c, l, 0:1, :], last_rates[c, l, end : end + 1, :])
    row = 24
    for a in range(numbers.shape[0]):
        for b in range(numbers.shape[1]):
            for s in range(0, numbers.shape[2], width):
                part = numbers[a, b : b + 1, s : s + width].astype(f32)
                to_first[row : row + 1, :] = part
                to_second[row : row + 1, :] = part
                row += 1


def coefficients(meridional, zonal):
    return (
        (1.0 - 4.0 * DIFFUSION) - jnp.abs(zonal) - jnp.abs(meridional),
        DIFFUSION + jnp.maximum(zonal, 0.0),
        DIFFUSION - jnp.minimum(zonal, 0.0),
        DIFFUSION + jnp.maximum(meridional, 0.0),
        DIFFUSION - jnp.minimum(meridional, 0.0),
    )


def stencil(current, south, north, factors):
    width = current.shape[1]
    centre, from_west, from_east, from_south, from_north = factors
    west = pltpu.roll(current, 1, 1)
    east = pltpu.roll(current, width - 1, 1)
    return (
        centre * current
        + from_west * west
        + from_east * east
        + from_south * south
        + from_north * north
    )


def beside(first, second, tile):
    even = lax.rem(tile, 2) == 0
    return jnp.where(even, second, first), jnp.where(even, first, second)


def swap(first, second, tiles):
    pairs = lambda start: [
        pair for i in range(start, tiles - 1, 2) for pair in ((i, i + 1), (i + 1, i))
    ]
    return lax.ppermute(first, "tile", pairs(0)), lax.ppermute(second, "tile", pairs(1))


def forecast_body(
    tracer, courant, first, second, cell, forecast, send, table, *, tiles, height
):
    members, levels, side, width = tracer.shape
    blocks = width // side
    tile = lax.axis_index("tile")
    planes = members * levels

    south, north = beside(first[0:24, :], second[0:24, :], tile)
    own = lambda at: jnp.concatenate(
        [tracer[b, l, at : at + 1, :] for b in range(members) for l in range(levels)], axis=0
    )
    inside_south, inside_north = tile > 0, tile < tiles - 1
    low, lowest = south[0:planes], south[8 : 8 + planes]
    high, highest = north[0:planes], north[8 : 8 + planes]

    def edge(source):
        twice = lambda at: jnp.concatenate([source[at : at + levels]] * members, axis=0)
        return coefficients(twice(16), twice(16 + levels))

    below = stencil(low, lowest, own(0), edge(south))
    above = stencil(high, own(side - 1), highest, edge(north))
    below = jnp.where(inside_south, below, 0.0)
    above = jnp.where(inside_north, above, 0.0)
    row = iota((side, width), 0)
    for l in range(levels):
        factors = coefficients(courant[0, l], courant[1, l])
        for b in range(members):
            plane = b * levels + l
            current = tracer[b, l]
            for under, over in ((low, high), (below, above)):
                under, over = under[plane : plane + 1, :], over[plane : plane + 1, :]
                lower = jnp.where(row == 0, under, pltpu.roll(current, 1, 0))
                upper = jnp.where(row == side - 1, over, pltpu.roll(current, side - 1, 0))
                current = stencil(current, lower, upper, factors)
            forecast[b, l] = current

    region_rows = planes * BLOCK
    for q in range(width // LANES):
        parts = [
            forecast[:, :, r : r + BLOCK, q * LANES : (q + 1) * LANES].reshape(region_rows, LANES)
            for r in range(0, side, BLOCK)
        ]
        for c, part in enumerate(transpose_chunks(parts)):
            rounded = part.astype(bf16)
            send[4 * q + c, 0:region_rows, :] = rounded
            table[4 * q + c] = rounded.astype(f32)

    hits = levels * BLOCK
    observed = []
    first = pl.multiple_of(tile * BLOCK, BLOCK)
    for c in range(blocks):
        cells = cell[c, pl.ds(first, BLOCK), :]
        above_row, column = split(cells, width)
        level, grid_row = split(above_row, height)
        _, local_row = split(grid_row, side)
        _, local_column = split(column, side)
        band, sub_row = split(local_row, BLOCK)
        high = level * BLOCK + sub_row
        low = band * side + local_column
        mine = [jnp.zeros((BLOCK, LANES), f32) for _ in range(members)]
        for h in range(hits):
            here = high == h
            for b in range(members):
                line = table[c, b * hits + h : b * hits + h + 1, :]
                line = jnp.broadcast_to(line, (BLOCK, LANES))
                mine[b] = jnp.where(here, pick_lanes(line, low), mine[b])
        observed.append(mine)
    for c in range(blocks):
        rows = [
            observed[(c + r - 1) % blocks][b] for b in range(members) for r in range(3)
        ]
        for i in range(0, len(rows), 2):
            at = region_rows + i * BLOCK
            send[c, at : at + 2 * BLOCK, :] = jnp.concatenate(rows[i : i + 2], axis=0).astype(bf16)


def weights_body(
    lists, first, second, cell, value, variance, weights, values, planes, *, tiles, blocks, height, width, side
):
    tile = lax.axis_index("tile")
    block = lax.axis_index("member")
    own_lists = slice(24, 24 + lists.shape[0] * lists.shape[1] * lists.shape[2] // width)
    south, north = beside(first[own_lists, :], second[own_lists, :], tile)
    per_side = side // PATCH
    patches = per_side * per_side
    slots = lists.shape[2]
    depth = 3 * BLOCK
    rows, columns, sizes = [], [], []
    for r in range(3):
        column_block = wrapped(block + (r - 1), blocks)
        first = pl.multiple_of((column_block * tiles + tile) * BLOCK, BLOCK)
        cells = cell[pl.ds(first, BLOCK), :]
        above_row, column = split(cells, width)
        _, grid_row = split(above_row, height)
        rows.append(grid_row)
        columns.append(column)
        sizes.append(variance[pl.ds(first, BLOCK), :])
        values[r * BLOCK : (r + 1) * BLOCK, :] = value[pl.ds(first, BLOCK), :]
    grid_row = jnp.concatenate(rows, axis=0)
    column = jnp.concatenate(columns, axis=0)
    size = jnp.concatenate(sizes, axis=0)

    def pieces(dt, p):
        if dt == 0:
            return [lists[p // per_side, p % per_side : p % per_side + 1, :]]
        source = south if dt < 0 else north
        each = slots // width
        return [
            source[p * each + i : p * each + i + 1].astype(jnp.int32) for i in range(each)
        ]

    index = 0
    for dt in (0, -1, 1):
        for p in range(patches):
            count = jnp.zeros((depth, LANES), f32)
            for part in pieces(dt, p):
                length = part.shape[1]
                region, within = split(part, BLOCK * LANES)
                region_column, region_row = split(region, tiles)
                line, lane = split(within, LANES)
                near = wrapped(region_column - block + 1, blocks)
                fits = (part >= 0) & (region_row == tile) & (near < 3)
                line = jnp.where(fits, near * BLOCK + line, -1)
                one = (iota((depth, length), 0) == line).astype(f32).astype(bf16)
                other = (iota((LANES, length), 0) == lane).astype(f32).astype(bf16)
                count += lax.dot_general(
                    one, other, (((1,), (1,)), ((), ())), preferred_element_type=f32
                )
            patch_row = (tile + dt) * per_side + p // per_side
            patch_column = block * per_side + p % per_side
            row_gap = (grid_row - patch_row * PATCH - PATCH // 2).astype(f32) + 0.5
            turned = column - patch_column * PATCH - PATCH // 2 + width // 2
            column_gap = (wrapped(turned, width) - width // 2).astype(f32) + 0.5
            near = jnp.exp(
                -(row_gap * row_gap + column_gap * column_gap) / (2.0 * LOC_LEN * LOC_LEN)
            )
            planes[index * depth : (index + 1) * depth, :] = count * (near / size)
            index += 1
    for extra in range(index, 16):
        planes[extra * depth : (extra + 1) * depth, :] = jnp.zeros((depth, LANES), f32)
    for i in range(depth):
        weights[:, i * LANES : (i + 1) * LANES] = planes[pl.ds(i, 16, stride=depth), :]


def halves(values):
    high = values.astype(bf16)
    return high, (values - high.astype(f32)).astype(bf16)


def dot_rows(left, right):
    return lax.dot_general(left, right, (((1,), (1,)), ((), ())), preferred_element_type=f32)


def systems_body(
    received, weights, values, own, to_first, to_second, planes, tall_high, tall_low, wide_high, wide_low, *, patches
):
    sources, all_rows, _ = received.shape
    depth = 3 * BLOCK
    region_rows = own_rows(received)
    members = (all_rows - region_rows) // depth
    ensemble = sources * members
    total = jnp.zeros((depth, LANES), f32)
    for s in range(sources):
        both = received[s, region_rows:all_rows, :].astype(f32)
        planes[s * members * depth : (s + 1) * members * depth, :] = both
        for b in range(members):
            total += both[b * depth : (b + 1) * depth, :]
    mean = total / ensemble
    for k in range(ensemble):
        planes[k * depth : (k + 1) * depth, :] -= mean
    planes[ensemble * depth : (ensemble + 1) * depth, :] = values[...] - mean
    for k in range(ensemble + 1, ensemble + 8):
        planes[k * depth : (k + 1) * depth, :] = jnp.zeros((depth, LANES), f32)
    for i in range(depth):
        at = slice(i * LANES, (i + 1) * LANES)
        tile = planes[pl.ds(i, ensemble + 8, stride=depth), :]
        high, low = halves(tile)
        wide_high[:, at] = high
        wide_low[:, at] = low
        spread = tile[0:ensemble, :]
        for p in range(3 * patches):
            high, low = halves(spread * weights[p : p + 1, at])
            tall_high[p * ensemble : (p + 1) * ensemble, at] = high
            tall_low[p * ensemble : (p + 1) * ensemble, at] = low
    result = (
        dot_rows(wide_high[...], tall_high[...])
        + dot_rows(wide_low[...], tall_high[...])
        + dot_rows(wide_high[...], tall_low[...])
    )
    count = patches * ensemble // 64
    even = lax.rem(lax.axis_index("tile"), 2) == 0
    found = []
    for n in range(3 * count):
        piece = result[:, n // 2 * LANES : (n // 2 + 1) * LANES] if n // 2 * LANES + LANES <= result.shape[1] else None
        if piece is None:
            piece = jnp.concatenate([result[:, n * 64 :], jnp.zeros((ensemble + 8, 64), f32)], axis=1)
        else:
            if n % 2:
                piece = pltpu.roll(piece, 64, 1)
            piece = jnp.where(iota(piece.shape, 1) < 64, piece, 0.0)
        found.append(piece)
    for i in range(count):
        at = slice(i * LANES, (i + 1) * LANES)
        own[:, at] = found[i]
        for_south, for_north = found[count + i], found[2 * count + i]
        to_first[:, at] = jnp.where(even, for_north, for_south)
        to_second[:, at] = jnp.where(even, for_south, for_north)


def own_rows(received):
    return 64


def analysis_body(received, own, first, second, send, centred, factors, *, patches):
    sources, all_rows, _ = received.shape
    region_rows = own_rows(received)
    members = send.shape[1] * sources // received.shape[0] // (region_rows // 2)
    ensemble = sources * members
    hits = region_rows // members
    total = jnp.zeros((hits, LANES), f32)
    for s in range(sources):
        part = received[s, 0:region_rows, :].astype(f32)
        for b in range(members):
            one = part[b * hits : (b + 1) * hits, :]
            centred[s * members + b] = one
            total += one
    mean = total / ensemble
    for k in range(ensemble):
        centred[k] -= mean

    count = patches * ensemble // 64
    group = 64 // ensemble
    row = iota((ensemble + 8, LANES), 0)
    lane = iota((ensemble + 8, LANES), 1)
    within = lane & (ensemble - 1)
    start = jnp.where(
        (row == within) & (row < ensemble), jnp.where(lane < 64, ensemble - 1.0, 1.0), 0.0
    )
    lane8 = iota((BLOCK, LANES), 1)
    group_start = (lane8 & 63) & ~(ensemble - 1)
    transforms = []
    for i in range(count):
        at = slice(i * LANES, (i + 1) * LANES)
        state = own[:, at] + first[:, at] + second[:, at] + start
        pivots = jnp.ones((ensemble, LANES), f32)
        for k in range(ensemble):
            column = pick_lanes(state, group_start + k)
            pivot = column[k : k + 1, :]
            scaled = state[k : k + 1, :] / pivot
            state = state - jnp.where(row > k, column, 0.0) * scaled
            pivots = jnp.where(row[0:ensemble] == k, pivot, pivots)
        inverse = state[0:ensemble, :] * lax.rsqrt(pivots)
        mean_weight = -state[ensemble : ensemble + 1, :]
        unit = jnp.where(row[0:ensemble] == within[0:ensemble], 1.0, 0.0)
        transforms.append(mean_weight + (ensemble - 1.0) ** 0.5 * inverse - unit)

    side_lanes = 32
    patch = (lane8 // (2 * side_lanes)) * 2 + (lane8 & (side_lanes - 1)) // PATCH
    inside = 64 + (patch & (group - 1)) * ensemble if group > 1 else 64 + 0 * patch
    which = patch // group
    for j in range(ensemble):
        chosen = pick_lanes(transforms[0], inside + j)
        for i in range(1, count):
            other = pick_lanes(transforms[i], inside + j)
            chosen = jnp.where(jnp.broadcast_to(which[0:1] == i, chosen.shape), other, chosen)
        factors[j] = chosen

    def one_destination(d, _):
        totals = [jnp.zeros((hits, LANES), f32) for _ in range(members)]
        for j in range(ensemble):
            block = centred[j]
            for b in range(members):
                totals[b] += factors[j, pl.ds(d * members + b, 1), :] * block
        send[d] = jnp.concatenate(totals, axis=0).astype(bf16)
        return 0

    lax.fori_loop(0, sources, one_destination, 0)


def output_body(forecast, received, analysis):
    members, levels, side, width = forecast.shape
    for q in range(width // LANES):
        parts = [received[4 * q + c].astype(f32) for c in range(4)]
        at = slice(q * LANES, (q + 1) * LANES)
        for r, part in enumerate(transpose_chunks(parts)):
            rows = slice(r * BLOCK, (r + 1) * BLOCK)
            analysis[:, :, rows, at] = forecast[:, :, rows, at] + part.reshape(
                members, levels, BLOCK, LANES
            )


def shards(member_concentration, courant_pairs, obs_cell, obs_value, obs_error, obs_list):
    members, levels, side, width = member_concentration.shape
    blocks = lax.axis_size("member")
    tiles = lax.axis_size("tile")
    height = side * tiles
    ensemble = members * blocks
    per_side = side // PATCH
    patches = per_side * per_side
    slots = obs_list.shape[2]
    region_rows = members * levels * BLOCK
    depth = 3 * BLOCK
    all_rows = region_rows + members * depth
    edge_rows = -(-(24 + patches * slots // width) // 8) * 8
    edge_shape = (members, levels, BLOCK, width)
    rate_shape = (2, levels, BLOCK, width)

    to_first, to_second = call(
        pack_edges,
        [((edge_rows, width), f32)] * 2,
        [
            pltpu.VMEM(edge_shape, f32),
            pltpu.VMEM(edge_shape, f32),
            pltpu.VMEM(rate_shape, f32),
            pltpu.VMEM(rate_shape, f32),
            pltpu.VMEM(obs_list.shape, jnp.int32),
            pltpu.SemaphoreType.DMA((5,)),
        ],
        specs=[pl.BlockSpec(memory_space=pltpu.HBM)] * 3,
        vmem=63,
    )(member_concentration, courant_pairs, obs_list)
    first, second = swap(to_first, to_second, tiles)

    flat = lambda array: array.reshape(-1, LANES)
    cell = flat(obs_cell)
    forecast, send = call(
        functools.partial(forecast_body, tiles=tiles, height=height),
        [(member_concentration.shape, f32), ((blocks, all_rows, LANES), bf16)],
        [pltpu.VMEM((blocks, region_rows, LANES), f32)],
    )(
        member_concentration,
        courant_pairs,
        first,
        second,
        cell.reshape(blocks, tiles * BLOCK, LANES),
    )
    received = lax.all_to_all(send, "member", split_axis=0, concat_axis=0, tiled=True)
    weights, values = call(
        functools.partial(
            weights_body, tiles=tiles, blocks=blocks, height=height, width=width, side=side
        ),
        [((16, depth * LANES), f32), ((depth, LANES), f32)],
        [pltpu.VMEM((16 * depth, LANES), f32)],
        flops=100_000_000,
    )(obs_list, first, second, cell, flat(obs_value), flat(obs_error))

    tall = 3 * patches * ensemble
    system_shape = (ensemble + 8, patches * ensemble // 64 * LANES)
    own, to_first, to_second = call(
        functools.partial(systems_body, patches=patches),
        [(system_shape, f32)] * 3,
        [
            pltpu.VMEM(((ensemble + 8) * depth, LANES), f32),
            pltpu.VMEM((tall, depth * LANES), bf16),
            pltpu.VMEM((tall, depth * LANES), bf16),
            pltpu.VMEM((ensemble + 8, depth * LANES), bf16),
            pltpu.VMEM((ensemble + 8, depth * LANES), bf16),
        ],
    )(received, weights, values)
    first, second = swap(to_first, to_second, tiles)

    (change,) = call(
        functools.partial(analysis_body, patches=patches),
        [((blocks, region_rows, LANES), bf16)],
        [
            pltpu.VMEM((ensemble, levels * BLOCK, LANES), f32),
            pltpu.VMEM((ensemble, ensemble, LANES), f32),
        ],
    )(received, own, first, second)
    returned = lax.all_to_all(change, "member", split_axis=0, concat_axis=0, tiled=True)
    (analysis,) = call(output_body, [(forecast.shape, f32)])(forecast, returned)
    return analysis


def solution(mesh):
    return jax.shard_map(
        shards,
        mesh=mesh,
        in_specs=(
            P("member", None, "tile", None),
            P(None, None, "tile", None),
            P(),
            P(),
            P(),
            P("tile", "member", None),
        ),
        out_specs=P("member", None, "tile", None),
        check_vma=False,
    )
```

```python
import functools

import jax
import jax.numpy as jnp
from jax import lax
from jax.experimental import pallas as pl
from jax.experimental.pallas import tpu as pltpu
from jax.sharding import PartitionSpec as P

PATCH = 16
LOC_LEN = 16
DIFFUSION = 0.05
LANES = 128
BLOCK = 8

f32 = jnp.float32
bf16 = jnp.bfloat16


def call(body, outs, scratch=(), flops=1_000_000, moved=1_000_000, specs=None, vmem=48):
    specs = {} if specs is None else {"in_specs": specs}
    return pl.pallas_call(
        body,
        **specs,
        out_shape=[jax.ShapeDtypeStruct(shape, kind) for shape, kind in outs],
        scratch_shapes=list(scratch),
        compiler_params=pltpu.CompilerParams(vmem_limit_bytes=vmem * 1024 * 1024),
        cost_estimate=pl.CostEstimate(flops=flops, bytes_accessed=moved, transcendentals=0),
    )


def split(number, size):
    if size & (size - 1) == 0:
        return number >> (size.bit_length() - 1), number & (size - 1)
    quotient = number // size
    return quotient, number - quotient * size


def wrapped(number, size):
    if size & (size - 1) == 0:
        return number & (size - 1)
    return lax.rem(number + size, size)


def iota(shape, axis):
    return lax.broadcasted_iota(jnp.int32, shape, axis)


def pick_lanes(values, index):
    rows = [
        jnp.take_along_axis(values[r : r + BLOCK], index, axis=1, mode="promise_in_bounds")
        for r in range(0, values.shape[0], BLOCK)
    ]
    return rows[0] if len(rows) == 1 else jnp.concatenate(rows, axis=0)


def transpose_chunks(parts):
    lane = iota(parts[0].shape, 1)
    low = lane < 64
    even = (lane & 32) == 0
    parts = list(parts)
    for i in (0, 1):
        a, b = parts[i], parts[i + 2]
        parts[i] = jnp.where(low, a, pltpu.roll(b, 64, 1))
        parts[i + 2] = jnp.where(low, pltpu.roll(a, 64, 1), b)
    for i in (0, 2):
        a, b = parts[i], parts[i + 1]
        parts[i] = jnp.where(even, a, pltpu.roll(b, 32, 1))
        parts[i + 1] = jnp.where(even, pltpu.roll(a, 96, 1), b)
    return parts


def pack_edges(
    tracer, courant, lists, to_first, to_second, first, last, first_rates, last_rates, numbers, arrived
):
    members, levels, side, width = tracer.shape
    copies = [
        pltpu.make_async_copy(source, target, arrived.at[i])
        for i, (source, target) in enumerate(
            (
                (tracer.at[:, :, 0:BLOCK, :], first),
                (tracer.at[:, :, side - BLOCK : side, :], last),
                (courant.at[:, :, 0:BLOCK, :], first_rates),
                (courant.at[:, :, side - BLOCK : side, :], last_rates),
                (lists, numbers),
            )
        )
    ]
    for copy in copies:
        copy.start()
    for copy in copies:
        copy.wait()
    even = lax.rem(lax.axis_index("tile"), 2) == 0

    def put(row, low, high):
        to_first[row : row + 1, :] = jnp.where(even, high, low)
        to_second[row : row + 1, :] = jnp.where(even, low, high)

    end = BLOCK - 1
    for b in range(members):
        for l in range(levels):
            row = b * levels + l
            put(row, first[b, l, 0:1, :], last[b, l, end : end + 1, :])
            put(8 + row, first[b, l, 1:2, :], last[b, l, end - 1 : end, :])
    for c in range(2):
        for l in range(levels):
            put(16 + c * levels + l, first_rates[c, l, 0:1, :], last_rates[c, l, end : end + 1, :])
    row = 24
    for a in range(numbers.shape[0]):
        for b in range(numbers.shape[1]):
            for s in range(0, numbers.shape[2], width):
                part = numbers[a, b : b + 1, s : s + width].astype(f32)
                to_first[row : row + 1, :] = part
                to_second[row : row + 1, :] = part
                row += 1


def coefficients(meridional, zonal):
    return (
        (1.0 - 4.0 * DIFFUSION) - jnp.abs(zonal) - jnp.abs(meridional),
        DIFFUSION + jnp.maximum(zonal, 0.0),
        DIFFUSION - jnp.minimum(zonal, 0.0),
        DIFFUSION + jnp.maximum(meridional, 0.0),
        DIFFUSION - jnp.minimum(meridional, 0.0),
    )


def stencil(current, south, north, factors):
    width = current.shape[1]
    centre, from_west, from_east, from_south, from_north = factors
    west = pltpu.roll(current, 1, 1)
    east = pltpu.roll(current, width - 1, 1)
    return (
        centre * current
        + from_west * west
        + from_east * east
        + from_south * south
        + from_north * north
    )


def beside(first, second, tile):
    even = lax.rem(tile, 2) == 0
    return jnp.where(even, second, first), jnp.where(even, first, second)


def swap(first, second, tiles):
    pairs = lambda start: [
        pair for i in range(start, tiles - 1, 2) for pair in ((i, i + 1), (i + 1, i))
    ]
    return lax.ppermute(first, "tile", pairs(0)), lax.ppermute(second, "tile", pairs(1))


def exchange(chunks):
    size = len(chunks)
    swaps = lambda s: [(i, i ^ s) for i in range(size)]
    received = {s: lax.ppermute(chunks[s], "member", swaps(s)) for s in range(size - 1, 0, -1)}
    return [chunks[0]] + [received[s] for s in range(1, size)]


def forecast_body(
    tracer, courant, first, second, cell, forecast, *rest, tiles, height
):
    *chunks, send, table = rest
    members, levels, side, width = tracer.shape
    blocks = width // side
    tile = lax.axis_index("tile")
    planes = members * levels

    south, north = beside(first[0:24, :], second[0:24, :], tile)
    own = lambda at: jnp.concatenate(
        [tracer[b, l, at : at + 1, :] for b in range(members) for l in range(levels)], axis=0
    )
    inside_south, inside_north = tile > 0, tile < tiles - 1
    low, lowest = south[0:planes], south[8 : 8 + planes]
    high, highest = north[0:planes], north[8 : 8 + planes]

    def edge(source):
        twice = lambda at: jnp.concatenate([source[at : at + levels]] * members, axis=0)
        return coefficients(twice(16), twice(16 + levels))

    below = stencil(low, lowest, own(0), edge(south))
    above = stencil(high, own(side - 1), highest, edge(north))
    below = jnp.where(inside_south, below, 0.0)
    above = jnp.where(inside_north, above, 0.0)
    row = iota((side, width), 0)
    for l in range(levels):
        factors = coefficients(courant[0, l], courant[1, l])
        for b in range(members):
            plane = b * levels + l
            current = tracer[b, l]
            for under, over in ((low, high), (below, above)):
                under, over = under[plane : plane + 1, :], over[plane : plane + 1, :]
                lower = jnp.where(row == 0, under, pltpu.roll(current, 1, 0))
                upper = jnp.where(row == side - 1, over, pltpu.roll(current, side - 1, 0))
                current = stencil(current, lower, upper, factors)
            forecast[b, l] = current

    region_rows = planes * BLOCK
    for q in range(width // LANES):
        parts = [
            forecast[:, :, r : r + BLOCK, q * LANES : (q + 1) * LANES].reshape(region_rows, LANES)
            for r in range(0, side, BLOCK)
        ]
        for c, part in enumerate(transpose_chunks(parts)):
            rounded = part.astype(bf16)
            send[4 * q + c, 0:region_rows, :] = rounded
            table[4 * q + c] = rounded.astype(f32)

    hits = levels * BLOCK
    observed = []
    for c in range(blocks):
        cells = cell[c]
        above_row, column = split(cells, width)
        level, grid_row = split(above_row, height)
        _, local_row = split(grid_row, side)
        _, local_column = split(column, side)
        band, sub_row = split(local_row, BLOCK)
        high = level * BLOCK + sub_row
        low = band * side + local_column
        mine = [jnp.zeros((BLOCK, LANES), f32) for _ in range(members)]
        for h in range(hits):
            here = high == h
            for b in range(members):
                line = table[c, b * hits + h : b * hits + h + 1, :]
                line = jnp.broadcast_to(line, (BLOCK, LANES))
                mine[b] = jnp.where(here, pick_lanes(line, low), mine[b])
        observed.append(mine)
    for c in range(blocks):
        rows = [
            observed[(c + r - 1) % blocks][b] for b in range(members) for r in range(3)
        ]
        for i in range(0, len(rows), 2):
            at = region_rows + i * BLOCK
            send[c, at : at + 2 * BLOCK, :] = jnp.concatenate(rows[i : i + 2], axis=0).astype(bf16)
    block = lax.axis_index("member")
    for s, chunk in enumerate(chunks):
        chunk[...] = send[block ^ s]


def weights_body(
    lists, first, second, cell, value, variance, weights, values, planes, *, tiles, blocks, height, width, side
):
    tile = lax.axis_index("tile")
    block = lax.axis_index("member")
    own_lists = slice(24, 24 + lists.shape[0] * lists.shape[1] * lists.shape[2] // width)
    south, north = beside(first[own_lists, :], second[own_lists, :], tile)
    per_side = side // PATCH
    patches = per_side * per_side
    slots = lists.shape[2]
    depth = 3 * BLOCK
    rows, columns, sizes = [], [], []
    for r in range(3):
        column_block = wrapped(block + (r - 1), blocks)
        first = pl.multiple_of((column_block * tiles + tile) * BLOCK, BLOCK)
        cells = cell[pl.ds(first, BLOCK), :]
        above_row, column = split(cells, width)
        _, grid_row = split(above_row, height)
        rows.append(grid_row)
        columns.append(column)
        sizes.append(variance[pl.ds(first, BLOCK), :])
        values[r * BLOCK : (r + 1) * BLOCK, :] = value[pl.ds(first, BLOCK), :]
    grid_row = jnp.concatenate(rows, axis=0)
    column = jnp.concatenate(columns, axis=0)
    size = jnp.concatenate(sizes, axis=0)

    def pieces(dt, p):
        if dt == 0:
            return [lists[p // per_side, p % per_side : p % per_side + 1, :]]
        source = south if dt < 0 else north
        each = slots // width
        return [
            source[p * each + i : p * each + i + 1].astype(jnp.int32) for i in range(each)
        ]

    index = 0
    for dt in (0, -1, 1):
        for p in range(patches):
            count = jnp.zeros((depth, LANES), f32)
            for part in pieces(dt, p):
                length = part.shape[1]
                region, within = split(part, BLOCK * LANES)
                region_column, region_row = split(region, tiles)
                line, lane = split(within, LANES)
                near = wrapped(region_column - block + 1, blocks)
                fits = (part >= 0) & (region_row == tile) & (near < 3)
                line = jnp.where(fits, near * BLOCK + line, -1)
                one = (iota((depth, length), 0) == line).astype(f32).astype(bf16)
                other = (iota((LANES, length), 0) == lane).astype(f32).astype(bf16)
                count += lax.dot_general(
                    one, other, (((1,), (1,)), ((), ())), preferred_element_type=f32
                )
            patch_row = (tile + dt) * per_side + p // per_side
            patch_column = block * per_side + p % per_side
            row_gap = (grid_row - patch_row * PATCH - PATCH // 2).astype(f32) + 0.5
            turned = column - patch_column * PATCH - PATCH // 2 + width // 2
            column_gap = (wrapped(turned, width) - width // 2).astype(f32) + 0.5
            near = jnp.exp(
                -(row_gap * row_gap + column_gap * column_gap) / (2.0 * LOC_LEN * LOC_LEN)
            )
            planes[index * depth : (index + 1) * depth, :] = count * (near / size)
            index += 1
    for extra in range(index, 16):
        planes[extra * depth : (extra + 1) * depth, :] = jnp.zeros((depth, LANES), f32)
    for i in range(depth):
        weights[:, i * LANES : (i + 1) * LANES] = planes[pl.ds(i, 16, stride=depth), :]


def halves(values):
    high = values.astype(bf16)
    return high, (values - high.astype(f32)).astype(bf16)


def dot_rows(left, right):
    return lax.dot_general(left, right, (((1,), (1,)), ((), ())), preferred_element_type=f32)


def systems_body(*refs, patches, sources, members, region_rows):
    received, rest = refs[:sources], refs[sources:]
    weights, values, own, to_first, to_second, planes, tall_high, tall_low, wide_high, wide_low = rest
    depth = 3 * BLOCK
    all_rows = received[0].shape[0]
    block = lax.axis_index("member")
    ensemble = sources * members
    total = jnp.zeros((depth, LANES), f32)
    for s in range(sources):
        both = received[s][region_rows:all_rows, :].astype(f32)
        at = pl.multiple_of((block ^ s) * (members * depth), BLOCK)
        planes[pl.ds(at, members * depth), :] = both
        for b in range(members):
            total += both[b * depth : (b + 1) * depth, :]
    mean = total / ensemble
    for k in range(ensemble):
        planes[k * depth : (k + 1) * depth, :] -= mean
    planes[ensemble * depth : (ensemble + 1) * depth, :] = values[...] - mean
    for k in range(ensemble + 1, ensemble + 8):
        planes[k * depth : (k + 1) * depth, :] = jnp.zeros((depth, LANES), f32)
    for i in range(depth):
        at = slice(i * LANES, (i + 1) * LANES)
        tile = planes[pl.ds(i, ensemble + 8, stride=depth), :]
        high, low = halves(tile)
        wide_high[:, at] = high
        wide_low[:, at] = low
        spread = tile[0:ensemble, :]
        for p in range(3 * patches):
            high, low = halves(spread * weights[p : p + 1, at])
            tall_high[p * ensemble : (p + 1) * ensemble, at] = high
            tall_low[p * ensemble : (p + 1) * ensemble, at] = low
    result = (
        dot_rows(wide_high[...], tall_high[...])
        + dot_rows(wide_low[...], tall_high[...])
        + dot_rows(wide_high[...], tall_low[...])
    )
    count = patches * ensemble // 64
    even = lax.rem(lax.axis_index("tile"), 2) == 0
    found = []
    for n in range(3 * count):
        piece = result[:, n // 2 * LANES : (n // 2 + 1) * LANES] if n // 2 * LANES + LANES <= result.shape[1] else None
        if piece is None:
            piece = jnp.concatenate([result[:, n * 64 :], jnp.zeros((ensemble + 8, 64), f32)], axis=1)
        else:
            if n % 2:
                piece = pltpu.roll(piece, 64, 1)
            piece = jnp.where(iota(piece.shape, 1) < 64, piece, 0.0)
        found.append(piece)
    for i in range(count):
        at = slice(i * LANES, (i + 1) * LANES)
        own[:, at] = found[i]
        for_south, for_north = found[count + i], found[2 * count + i]
        to_first[:, at] = jnp.where(even, for_north, for_south)
        to_second[:, at] = jnp.where(even, for_south, for_north)


def analysis_body(*refs, patches, sources, members, region_rows):
    received, rest = refs[:sources], refs[sources:]
    own, first, second = rest[:3]
    chunks, (centred, factors) = rest[3:-2], rest[-2:]
    block = lax.axis_index("member")
    ensemble = sources * members
    hits = region_rows // members
    total = jnp.zeros((hits, LANES), f32)
    for s in range(sources):
        part = received[s][0:region_rows, :].astype(f32)
        for b in range(members):
            one = part[b * hits : (b + 1) * hits, :]
            centred[(block ^ s) * members + b] = one
            total += one
    mean = total / ensemble
    for k in range(ensemble):
        centred[k] -= mean

    count = patches * ensemble // 64
    group = 64 // ensemble
    row = iota((ensemble + 8, LANES), 0)
    lane = iota((ensemble + 8, LANES), 1)
    within = lane & (ensemble - 1)
    start = jnp.where(
        (row == within) & (row < ensemble), jnp.where(lane < 64, ensemble - 1.0, 1.0), 0.0
    )
    lane8 = iota((BLOCK, LANES), 1)
    group_start = (lane8 & 63) & ~(ensemble - 1)
    transforms = []
    for i in range(count):
        at = slice(i * LANES, (i + 1) * LANES)
        state = own[:, at] + first[:, at] + second[:, at] + start
        pivots = jnp.ones((ensemble, LANES), f32)
        for k in range(ensemble):
            column = pick_lanes(state, group_start + k)
            pivot = column[k : k + 1, :]
            scaled = state[k : k + 1, :] / pivot
            state = state - jnp.where(row > k, column, 0.0) * scaled
            pivots = jnp.where(row[0:ensemble] == k, pivot, pivots)
        inverse = state[0:ensemble, :] * lax.rsqrt(pivots)
        mean_weight = -state[ensemble : ensemble + 1, :]
        unit = jnp.where(row[0:ensemble] == within[0:ensemble], 1.0, 0.0)
        transforms.append(mean_weight + (ensemble - 1.0) ** 0.5 * inverse - unit)

    side_lanes = 32
    patch = (lane8 // (2 * side_lanes)) * 2 + (lane8 & (side_lanes - 1)) // PATCH
    inside = 64 + (patch & (group - 1)) * ensemble if group > 1 else 64 + 0 * patch
    which = patch // group
    for j in range(ensemble):
        chosen = pick_lanes(transforms[0], inside + j)
        for i in range(1, count):
            other = pick_lanes(transforms[i], inside + j)
            chosen = jnp.where(jnp.broadcast_to(which[0:1] == i, chosen.shape), other, chosen)
        factors[j] = chosen

    for s, chunk in enumerate(chunks):
        target = block ^ s
        totals = [jnp.zeros((hits, LANES), f32) for _ in range(members)]
        for j in range(ensemble):
            centred_j = centred[j]
            for b in range(members):
                totals[b] += factors[j, pl.ds(target * members + b, 1), :] * centred_j
        chunk[...] = jnp.concatenate(totals, axis=0).astype(bf16)


def output_body(forecast, *refs):
    received, (analysis, ordered) = refs[:-2], refs[-2:]
    members, levels, side, width = forecast.shape
    block = lax.axis_index("member")
    for s, part in enumerate(received):
        ordered[block ^ s] = part[...].astype(f32)
    for q in range(width // LANES):
        parts = [ordered[4 * q + c] for c in range(4)]
        at = slice(q * LANES, (q + 1) * LANES)
        for r, part in enumerate(transpose_chunks(parts)):
            rows = slice(r * BLOCK, (r + 1) * BLOCK)
            analysis[:, :, rows, at] = forecast[:, :, rows, at] + part.reshape(
                members, levels, BLOCK, LANES
            )


def shards(member_concentration, courant_pairs, obs_cell, obs_value, obs_error, obs_list):
    members, levels, side, width = member_concentration.shape
    blocks = lax.axis_size("member")
    tiles = lax.axis_size("tile")
    height = side * tiles
    ensemble = members * blocks
    per_side = side // PATCH
    patches = per_side * per_side
    slots = obs_list.shape[2]
    region_rows = members * levels * BLOCK
    depth = 3 * BLOCK
    all_rows = region_rows + members * depth
    edge_rows = -(-(24 + patches * slots // width) // 8) * 8
    edge_shape = (members, levels, BLOCK, width)
    rate_shape = (2, levels, BLOCK, width)

    to_first, to_second = call(
        pack_edges,
        [((edge_rows, width), f32)] * 2,
        [
            pltpu.VMEM(edge_shape, f32),
            pltpu.VMEM(edge_shape, f32),
            pltpu.VMEM(rate_shape, f32),
            pltpu.VMEM(rate_shape, f32),
            pltpu.VMEM(obs_list.shape, jnp.int32),
            pltpu.SemaphoreType.DMA((5,)),
        ],
        specs=[pl.BlockSpec(memory_space=pltpu.HBM)] * 3,
        vmem=63,
    )(member_concentration, courant_pairs, obs_list)
    first, second = swap(to_first, to_second, tiles)

    flat = lambda array: array.reshape(-1, LANES)
    cell = flat(obs_cell)
    cell_row = lax.dynamic_index_in_dim(
        cell.reshape(blocks, tiles, BLOCK, LANES), lax.axis_index("tile"), 1, False
    )
    forecast, *chunks = call(
        functools.partial(forecast_body, tiles=tiles, height=height),
        [(member_concentration.shape, f32)] + [((all_rows, LANES), bf16)] * blocks,
        [
            pltpu.VMEM((blocks, all_rows, LANES), bf16),
            pltpu.VMEM((blocks, region_rows, LANES), f32),
        ],
    )(
        member_concentration,
        courant_pairs,
        first,
        second,
        cell_row,
    )
    received = exchange(chunks)
    weights, values = call(
        functools.partial(
            weights_body, tiles=tiles, blocks=blocks, height=height, width=width, side=side
        ),
        [((16, depth * LANES), f32), ((depth, LANES), f32)],
        [pltpu.VMEM((16 * depth, LANES), f32)],
        flops=100_000_000,
    )(obs_list, first, second, cell, flat(obs_value), flat(obs_error))

    sizes = dict(patches=patches, sources=blocks, members=members, region_rows=region_rows)
    tall = 3 * patches * ensemble
    system_shape = (ensemble + 8, patches * ensemble // 64 * LANES)
    own, to_first, to_second = call(
        functools.partial(systems_body, **sizes),
        [(system_shape, f32)] * 3,
        [
            pltpu.VMEM(((ensemble + 8) * depth, LANES), f32),
            pltpu.VMEM((tall, depth * LANES), bf16),
            pltpu.VMEM((tall, depth * LANES), bf16),
            pltpu.VMEM((ensemble + 8, depth * LANES), bf16),
            pltpu.VMEM((ensemble + 8, depth * LANES), bf16),
        ],
    )(*received, weights, values)
    first, second = swap(to_first, to_second, tiles)

    changes = call(
        functools.partial(analysis_body, **sizes),
        [((region_rows, LANES), bf16)] * blocks,
        [
            pltpu.VMEM((ensemble, levels * BLOCK, LANES), f32),
            pltpu.VMEM((ensemble, ensemble, LANES), f32),
        ],
    )(*received, own, first, second)
    returned = exchange(changes)
    (analysis,) = call(
        output_body, [(forecast.shape, f32)], [pltpu.VMEM((blocks, region_rows, LANES), f32)]
    )(forecast, *returned)
    return analysis


def solution(mesh):
    return jax.shard_map(
        shards,
        mesh=mesh,
        in_specs=(
            P("member", None, "tile", None),
            P(None, None, "tile", None),
            P(),
            P(),
            P(),
            P("tile", "member", None),
        ),
        out_specs=P("member", None, "tile", None),
        check_vma=False,
    )
```

```python
import functools

import jax
import jax.numpy as jnp
from jax import lax
from jax.experimental import pallas as pl
from jax.experimental.pallas import tpu as pltpu
from jax.sharding import PartitionSpec as P

PATCH = 16
LOC_LEN = 16
DIFFUSION = 0.05
LANES = 128
BLOCK = 8

f32 = jnp.float32
bf16 = jnp.bfloat16


def call(body, outs, scratch=(), flops=1_000_000, moved=1_000_000, specs=None, vmem=48):
    specs = {} if specs is None else {"in_specs": specs}
    return pl.pallas_call(
        body,
        **specs,
        out_shape=[jax.ShapeDtypeStruct(shape, kind) for shape, kind in outs],
        scratch_shapes=list(scratch),
        compiler_params=pltpu.CompilerParams(vmem_limit_bytes=vmem * 1024 * 1024),
        cost_estimate=pl.CostEstimate(flops=flops, bytes_accessed=moved, transcendentals=0),
    )


def split(number, size):
    if size & (size - 1) == 0:
        return number >> (size.bit_length() - 1), number & (size - 1)
    quotient = number // size
    return quotient, number - quotient * size


def wrapped(number, size):
    if size & (size - 1) == 0:
        return number & (size - 1)
    return lax.rem(number + size, size)


def iota(shape, axis):
    return lax.broadcasted_iota(jnp.int32, shape, axis)


def pick_lanes(values, index):
    rows = [
        jnp.take_along_axis(values[r : r + BLOCK], index, axis=1, mode="promise_in_bounds")
        for r in range(0, values.shape[0], BLOCK)
    ]
    return rows[0] if len(rows) == 1 else jnp.concatenate(rows, axis=0)


def transpose_chunks(parts):
    lane = iota(parts[0].shape, 1)
    low = lane < 64
    even = (lane & 32) == 0
    parts = list(parts)
    for i in (0, 1):
        a, b = parts[i], parts[i + 2]
        parts[i] = jnp.where(low, a, pltpu.roll(b, 64, 1))
        parts[i + 2] = jnp.where(low, pltpu.roll(a, 64, 1), b)
    for i in (0, 2):
        a, b = parts[i], parts[i + 1]
        parts[i] = jnp.where(even, a, pltpu.roll(b, 32, 1))
        parts[i + 1] = jnp.where(even, pltpu.roll(a, 96, 1), b)
    return parts


def pack_edges(
    tracer, courant, lists, to_first, to_second, first, last, first_rates, last_rates, numbers, arrived
):
    members, levels, side, width = tracer.shape
    copies = [
        pltpu.make_async_copy(source, target, arrived.at[i])
        for i, (source, target) in enumerate(
            (
                (tracer.at[:, :, 0:BLOCK, :], first),
                (tracer.at[:, :, side - BLOCK : side, :], last),
                (courant.at[:, :, 0:BLOCK, :], first_rates),
                (courant.at[:, :, side - BLOCK : side, :], last_rates),
                (lists, numbers),
            )
        )
    ]
    for copy in copies:
        copy.start()
    for copy in copies:
        copy.wait()
    even = lax.rem(lax.axis_index("tile"), 2) == 0

    def put(row, low, high):
        to_first[row : row + 1, :] = jnp.where(even, high, low)
        to_second[row : row + 1, :] = jnp.where(even, low, high)

    end = BLOCK - 1
    for b in range(members):
        for l in range(levels):
            row = b * levels + l
            put(row, first[b, l, 0:1, :], last[b, l, end : end + 1, :])
            put(8 + row, first[b, l, 1:2, :], last[b, l, end - 1 : end, :])
    for c in range(2):
        for l in range(levels):
            put(16 + c * levels + l, first_rates[c, l, 0:1, :], last_rates[c, l, end : end + 1, :])
    row = 24
    for a in range(numbers.shape[0]):
        for b in range(numbers.shape[1]):
            for s in range(0, numbers.shape[2], width):
                part = numbers[a, b : b + 1, s : s + width].astype(f32)
                to_first[row : row + 1, :] = part
                to_second[row : row + 1, :] = part
                row += 1


def coefficients(meridional, zonal):
    return (
        (1.0 - 4.0 * DIFFUSION) - jnp.abs(zonal) - jnp.abs(meridional),
        DIFFUSION + jnp.maximum(zonal, 0.0),
        DIFFUSION - jnp.minimum(zonal, 0.0),
        DIFFUSION + jnp.maximum(meridional, 0.0),
        DIFFUSION - jnp.minimum(meridional, 0.0),
    )


def stencil(current, south, north, factors):
    width = current.shape[1]
    centre, from_west, from_east, from_south, from_north = factors
    west = pltpu.roll(current, 1, 1)
    east = pltpu.roll(current, width - 1, 1)
    return (
        centre * current
        + from_west * west
        + from_east * east
        + from_south * south
        + from_north * north
    )


def beside(first, second, tile):
    even = lax.rem(tile, 2) == 0
    return jnp.where(even, second, first), jnp.where(even, first, second)


def swap(first, second, tiles):
    pairs = lambda start: [
        pair for i in range(start, tiles - 1, 2) for pair in ((i, i + 1), (i + 1, i))
    ]
    return lax.ppermute(first, "tile", pairs(0)), lax.ppermute(second, "tile", pairs(1))


def exchange(chunks):
    chips = len(chunks)
    device = lambda chip, core: 2 * chip + core
    swaps = lambda s: [(device(i, c), device(i ^ s, c)) for i in range(chips) for c in (0, 1)]
    received = {s: lax.ppermute(chunks[s], "member", swaps(s)) for s in range(chips - 1, 0, -1)}
    return [chunks[0]] + [received[s] for s in range(1, chips)]


def swap_cores(array):
    return lax.ppermute(array, "member", [(i, i ^ 1) for i in range(lax.axis_size("member"))])


def place():
    block = lax.axis_index("member")
    core = lax.rem(block, 2)
    return block, (block - core) // 2, core


def share_body(*refs, region_rows):
    chunks, (own, other) = refs[:-2], refs[-2:]
    _, _, core = place()
    first = core == 0
    each = own.shape[0] // len(chunks)
    half = chunks[0].shape[0] - 2 * region_rows
    lines = half // 2
    for s, chunk in enumerate(chunks):
        low, high = chunk[0:region_rows, :], chunk[region_rows : 2 * region_rows, :]
        row = s * each
        own[row : row + region_rows, :] = jnp.where(first, low, high)
        other[row : row + region_rows, :] = jnp.where(first, high, low)
        if each == region_rows:
            continue
        seen = chunk[2 * region_rows :, :].astype(f32)
        west = jnp.concatenate([seen[0 : lines - 8], seen[lines : 2 * lines - 8]], axis=0)
        east = jnp.concatenate([seen[8:lines], seen[lines + 8 : 2 * lines]], axis=0)
        own[row + region_rows : row + each, :] = jnp.where(first, west, east).astype(bf16)
        other[row + region_rows : row + each, :] = jnp.where(first, east, west).astype(bf16)


def forecast_body(
    tracer, courant, first, second, cell, forecast, *rest, tiles, height
):
    *chunks, send, table = rest
    members, levels, side, width = tracer.shape
    blocks = width // side
    tile = lax.axis_index("tile")
    planes = members * levels

    south, north = beside(first[0:24, :], second[0:24, :], tile)
    own = lambda at: jnp.concatenate(
        [tracer[b, l, at : at + 1, :] for b in range(members) for l in range(levels)], axis=0
    )
    inside_south, inside_north = tile > 0, tile < tiles - 1
    low, lowest = south[0:planes], south[8 : 8 + planes]
    high, highest = north[0:planes], north[8 : 8 + planes]

    def edge(source):
        twice = lambda at: jnp.concatenate([source[at : at + levels]] * members, axis=0)
        return coefficients(twice(16), twice(16 + levels))

    below = stencil(low, lowest, own(0), edge(south))
    above = stencil(high, own(side - 1), highest, edge(north))
    below = jnp.where(inside_south, below, 0.0)
    above = jnp.where(inside_north, above, 0.0)
    row = iota((side, width), 0)
    for l in range(levels):
        factors = coefficients(courant[0, l], courant[1, l])
        for b in range(members):
            plane = b * levels + l
            current = tracer[b, l]
            for under, over in ((low, high), (below, above)):
                under, over = under[plane : plane + 1, :], over[plane : plane + 1, :]
                lower = jnp.where(row == 0, under, pltpu.roll(current, 1, 0))
                upper = jnp.where(row == side - 1, over, pltpu.roll(current, side - 1, 0))
                current = stencil(current, lower, upper, factors)
            forecast[b, l] = current

    region_rows = planes * BLOCK
    for q in range(width // LANES):
        parts = [
            forecast[:, :, r : r + BLOCK, q * LANES : (q + 1) * LANES].reshape(region_rows, LANES)
            for r in range(0, side, BLOCK)
        ]
        for i, part in enumerate(transpose_chunks(parts)):
            c = 4 * q + i
            rounded = part.astype(bf16)
            send[c // 2, c % 2 * region_rows : (c % 2 + 1) * region_rows, :] = rounded
            table[c] = rounded.astype(f32)

    hits = levels * BLOCK
    observed = []
    for c in range(blocks):
        cells = cell[c]
        above_row, column = split(cells, width)
        level, grid_row = split(above_row, height)
        _, local_row = split(grid_row, side)
        _, local_column = split(column, side)
        band, sub_row = split(local_row, BLOCK)
        high = level * BLOCK + sub_row
        low = band * side + local_column
        mine = [jnp.zeros((BLOCK, LANES), f32) for _ in range(members)]
        for h in range(hits):
            here = high == h
            for b in range(members):
                line = table[c, b * hits + h : b * hits + h + 1, :]
                line = jnp.broadcast_to(line, (BLOCK, LANES))
                mine[b] = jnp.where(here, pick_lanes(line, low), mine[b])
        observed.append(mine)
    for chip in range(blocks // 2):
        rows = [
            observed[(2 * chip + r - 1) % blocks][b] for b in range(members) for r in range(4)
        ]
        for i in range(0, len(rows), 2):
            at = 2 * region_rows + i * BLOCK
            send[chip, at : at + 2 * BLOCK, :] = jnp.concatenate(rows[i : i + 2], axis=0).astype(
                bf16
            )
    _, chip, _ = place()
    for s, chunk in enumerate(chunks):
        chunk[...] = send[chip ^ s]


def weights_body(
    lists, first, second, cell, value, variance, weights, values, planes, *, tiles, blocks, height, width, side
):
    tile = lax.axis_index("tile")
    block = lax.axis_index("member")
    own_lists = slice(24, 24 + lists.shape[0] * lists.shape[1] * lists.shape[2] // width)
    south, north = beside(first[own_lists, :], second[own_lists, :], tile)
    per_side = side // PATCH
    patches = per_side * per_side
    slots = lists.shape[2]
    depth = 3 * BLOCK
    rows, columns, sizes = [], [], []
    for r in range(3):
        column_block = wrapped(block + (r - 1), blocks)
        first = pl.multiple_of((column_block * tiles + tile) * BLOCK, BLOCK)
        cells = cell[pl.ds(first, BLOCK), :]
        above_row, column = split(cells, width)
        _, grid_row = split(above_row, height)
        rows.append(grid_row)
        columns.append(column)
        sizes.append(variance[pl.ds(first, BLOCK), :])
        values[r * BLOCK : (r + 1) * BLOCK, :] = value[pl.ds(first, BLOCK), :]
    grid_row = jnp.concatenate(rows, axis=0)
    column = jnp.concatenate(columns, axis=0)
    size = jnp.concatenate(sizes, axis=0)

    def pieces(dt, p):
        if dt == 0:
            return [lists[p // per_side, p % per_side : p % per_side + 1, :]]
        source = south if dt < 0 else north
        each = slots // width
        return [
            source[p * each + i : p * each + i + 1].astype(jnp.int32) for i in range(each)
        ]

    index = 0
    for dt in (0, -1, 1):
        for p in range(patches):
            count = jnp.zeros((depth, LANES), f32)
            for part in pieces(dt, p):
                length = part.shape[1]
                region, within = split(part, BLOCK * LANES)
                region_column, region_row = split(region, tiles)
                line, lane = split(within, LANES)
                near = wrapped(region_column - block + 1, blocks)
                fits = (part >= 0) & (region_row == tile) & (near < 3)
                line = jnp.where(fits, near * BLOCK + line, -1)
                one = (iota((depth, length), 0) == line).astype(f32).astype(bf16)
                other = (iota((LANES, length), 0) == lane).astype(f32).astype(bf16)
                count += lax.dot_general(
                    one, other, (((1,), (1,)), ((), ())), preferred_element_type=f32
                )
            patch_row = (tile + dt) * per_side + p // per_side
            patch_column = block * per_side + p % per_side
            row_gap = (grid_row - patch_row * PATCH - PATCH // 2).astype(f32) + 0.5
            turned = column - patch_column * PATCH - PATCH // 2 + width // 2
            column_gap = (wrapped(turned, width) - width // 2).astype(f32) + 0.5
            near = jnp.exp(
                -(row_gap * row_gap + column_gap * column_gap) / (2.0 * LOC_LEN * LOC_LEN)
            )
            planes[index * depth : (index + 1) * depth, :] = count * (near / size)
            index += 1
    for extra in range(index, 16):
        planes[extra * depth : (extra + 1) * depth, :] = jnp.zeros((depth, LANES), f32)
    for i in range(depth):
        weights[:, i * LANES : (i + 1) * LANES] = planes[pl.ds(i, 16, stride=depth), :]


def halves(values):
    high = values.astype(bf16)
    return high, (values - high.astype(f32)).astype(bf16)


def dot_rows(left, right):
    return lax.dot_general(left, right, (((1,), (1,)), ((), ())), preferred_element_type=f32)


def systems_body(*refs, patches, sources, members, region_rows):
    mine, theirs, weights, values, own, to_first, to_second = refs[:7]
    planes, tall_high, tall_low, wide_high, wide_low = refs[7:]
    depth = 3 * BLOCK
    each = 2 * mine.shape[0] // sources
    _, chip, core = place()
    ensemble = sources * members
    total = jnp.zeros((depth, LANES), f32)
    for s in range(sources):
        source, row = (mine, theirs)[s % 2], s // 2 * each
        both = source[row + region_rows : row + each, :].astype(f32)
        device = 2 * (chip ^ (s // 2)) + (core ^ (s % 2))
        at = pl.multiple_of(device * (members * depth), BLOCK)
        planes[pl.ds(at, members * depth), :] = both
        for b in range(members):
            total += both[b * depth : (b + 1) * depth, :]
    mean = total / ensemble
    for k in range(ensemble):
        planes[k * depth : (k + 1) * depth, :] -= mean
    planes[ensemble * depth : (ensemble + 1) * depth, :] = values[...] - mean
    for k in range(ensemble + 1, ensemble + 8):
        planes[k * depth : (k + 1) * depth, :] = jnp.zeros((depth, LANES), f32)
    for i in range(depth):
        at = slice(i * LANES, (i + 1) * LANES)
        tile = planes[pl.ds(i, ensemble + 8, stride=depth), :]
        high, low = halves(tile)
        wide_high[:, at] = high
        wide_low[:, at] = low
        spread = tile[0:ensemble, :]
        for p in range(3 * patches):
            high, low = halves(spread * weights[p : p + 1, at])
            tall_high[p * ensemble : (p + 1) * ensemble, at] = high
            tall_low[p * ensemble : (p + 1) * ensemble, at] = low
    result = (
        dot_rows(wide_high[...], tall_high[...])
        + dot_rows(wide_low[...], tall_high[...])
        + dot_rows(wide_high[...], tall_low[...])
    )
    count = patches * ensemble // 64
    even = lax.rem(lax.axis_index("tile"), 2) == 0
    found = []
    for n in range(3 * count):
        piece = result[:, n // 2 * LANES : (n // 2 + 1) * LANES] if n // 2 * LANES + LANES <= result.shape[1] else None
        if piece is None:
            piece = jnp.concatenate([result[:, n * 64 :], jnp.zeros((ensemble + 8, 64), f32)], axis=1)
        else:
            if n % 2:
                piece = pltpu.roll(piece, 64, 1)
            piece = jnp.where(iota(piece.shape, 1) < 64, piece, 0.0)
        found.append(piece)
    for i in range(count):
        at = slice(i * LANES, (i + 1) * LANES)
        own[:, at] = found[i]
        for_south, for_north = found[count + i], found[2 * count + i]
        to_first[:, at] = jnp.where(even, for_north, for_south)
        to_second[:, at] = jnp.where(even, for_south, for_north)


def analysis_body(*refs, patches, sources, members, region_rows):
    mine, theirs, own, first, second = refs[:5]
    chunks, (centred, factors) = refs[5:-2], refs[-2:]
    each = 2 * mine.shape[0] // sources
    _, chip, core = place()
    ensemble = sources * members
    hits = region_rows // members
    total = jnp.zeros((hits, LANES), f32)
    for s in range(sources):
        source, row = (mine, theirs)[s % 2], s // 2 * each
        device = 2 * (chip ^ (s // 2)) + (core ^ (s % 2))
        part = source[row : row + region_rows, :].astype(f32)
        for b in range(members):
            one = part[b * hits : (b + 1) * hits, :]
            centred[device * members + b] = one
            total += one
    mean = total / ensemble
    for k in range(ensemble):
        centred[k] -= mean

    count = patches * ensemble // 64
    group = 64 // ensemble
    row = iota((ensemble + 8, LANES), 0)
    lane = iota((ensemble + 8, LANES), 1)
    within = lane & (ensemble - 1)
    start = jnp.where(
        (row == within) & (row < ensemble), jnp.where(lane < 64, ensemble - 1.0, 1.0), 0.0
    )
    lane8 = iota((BLOCK, LANES), 1)
    group_start = (lane8 & 63) & ~(ensemble - 1)
    transforms = []
    for i in range(count):
        at = slice(i * LANES, (i + 1) * LANES)
        state = own[:, at] + first[:, at] + second[:, at] + start
        pivots = jnp.ones((ensemble, LANES), f32)
        for k in range(ensemble):
            column = pick_lanes(state, group_start + k)
            pivot = column[k : k + 1, :]
            scaled = state[k : k + 1, :] / pivot
            state = state - jnp.where(row > k, column, 0.0) * scaled
            pivots = jnp.where(row[0:ensemble] == k, pivot, pivots)
        inverse = state[0:ensemble, :] * lax.rsqrt(pivots)
        mean_weight = -state[ensemble : ensemble + 1, :]
        unit = jnp.where(row[0:ensemble] == within[0:ensemble], 1.0, 0.0)
        transforms.append(mean_weight + (ensemble - 1.0) ** 0.5 * inverse - unit)

    side_lanes = 32
    patch = (lane8 // (2 * side_lanes)) * 2 + (lane8 & (side_lanes - 1)) // PATCH
    inside = 64 + (patch & (group - 1)) * ensemble if group > 1 else 64 + 0 * patch
    which = patch // group
    for j in range(ensemble):
        chosen = pick_lanes(transforms[0], inside + j)
        for i in range(1, count):
            other = pick_lanes(transforms[i], inside + j)
            chosen = jnp.where(jnp.broadcast_to(which[0:1] == i, chosen.shape), other, chosen)
        factors[j] = chosen

    for s, chunk in enumerate(chunks):
        for c in (0, 1):
            first_member = (2 * (chip ^ s) + c) * members
            totals = [jnp.zeros((hits, LANES), f32) for _ in range(members)]
            for j in range(ensemble):
                centred_j = centred[j]
                for b in range(members):
                    totals[b] += factors[j, pl.ds(first_member + b, 1), :] * centred_j
            at = slice(c * region_rows, (c + 1) * region_rows)
            chunk[at, :] = jnp.concatenate(totals, axis=0).astype(bf16)


def output_body(forecast, mine, theirs, analysis, ordered):
    members, levels, side, width = forecast.shape
    _, chip, core = place()
    rows = ordered.shape[1]
    for s in range(mine.shape[0] // rows):
        at = slice(s * rows, (s + 1) * rows)
        ordered[2 * (chip ^ s) + core] = mine[at, :].astype(f32)
        ordered[2 * (chip ^ s) + (core ^ 1)] = theirs[at, :].astype(f32)
    for q in range(width // LANES):
        parts = [ordered[4 * q + c] for c in range(4)]
        at = slice(q * LANES, (q + 1) * LANES)
        for r, part in enumerate(transpose_chunks(parts)):
            rows = slice(r * BLOCK, (r + 1) * BLOCK)
            analysis[:, :, rows, at] = forecast[:, :, rows, at] + part.reshape(
                members, levels, BLOCK, LANES
            )


def shards(member_concentration, courant_pairs, obs_cell, obs_value, obs_error, obs_list):
    members, levels, side, width = member_concentration.shape
    blocks = lax.axis_size("member")
    tiles = lax.axis_size("tile")
    height = side * tiles
    ensemble = members * blocks
    per_side = side // PATCH
    patches = per_side * per_side
    slots = obs_list.shape[2]
    region_rows = members * levels * BLOCK
    depth = 3 * BLOCK
    all_rows = region_rows + members * depth
    chips = blocks // 2
    chip_rows = 2 * region_rows + members * 4 * BLOCK
    edge_rows = -(-(24 + patches * slots // width) // 8) * 8
    edge_shape = (members, levels, BLOCK, width)
    rate_shape = (2, levels, BLOCK, width)

    to_first, to_second = call(
        pack_edges,
        [((edge_rows, width), f32)] * 2,
        [
            pltpu.VMEM(edge_shape, f32),
            pltpu.VMEM(edge_shape, f32),
            pltpu.VMEM(rate_shape, f32),
            pltpu.VMEM(rate_shape, f32),
            pltpu.VMEM(obs_list.shape, jnp.int32),
            pltpu.SemaphoreType.DMA((5,)),
        ],
        specs=[pl.BlockSpec(memory_space=pltpu.HBM)] * 3,
        vmem=63,
    )(member_concentration, courant_pairs, obs_list)
    first, second = swap(to_first, to_second, tiles)

    flat = lambda array: array.reshape(-1, LANES)
    cell = flat(obs_cell)
    cell_row = lax.dynamic_index_in_dim(
        cell.reshape(blocks, tiles, BLOCK, LANES), lax.axis_index("tile"), 1, False
    )
    forecast, *chunks = call(
        functools.partial(forecast_body, tiles=tiles, height=height),
        [(member_concentration.shape, f32)] + [((chip_rows, LANES), bf16)] * chips,
        [
            pltpu.VMEM((chips, chip_rows, LANES), bf16),
            pltpu.VMEM((blocks, region_rows, LANES), f32),
        ],
    )(
        member_concentration,
        courant_pairs,
        first,
        second,
        cell_row,
    )
    received = exchange(chunks)
    share = functools.partial(share_body, region_rows=region_rows)
    mine, theirs = call(share, [((chips * all_rows, LANES), bf16)] * 2)(*received)
    theirs = swap_cores(theirs)
    weights, values = call(
        functools.partial(
            weights_body, tiles=tiles, blocks=blocks, height=height, width=width, side=side
        ),
        [((16, depth * LANES), f32), ((depth, LANES), f32)],
        [pltpu.VMEM((16 * depth, LANES), f32)],
        flops=100_000_000,
    )(obs_list, first, second, cell, flat(obs_value), flat(obs_error))

    sizes = dict(patches=patches, sources=blocks, members=members, region_rows=region_rows)
    tall = 3 * patches * ensemble
    system_shape = (ensemble + 8, patches * ensemble // 64 * LANES)
    own, to_first, to_second = call(
        functools.partial(systems_body, **sizes),
        [(system_shape, f32)] * 3,
        [
            pltpu.VMEM(((ensemble + 8) * depth, LANES), f32),
            pltpu.VMEM((tall, depth * LANES), bf16),
            pltpu.VMEM((tall, depth * LANES), bf16),
            pltpu.VMEM((ensemble + 8, depth * LANES), bf16),
            pltpu.VMEM((ensemble + 8, depth * LANES), bf16),
        ],
    )(mine, theirs, weights, values)
    first, second = swap(to_first, to_second, tiles)

    changes = call(
        functools.partial(analysis_body, **sizes),
        [((2 * region_rows, LANES), bf16)] * chips,
        [
            pltpu.VMEM((ensemble, levels * BLOCK, LANES), f32),
            pltpu.VMEM((ensemble, ensemble, LANES), f32),
        ],
    )(mine, theirs, own, first, second)
    returned = exchange(changes)
    mine, theirs = call(share, [((chips * region_rows, LANES), bf16)] * 2)(*returned)
    theirs = swap_cores(theirs)
    (analysis,) = call(
        output_body, [(forecast.shape, f32)], [pltpu.VMEM((blocks, region_rows, LANES), f32)]
    )(forecast, mine, theirs)
    return analysis


def solution(mesh):
    return jax.shard_map(
        shards,
        mesh=mesh,
        in_specs=(
            P("member", None, "tile", None),
            P(None, None, "tile", None),
            P(),
            P(),
            P(),
            P("tile", "member", None),
        ),
        out_specs=P("member", None, "tile", None),
        check_vma=False,
    )
```

```python
import functools

import jax
import jax.numpy as jnp
from jax import lax
from jax.experimental import pallas as pl
from jax.experimental.pallas import tpu as pltpu
from jax.sharding import PartitionSpec as P

PATCH = 16
LOC_LEN = 16
DIFFUSION = 0.05
LANES = 128
BLOCK = 8

f32 = jnp.float32
bf16 = jnp.bfloat16


def call(body, outs, scratch=(), flops=1_000_000, moved=1_000_000, specs=None, vmem=48):
    specs = {} if specs is None else {"in_specs": specs}
    return pl.pallas_call(
        body,
        **specs,
        out_shape=[jax.ShapeDtypeStruct(shape, kind) for shape, kind in outs],
        scratch_shapes=list(scratch),
        compiler_params=pltpu.CompilerParams(vmem_limit_bytes=vmem * 1024 * 1024),
        cost_estimate=pl.CostEstimate(flops=flops, bytes_accessed=moved, transcendentals=0),
    )


def split(number, size):
    if size & (size - 1) == 0:
        return number >> (size.bit_length() - 1), number & (size - 1)
    quotient = number // size
    return quotient, number - quotient * size


def wrapped(number, size):
    if size & (size - 1) == 0:
        return number & (size - 1)
    return lax.rem(number + size, size)


def iota(shape, axis):
    return lax.broadcasted_iota(jnp.int32, shape, axis)


def pick_lanes(values, index):
    rows = [
        jnp.take_along_axis(values[r : r + BLOCK], index, axis=1, mode="promise_in_bounds")
        for r in range(0, values.shape[0], BLOCK)
    ]
    return rows[0] if len(rows) == 1 else jnp.concatenate(rows, axis=0)


def transpose_chunks(parts):
    lane = iota(parts[0].shape, 1)
    low = lane < 64
    even = (lane & 32) == 0
    parts = list(parts)
    for i in (0, 1):
        a, b = parts[i], parts[i + 2]
        parts[i] = jnp.where(low, a, pltpu.roll(b, 64, 1))
        parts[i + 2] = jnp.where(low, pltpu.roll(a, 64, 1), b)
    for i in (0, 2):
        a, b = parts[i], parts[i + 1]
        parts[i] = jnp.where(even, a, pltpu.roll(b, 32, 1))
        parts[i + 1] = jnp.where(even, pltpu.roll(a, 96, 1), b)
    return parts


def pack_edges(
    tracer, courant, lists, to_first, to_second, first, last, first_rates, last_rates, numbers, arrived
):
    members, levels, side, width = tracer.shape
    copies = [
        pltpu.make_async_copy(source, target, arrived.at[i])
        for i, (source, target) in enumerate(
            (
                (tracer.at[:, :, 0:BLOCK, :], first),
                (tracer.at[:, :, side - BLOCK : side, :], last),
                (courant.at[:, :, 0:BLOCK, :], first_rates),
                (courant.at[:, :, side - BLOCK : side, :], last_rates),
                (lists, numbers),
            )
        )
    ]
    for copy in copies:
        copy.start()
    for copy in copies:
        copy.wait()
    odd = lax.rem(lax.axis_index("tile"), 2) == 1

    def put(row, low, high):
        to_first[row : row + 1, :] = jnp.where(odd, high, low)
        to_second[row : row + 1, :] = jnp.where(odd, low, high)

    end = BLOCK - 1
    for b in range(members):
        for l in range(levels):
            row = b * levels + l
            put(row, first[b, l, 0:1, :], last[b, l, end : end + 1, :])
            put(8 + row, first[b, l, 1:2, :], last[b, l, end - 1 : end, :])
    for c in range(2):
        for l in range(levels):
            put(16 + c * levels + l, first_rates[c, l, 0:1, :], last_rates[c, l, end : end + 1, :])
    row = 24
    for a in range(numbers.shape[0]):
        for b in range(numbers.shape[1]):
            for s in range(0, numbers.shape[2], width):
                part = numbers[a, b : b + 1, s : s + width].astype(f32)
                to_first[row : row + 1, :] = part
                to_second[row : row + 1, :] = part
                row += 1


def coefficients(meridional, zonal):
    return (
        (1.0 - 4.0 * DIFFUSION) - jnp.abs(zonal) - jnp.abs(meridional),
        DIFFUSION + jnp.maximum(zonal, 0.0),
        DIFFUSION - jnp.minimum(zonal, 0.0),
        DIFFUSION + jnp.maximum(meridional, 0.0),
        DIFFUSION - jnp.minimum(meridional, 0.0),
    )


def stencil(current, south, north, factors):
    width = current.shape[1]
    centre, from_west, from_east, from_south, from_north = factors
    west = pltpu.roll(current, 1, 1)
    east = pltpu.roll(current, width - 1, 1)
    return (
        centre * current
        + from_west * west
        + from_east * east
        + from_south * south
        + from_north * north
    )


def beside(first, second, tile):
    odd = lax.rem(tile, 2) == 1
    return jnp.where(odd, second, first), jnp.where(odd, first, second)


def swap(first, second, tiles):
    pairs = lambda start: [
        pair for i in range(start, tiles - 1, 2) for pair in ((i, i + 1), (i + 1, i))
    ]
    return lax.ppermute(first, "tile", pairs(1)), lax.ppermute(second, "tile", pairs(0))


def exchange(chunks):
    chips = len(chunks)
    device = lambda chip, core: 2 * chip + core
    swaps = lambda s: [(device(i, c), device(i ^ s, c)) for i in range(chips) for c in (0, 1)]
    received = {s: lax.ppermute(chunks[s], "member", swaps(s)) for s in range(chips - 1, 0, -1)}
    return [chunks[0]] + [received[s] for s in range(1, chips)]


def swap_cores(array):
    return lax.ppermute(array, "member", [(i, i ^ 1) for i in range(lax.axis_size("member"))])


def place():
    block = lax.axis_index("member")
    core = lax.rem(block, 2)
    return block, (block - core) // 2, core


def share_body(*refs, region_rows):
    chunks, (own, other) = refs[:-2], refs[-2:]
    _, _, core = place()
    first = core == 0
    each = own.shape[0] // len(chunks)
    half = chunks[0].shape[0] - 2 * region_rows
    lines = half // 2
    for s, chunk in enumerate(chunks):
        low, high = chunk[0:region_rows, :], chunk[region_rows : 2 * region_rows, :]
        row = s * each
        own[row : row + region_rows, :] = jnp.where(first, low, high)
        other[row : row + region_rows, :] = jnp.where(first, high, low)
        if each == region_rows:
            continue
        seen = chunk[2 * region_rows :, :].astype(f32)
        west = jnp.concatenate([seen[0 : lines - 8], seen[lines : 2 * lines - 8]], axis=0)
        east = jnp.concatenate([seen[8:lines], seen[lines + 8 : 2 * lines]], axis=0)
        own[row + region_rows : row + each, :] = jnp.where(first, west, east).astype(bf16)
        other[row + region_rows : row + each, :] = jnp.where(first, east, west).astype(bf16)


def forecast_body(
    tracer, courant, first, second, cell, forecast, *rest, tiles, height
):
    *chunks, send, table = rest
    members, levels, side, width = tracer.shape
    blocks = width // side
    tile = lax.axis_index("tile")
    planes = members * levels

    south, north = beside(first[0:24, :], second[0:24, :], tile)
    own = lambda at: jnp.concatenate(
        [tracer[b, l, at : at + 1, :] for b in range(members) for l in range(levels)], axis=0
    )
    inside_south, inside_north = tile > 0, tile < tiles - 1
    low, lowest = south[0:planes], south[8 : 8 + planes]
    high, highest = north[0:planes], north[8 : 8 + planes]

    def edge(source):
        twice = lambda at: jnp.concatenate([source[at : at + levels]] * members, axis=0)
        return coefficients(twice(16), twice(16 + levels))

    below = stencil(low, lowest, own(0), edge(south))
    above = stencil(high, own(side - 1), highest, edge(north))
    below = jnp.where(inside_south, below, 0.0)
    above = jnp.where(inside_north, above, 0.0)
    row = iota((side, width), 0)
    for l in range(levels):
        factors = coefficients(courant[0, l], courant[1, l])
        for b in range(members):
            plane = b * levels + l
            current = tracer[b, l]
            for under, over in ((low, high), (below, above)):
                under, over = under[plane : plane + 1, :], over[plane : plane + 1, :]
                lower = jnp.where(row == 0, under, pltpu.roll(current, 1, 0))
                upper = jnp.where(row == side - 1, over, pltpu.roll(current, side - 1, 0))
                current = stencil(current, lower, upper, factors)
            forecast[b, l] = current

    region_rows = planes * BLOCK
    for q in range(width // LANES):
        parts = [
            forecast[:, :, r : r + BLOCK, q * LANES : (q + 1) * LANES].reshape(region_rows, LANES)
            for r in range(0, side, BLOCK)
        ]
        for i, part in enumerate(transpose_chunks(parts)):
            c = 4 * q + i
            rounded = part.astype(bf16)
            send[c // 2, c % 2 * region_rows : (c % 2 + 1) * region_rows, :] = rounded
            table[c] = rounded.astype(f32)

    hits = levels * BLOCK
    observed = []
    for c in range(blocks):
        cells = cell[c]
        above_row, column = split(cells, width)
        level, grid_row = split(above_row, height)
        _, local_row = split(grid_row, side)
        _, local_column = split(column, side)
        band, sub_row = split(local_row, BLOCK)
        high = level * BLOCK + sub_row
        low = band * side + local_column
        mine = [jnp.zeros((BLOCK, LANES), f32) for _ in range(members)]
        for h in range(hits):
            here = high == h
            for b in range(members):
                line = table[c, b * hits + h : b * hits + h + 1, :]
                line = jnp.broadcast_to(line, (BLOCK, LANES))
                mine[b] = jnp.where(here, pick_lanes(line, low), mine[b])
        observed.append(mine)
    for chip in range(blocks // 2):
        rows = [
            observed[(2 * chip + r - 1) % blocks][b] for b in range(members) for r in range(4)
        ]
        for i in range(0, len(rows), 2):
            at = 2 * region_rows + i * BLOCK
            send[chip, at : at + 2 * BLOCK, :] = jnp.concatenate(rows[i : i + 2], axis=0).astype(
                bf16
            )
    _, chip, _ = place()
    for s, chunk in enumerate(chunks):
        chunk[...] = send[chip ^ s]


def weights_body(
    lists, first, second, cell, value, variance, weights, values, planes, *, tiles, blocks, height, width, side
):
    tile = lax.axis_index("tile")
    block = lax.axis_index("member")
    own_lists = slice(24, 24 + lists.shape[0] * lists.shape[1] * lists.shape[2] // width)
    south, north = beside(first[own_lists, :], second[own_lists, :], tile)
    per_side = side // PATCH
    patches = per_side * per_side
    slots = lists.shape[2]
    depth = 3 * BLOCK
    rows, columns, sizes = [], [], []
    for r in range(3):
        column_block = wrapped(block + (r - 1), blocks)
        first = pl.multiple_of((column_block * tiles + tile) * BLOCK, BLOCK)
        cells = cell[pl.ds(first, BLOCK), :]
        above_row, column = split(cells, width)
        _, grid_row = split(above_row, height)
        rows.append(grid_row)
        columns.append(column)
        sizes.append(variance[pl.ds(first, BLOCK), :])
        values[r * BLOCK : (r + 1) * BLOCK, :] = value[pl.ds(first, BLOCK), :]
    grid_row = jnp.concatenate(rows, axis=0)
    column = jnp.concatenate(columns, axis=0)
    size = jnp.concatenate(sizes, axis=0)

    def pieces(dt, p):
        if dt == 0:
            return [lists[p // per_side, p % per_side : p % per_side + 1, :]]
        source = south if dt < 0 else north
        each = slots // width
        return [
            source[p * each + i : p * each + i + 1].astype(jnp.int32) for i in range(each)
        ]

    index = 0
    for dt in (0, -1, 1):
        for p in range(patches):
            count = jnp.zeros((depth, LANES), f32)
            for part in pieces(dt, p):
                length = part.shape[1]
                region, within = split(part, BLOCK * LANES)
                region_column, region_row = split(region, tiles)
                line, lane = split(within, LANES)
                near = wrapped(region_column - block + 1, blocks)
                fits = (part >= 0) & (region_row == tile) & (near < 3)
                line = jnp.where(fits, near * BLOCK + line, -1)
                one = (iota((depth, length), 0) == line).astype(f32).astype(bf16)
                other = (iota((LANES, length), 0) == lane).astype(f32).astype(bf16)
                count += lax.dot_general(
                    one, other, (((1,), (1,)), ((), ())), preferred_element_type=f32
                )
            patch_row = (tile + dt) * per_side + p // per_side
            patch_column = block * per_side + p % per_side
            row_gap = (grid_row - patch_row * PATCH - PATCH // 2).astype(f32) + 0.5
            turned = column - patch_column * PATCH - PATCH // 2 + width // 2
            column_gap = (wrapped(turned, width) - width // 2).astype(f32) + 0.5
            near = jnp.exp(
                -(row_gap * row_gap + column_gap * column_gap) / (2.0 * LOC_LEN * LOC_LEN)
            )
            planes[index * depth : (index + 1) * depth, :] = count * (near / size)
            index += 1
    for extra in range(index, 16):
        planes[extra * depth : (extra + 1) * depth, :] = jnp.zeros((depth, LANES), f32)
    for i in range(depth):
        weights[:, i * LANES : (i + 1) * LANES] = planes[pl.ds(i, 16, stride=depth), :]


def halves(values):
    high = values.astype(bf16)
    return high, (values - high.astype(f32)).astype(bf16)


def dot_rows(left, right):
    return lax.dot_general(left, right, (((1,), (1,)), ((), ())), preferred_element_type=f32)


def systems_body(*refs, patches, sources, members, region_rows):
    mine, theirs, weights, values, own, to_first, to_second = refs[:7]
    planes, tall_high, tall_low, wide_high, wide_low = refs[7:]
    depth = 3 * BLOCK
    each = 2 * mine.shape[0] // sources
    _, chip, core = place()
    ensemble = sources * members
    total = jnp.zeros((depth, LANES), f32)
    for s in range(sources):
        source, row = (mine, theirs)[s % 2], s // 2 * each
        both = source[row + region_rows : row + each, :].astype(f32)
        device = 2 * (chip ^ (s // 2)) + (core ^ (s % 2))
        at = pl.multiple_of(device * (members * depth), BLOCK)
        planes[pl.ds(at, members * depth), :] = both
        for b in range(members):
            total += both[b * depth : (b + 1) * depth, :]
    mean = total / ensemble
    for k in range(ensemble):
        planes[k * depth : (k + 1) * depth, :] -= mean
    planes[ensemble * depth : (ensemble + 1) * depth, :] = values[...] - mean
    for k in range(ensemble + 1, ensemble + 8):
        planes[k * depth : (k + 1) * depth, :] = jnp.zeros((depth, LANES), f32)
    for i in range(depth):
        at = slice(i * LANES, (i + 1) * LANES)
        tile = planes[pl.ds(i, ensemble + 8, stride=depth), :]
        high, low = halves(tile)
        wide_high[:, at] = high
        wide_low[:, at] = low
        spread = tile[0:ensemble, :]
        for p in range(3 * patches):
            high, low = halves(spread * weights[p : p + 1, at])
            tall_high[p * ensemble : (p + 1) * ensemble, at] = high
            tall_low[p * ensemble : (p + 1) * ensemble, at] = low
    result = (
        dot_rows(wide_high[...], tall_high[...])
        + dot_rows(wide_low[...], tall_high[...])
        + dot_rows(wide_high[...], tall_low[...])
    )
    count = patches * ensemble // 64
    odd = lax.rem(lax.axis_index("tile"), 2) == 1
    found = []
    for n in range(3 * count):
        piece = result[:, n // 2 * LANES : (n // 2 + 1) * LANES] if n // 2 * LANES + LANES <= result.shape[1] else None
        if piece is None:
            piece = jnp.concatenate([result[:, n * 64 :], jnp.zeros((ensemble + 8, 64), f32)], axis=1)
        else:
            if n % 2:
                piece = pltpu.roll(piece, 64, 1)
            piece = jnp.where(iota(piece.shape, 1) < 64, piece, 0.0)
        found.append(piece)
    for i in range(count):
        at = slice(i * LANES, (i + 1) * LANES)
        own[:, at] = found[i]
        for_south, for_north = found[count + i], found[2 * count + i]
        to_first[:, at] = jnp.where(odd, for_north, for_south)
        to_second[:, at] = jnp.where(odd, for_south, for_north)


def analysis_body(*refs, patches, sources, members, region_rows):
    mine, theirs, own, first, second = refs[:5]
    chunks, (centred, factors) = refs[5:-2], refs[-2:]
    each = 2 * mine.shape[0] // sources
    _, chip, core = place()
    ensemble = sources * members
    hits = region_rows // members
    total = jnp.zeros((hits, LANES), f32)
    for s in range(sources):
        source, row = (mine, theirs)[s % 2], s // 2 * each
        device = 2 * (chip ^ (s // 2)) + (core ^ (s % 2))
        part = source[row : row + region_rows, :].astype(f32)
        for b in range(members):
            one = part[b * hits : (b + 1) * hits, :]
            centred[device * members + b] = one
            total += one
    mean = total / ensemble
    for k in range(ensemble):
        centred[k] -= mean

    count = patches * ensemble // 64
    group = 64 // ensemble
    row = iota((ensemble + 8, LANES), 0)
    lane = iota((ensemble + 8, LANES), 1)
    within = lane & (ensemble - 1)
    start = jnp.where(
        (row == within) & (row < ensemble), jnp.where(lane < 64, ensemble - 1.0, 1.0), 0.0
    )
    lane8 = iota((BLOCK, LANES), 1)
    group_start = (lane8 & 63) & ~(ensemble - 1)
    transforms = []
    for i in range(count):
        at = slice(i * LANES, (i + 1) * LANES)
        state = own[:, at] + first[:, at] + second[:, at] + start
        pivots = jnp.ones((ensemble, LANES), f32)
        for k in range(ensemble):
            column = pick_lanes(state, group_start + k)
            pivot = column[k : k + 1, :]
            scaled = state[k : k + 1, :] / pivot
            state = state - jnp.where(row > k, column, 0.0) * scaled
            pivots = jnp.where(row[0:ensemble] == k, pivot, pivots)
        inverse = state[0:ensemble, :] * lax.rsqrt(pivots)
        mean_weight = -state[ensemble : ensemble + 1, :]
        unit = jnp.where(row[0:ensemble] == within[0:ensemble], 1.0, 0.0)
        transforms.append(mean_weight + (ensemble - 1.0) ** 0.5 * inverse - unit)

    side_lanes = 32
    patch = (lane8 // (2 * side_lanes)) * 2 + (lane8 & (side_lanes - 1)) // PATCH
    inside = 64 + (patch & (group - 1)) * ensemble if group > 1 else 64 + 0 * patch
    which = patch // group
    for j in range(ensemble):
        chosen = pick_lanes(transforms[0], inside + j)
        for i in range(1, count):
            other = pick_lanes(transforms[i], inside + j)
            chosen = jnp.where(jnp.broadcast_to(which[0:1] == i, chosen.shape), other, chosen)
        factors[j] = chosen

    for s, chunk in enumerate(chunks):
        for c in (0, 1):
            first_member = (2 * (chip ^ s) + c) * members
            totals = [jnp.zeros((hits, LANES), f32) for _ in range(members)]
            for j in range(ensemble):
                centred_j = centred[j]
                for b in range(members):
                    totals[b] += factors[j, pl.ds(first_member + b, 1), :] * centred_j
            at = slice(c * region_rows, (c + 1) * region_rows)
            chunk[at, :] = jnp.concatenate(totals, axis=0).astype(bf16)


def output_body(forecast, mine, theirs, analysis, ordered):
    members, levels, side, width = forecast.shape
    _, chip, core = place()
    rows = ordered.shape[1]
    for s in range(mine.shape[0] // rows):
        at = slice(s * rows, (s + 1) * rows)
        ordered[2 * (chip ^ s) + core] = mine[at, :].astype(f32)
        ordered[2 * (chip ^ s) + (core ^ 1)] = theirs[at, :].astype(f32)
    for q in range(width // LANES):
        parts = [ordered[4 * q + c] for c in range(4)]
        at = slice(q * LANES, (q + 1) * LANES)
        for r, part in enumerate(transpose_chunks(parts)):
            rows = slice(r * BLOCK, (r + 1) * BLOCK)
            analysis[:, :, rows, at] = forecast[:, :, rows, at] + part.reshape(
                members, levels, BLOCK, LANES
            )


def shards(member_concentration, courant_pairs, obs_cell, obs_value, obs_error, obs_list):
    members, levels, side, width = member_concentration.shape
    blocks = lax.axis_size("member")
    tiles = lax.axis_size("tile")
    height = side * tiles
    ensemble = members * blocks
    per_side = side // PATCH
    patches = per_side * per_side
    slots = obs_list.shape[2]
    region_rows = members * levels * BLOCK
    depth = 3 * BLOCK
    all_rows = region_rows + members * depth
    chips = blocks // 2
    chip_rows = 2 * region_rows + members * 4 * BLOCK
    edge_rows = -(-(24 + patches * slots // width) // 8) * 8
    edge_shape = (members, levels, BLOCK, width)
    rate_shape = (2, levels, BLOCK, width)

    to_first, to_second = call(
        pack_edges,
        [((edge_rows, width), f32)] * 2,
        [
            pltpu.VMEM(edge_shape, f32),
            pltpu.VMEM(edge_shape, f32),
            pltpu.VMEM(rate_shape, f32),
            pltpu.VMEM(rate_shape, f32),
            pltpu.VMEM(obs_list.shape, jnp.int32),
            pltpu.SemaphoreType.DMA((5,)),
        ],
        specs=[pl.BlockSpec(memory_space=pltpu.HBM)] * 3,
        vmem=63,
    )(member_concentration, courant_pairs, obs_list)
    first, second = swap(to_first, to_second, tiles)

    flat = lambda array: array.reshape(-1, LANES)
    cell = flat(obs_cell)
    cell_row = lax.dynamic_index_in_dim(
        cell.reshape(blocks, tiles, BLOCK, LANES), lax.axis_index("tile"), 1, False
    )
    forecast, *chunks = call(
        functools.partial(forecast_body, tiles=tiles, height=height),
        [(member_concentration.shape, f32)] + [((chip_rows, LANES), bf16)] * chips,
        [
            pltpu.VMEM((chips, chip_rows, LANES), bf16),
            pltpu.VMEM((blocks, region_rows, LANES), f32),
        ],
    )(
        member_concentration,
        courant_pairs,
        first,
        second,
        cell_row,
    )
    received = exchange(chunks)
    share = functools.partial(share_body, region_rows=region_rows)
    mine, theirs = call(share, [((chips * all_rows, LANES), bf16)] * 2)(*received)
    theirs = swap_cores(theirs)
    weights, values = call(
        functools.partial(
            weights_body, tiles=tiles, blocks=blocks, height=height, width=width, side=side
        ),
        [((16, depth * LANES), f32), ((depth, LANES), f32)],
        [pltpu.VMEM((16 * depth, LANES), f32)],
        flops=100_000_000,
    )(obs_list, first, second, cell, flat(obs_value), flat(obs_error))

    sizes = dict(patches=patches, sources=blocks, members=members, region_rows=region_rows)
    tall = 3 * patches * ensemble
    system_shape = (ensemble + 8, patches * ensemble // 64 * LANES)
    own, to_first, to_second = call(
        functools.partial(systems_body, **sizes),
        [(system_shape, f32)] * 3,
        [
            pltpu.VMEM(((ensemble + 8) * depth, LANES), f32),
            pltpu.VMEM((tall, depth * LANES), bf16),
            pltpu.VMEM((tall, depth * LANES), bf16),
            pltpu.VMEM((ensemble + 8, depth * LANES), bf16),
            pltpu.VMEM((ensemble + 8, depth * LANES), bf16),
        ],
    )(mine, theirs, weights, values)
    first, second = swap(to_first, to_second, tiles)

    changes = call(
        functools.partial(analysis_body, **sizes),
        [((2 * region_rows, LANES), bf16)] * chips,
        [
            pltpu.VMEM((ensemble, levels * BLOCK, LANES), f32),
            pltpu.VMEM((ensemble, ensemble, LANES), f32),
        ],
    )(mine, theirs, own, first, second)
    returned = exchange(changes)
    mine, theirs = call(share, [((chips * region_rows, LANES), bf16)] * 2)(*returned)
    theirs = swap_cores(theirs)
    (analysis,) = call(
        output_body, [(forecast.shape, f32)], [pltpu.VMEM((blocks, region_rows, LANES), f32)]
    )(forecast, mine, theirs)
    return analysis


def solution(mesh):
    return jax.shard_map(
        shards,
        mesh=mesh,
        in_specs=(
            P("member", None, "tile", None),
            P(None, None, "tile", None),
            P(),
            P(),
            P(),
            P("tile", "member", None),
        ),
        out_specs=P("member", None, "tile", None),
        check_vma=False,
    )
```

```python
import functools

import jax
import jax.numpy as jnp
from jax import lax
from jax.experimental import pallas as pl
from jax.experimental.pallas import tpu as pltpu
from jax.sharding import PartitionSpec as P

PATCH = 16
LOC_LEN = 16
DIFFUSION = 0.05
LANES = 128
BLOCK = 8

f32 = jnp.float32
bf16 = jnp.bfloat16


def call(body, outs, scratch=(), flops=1_000_000, moved=1_000_000, specs=None, vmem=48):
    specs = {} if specs is None else {"in_specs": specs}
    return pl.pallas_call(
        body,
        **specs,
        out_shape=[jax.ShapeDtypeStruct(shape, kind) for shape, kind in outs],
        scratch_shapes=list(scratch),
        compiler_params=pltpu.CompilerParams(vmem_limit_bytes=vmem * 1024 * 1024),
        cost_estimate=pl.CostEstimate(flops=flops, bytes_accessed=moved, transcendentals=0),
    )


def split(number, size):
    if size & (size - 1) == 0:
        return number >> (size.bit_length() - 1), number & (size - 1)
    quotient = number // size
    return quotient, number - quotient * size


def wrapped(number, size):
    if size & (size - 1) == 0:
        return number & (size - 1)
    return lax.rem(number + size, size)


def iota(shape, axis):
    return lax.broadcasted_iota(jnp.int32, shape, axis)


def pick_lanes(values, index):
    rows = [
        jnp.take_along_axis(values[r : r + BLOCK], index, axis=1, mode="promise_in_bounds")
        for r in range(0, values.shape[0], BLOCK)
    ]
    return rows[0] if len(rows) == 1 else jnp.concatenate(rows, axis=0)


def transpose_chunks(parts):
    lane = iota(parts[0].shape, 1)
    low = lane < 64
    even = (lane & 32) == 0
    parts = list(parts)
    for i in (0, 1):
        a, b = parts[i], parts[i + 2]
        parts[i] = jnp.where(low, a, pltpu.roll(b, 64, 1))
        parts[i + 2] = jnp.where(low, pltpu.roll(a, 64, 1), b)
    for i in (0, 2):
        a, b = parts[i], parts[i + 1]
        parts[i] = jnp.where(even, a, pltpu.roll(b, 32, 1))
        parts[i + 1] = jnp.where(even, pltpu.roll(a, 96, 1), b)
    return parts


def pack_edges(
    tracer, courant, lists, to_first, to_second, first, last, first_rates, last_rates, numbers, arrived
):
    members, levels, side, width = tracer.shape
    copies = [
        pltpu.make_async_copy(source, target, arrived.at[i])
        for i, (source, target) in enumerate(
            (
                (tracer.at[:, :, 0:BLOCK, :], first),
                (tracer.at[:, :, side - BLOCK : side, :], last),
                (courant.at[:, :, 0:BLOCK, :], first_rates),
                (courant.at[:, :, side - BLOCK : side, :], last_rates),
                (lists, numbers),
            )
        )
    ]
    for copy in copies:
        copy.start()
    for copy in copies:
        copy.wait()
    even = lax.rem(lax.axis_index("tile"), 2) == 0

    def put(row, low, high):
        to_first[row : row + 1, :] = jnp.where(even, high, low)
        to_second[row : row + 1, :] = jnp.where(even, low, high)

    end = BLOCK - 1
    for b in range(members):
        for l in range(levels):
            row = b * levels + l
            put(row, first[b, l, 0:1, :], last[b, l, end : end + 1, :])
            put(8 + row, first[b, l, 1:2, :], last[b, l, end - 1 : end, :])
    for c in range(2):
        for l in range(levels):
            put(16 + c * levels + l, first_rates[c, l, 0:1, :], last_rates[c, l, end : end + 1, :])
    row = 24
    for a in range(numbers.shape[0]):
        for b in range(numbers.shape[1]):
            for s in range(0, numbers.shape[2], width):
                part = numbers[a, b : b + 1, s : s + width].astype(f32)
                to_first[row : row + 1, :] = part
                to_second[row : row + 1, :] = part
                row += 1


def coefficients(meridional, zonal):
    return (
        (1.0 - 4.0 * DIFFUSION) - jnp.abs(zonal) - jnp.abs(meridional),
        DIFFUSION + jnp.maximum(zonal, 0.0),
        DIFFUSION - jnp.minimum(zonal, 0.0),
        DIFFUSION + jnp.maximum(meridional, 0.0),
        DIFFUSION - jnp.minimum(meridional, 0.0),
    )


def stencil(current, south, north, factors):
    width = current.shape[1]
    centre, from_west, from_east, from_south, from_north = factors
    west = pltpu.roll(current, 1, 1)
    east = pltpu.roll(current, width - 1, 1)
    return (
        centre * current
        + from_west * west
        + from_east * east
        + from_south * south
        + from_north * north
    )


def beside(first, second, tile):
    even = lax.rem(tile, 2) == 0
    return jnp.where(even, second, first), jnp.where(even, first, second)


def swap(first, second, tiles):
    pairs = lambda start: [
        pair for i in range(start, tiles - 1, 2) for pair in ((i, i + 1), (i + 1, i))
    ]
    return lax.ppermute(first, "tile", pairs(0)), lax.ppermute(second, "tile", pairs(1))


def exchange(chunks):
    chips = chunks.shape[0]
    groups = [[2 * i + core for i in range(chips)] for core in (0, 1)]
    return lax.all_to_all(
        chunks, "member", split_axis=0, concat_axis=0, axis_index_groups=groups, tiled=True
    )


def swap_cores(array):
    return lax.ppermute(array, "member", [(i, i ^ 1) for i in range(lax.axis_size("member"))])


def place():
    block = lax.axis_index("member")
    core = lax.rem(block, 2)
    return block, (block - core) // 2, core


def share_body(*refs, region_rows):
    chunks, (own, other) = refs[0], refs[-2:]
    _, _, core = place()
    first = core == 0
    chips, chip_rows, _ = chunks.shape
    each = own.shape[0] // chips
    half = chip_rows - 2 * region_rows
    lines = half // 2
    for s in range(chips):
        chunk = chunks.at[s]
        low, high = chunk[0:region_rows, :], chunk[region_rows : 2 * region_rows, :]
        row = s * each
        own[row : row + region_rows, :] = jnp.where(first, low, high)
        other[row : row + region_rows, :] = jnp.where(first, high, low)
        if each == region_rows:
            continue
        seen = chunk[2 * region_rows :, :].astype(f32)
        west = jnp.concatenate([seen[0 : lines - 8], seen[lines : 2 * lines - 8]], axis=0)
        east = jnp.concatenate([seen[8:lines], seen[lines + 8 : 2 * lines]], axis=0)
        own[row + region_rows : row + each, :] = jnp.where(first, west, east).astype(bf16)
        other[row + region_rows : row + each, :] = jnp.where(first, east, west).astype(bf16)


def forecast_body(
    tracer, courant, first, second, cell, forecast, *rest, tiles, height
):
    send, table = rest
    members, levels, side, width = tracer.shape
    blocks = width // side
    tile = lax.axis_index("tile")
    planes = members * levels

    south, north = beside(first[0:24, :], second[0:24, :], tile)
    own = lambda at: jnp.concatenate(
        [tracer[b, l, at : at + 1, :] for b in range(members) for l in range(levels)], axis=0
    )
    inside_south, inside_north = tile > 0, tile < tiles - 1
    low, lowest = south[0:planes], south[8 : 8 + planes]
    high, highest = north[0:planes], north[8 : 8 + planes]

    def edge(source):
        twice = lambda at: jnp.concatenate([source[at : at + levels]] * members, axis=0)
        return coefficients(twice(16), twice(16 + levels))

    below = stencil(low, lowest, own(0), edge(south))
    above = stencil(high, own(side - 1), highest, edge(north))
    below = jnp.where(inside_south, below, 0.0)
    above = jnp.where(inside_north, above, 0.0)
    row = iota((side, width), 0)
    for l in range(levels):
        factors = coefficients(courant[0, l], courant[1, l])
        for b in range(members):
            plane = b * levels + l
            current = tracer[b, l]
            for under, over in ((low, high), (below, above)):
                under, over = under[plane : plane + 1, :], over[plane : plane + 1, :]
                lower = jnp.where(row == 0, under, pltpu.roll(current, 1, 0))
                upper = jnp.where(row == side - 1, over, pltpu.roll(current, side - 1, 0))
                current = stencil(current, lower, upper, factors)
            forecast[b, l] = current

    region_rows = planes * BLOCK
    for q in range(width // LANES):
        parts = [
            forecast[:, :, r : r + BLOCK, q * LANES : (q + 1) * LANES].reshape(region_rows, LANES)
            for r in range(0, side, BLOCK)
        ]
        for i, part in enumerate(transpose_chunks(parts)):
            c = 4 * q + i
            rounded = part.astype(bf16)
            send[c // 2, c % 2 * region_rows : (c % 2 + 1) * region_rows, :] = rounded
            table[c] = rounded.astype(f32)

    hits = levels * BLOCK
    observed = []
    for c in range(blocks):
        cells = cell[c]
        above_row, column = split(cells, width)
        level, grid_row = split(above_row, height)
        _, local_row = split(grid_row, side)
        _, local_column = split(column, side)
        band, sub_row = split(local_row, BLOCK)
        high = level * BLOCK + sub_row
        low = band * side + local_column
        mine = [jnp.zeros((BLOCK, LANES), f32) for _ in range(members)]
        for h in range(hits):
            here = high == h
            for b in range(members):
                line = table[c, b * hits + h : b * hits + h + 1, :]
                line = jnp.broadcast_to(line, (BLOCK, LANES))
                mine[b] = jnp.where(here, pick_lanes(line, low), mine[b])
        observed.append(mine)
    for chip in range(blocks // 2):
        rows = [
            observed[(2 * chip + r - 1) % blocks][b] for b in range(members) for r in range(4)
        ]
        for i in range(0, len(rows), 2):
            at = 2 * region_rows + i * BLOCK
            send[chip, at : at + 2 * BLOCK, :] = jnp.concatenate(rows[i : i + 2], axis=0).astype(
                bf16
            )


def weights_body(
    lists, first, second, cell, value, variance, weights, values, planes, *, tiles, blocks, height, width, side
):
    tile = lax.axis_index("tile")
    block = lax.axis_index("member")
    own_lists = slice(24, 24 + lists.shape[0] * lists.shape[1] * lists.shape[2] // width)
    south, north = beside(first[own_lists, :], second[own_lists, :], tile)
    per_side = side // PATCH
    patches = per_side * per_side
    slots = lists.shape[2]
    depth = 3 * BLOCK
    rows, columns, sizes = [], [], []
    for r in range(3):
        column_block = wrapped(block + (r - 1), blocks)
        first = pl.multiple_of((column_block * tiles + tile) * BLOCK, BLOCK)
        cells = cell[pl.ds(first, BLOCK), :]
        above_row, column = split(cells, width)
        _, grid_row = split(above_row, height)
        rows.append(grid_row)
        columns.append(column)
        sizes.append(variance[pl.ds(first, BLOCK), :])
        values[r * BLOCK : (r + 1) * BLOCK, :] = value[pl.ds(first, BLOCK), :]
    grid_row = jnp.concatenate(rows, axis=0)
    column = jnp.concatenate(columns, axis=0)
    size = jnp.concatenate(sizes, axis=0)

    def pieces(dt, p):
        if dt == 0:
            return [lists[p // per_side, p % per_side : p % per_side + 1, :]]
        source = south if dt < 0 else north
        each = slots // width
        return [
            source[p * each + i : p * each + i + 1].astype(jnp.int32) for i in range(each)
        ]

    index = 0
    for dt in (0, -1, 1):
        for p in range(patches):
            count = jnp.zeros((depth, LANES), f32)
            for part in pieces(dt, p):
                length = part.shape[1]
                region, within = split(part, BLOCK * LANES)
                region_column, region_row = split(region, tiles)
                line, lane = split(within, LANES)
                near = wrapped(region_column - block + 1, blocks)
                fits = (part >= 0) & (region_row == tile) & (near < 3)
                line = jnp.where(fits, near * BLOCK + line, -1)
                one = (iota((depth, length), 0) == line).astype(f32).astype(bf16)
                other = (iota((LANES, length), 0) == lane).astype(f32).astype(bf16)
                count += lax.dot_general(
                    one, other, (((1,), (1,)), ((), ())), preferred_element_type=f32
                )
            patch_row = (tile + dt) * per_side + p // per_side
            patch_column = block * per_side + p % per_side
            row_gap = (grid_row - patch_row * PATCH - PATCH // 2).astype(f32) + 0.5
            turned = column - patch_column * PATCH - PATCH // 2 + width // 2
            column_gap = (wrapped(turned, width) - width // 2).astype(f32) + 0.5
            near = jnp.exp(
                -(row_gap * row_gap + column_gap * column_gap) / (2.0 * LOC_LEN * LOC_LEN)
            )
            planes[index * depth : (index + 1) * depth, :] = count * (near / size)
            index += 1
    for extra in range(index, 16):
        planes[extra * depth : (extra + 1) * depth, :] = jnp.zeros((depth, LANES), f32)
    for i in range(depth):
        weights[:, i * LANES : (i + 1) * LANES] = planes[pl.ds(i, 16, stride=depth), :]


def halves(values):
    high = values.astype(bf16)
    return high, (values - high.astype(f32)).astype(bf16)


def dot_rows(left, right):
    return lax.dot_general(left, right, (((1,), (1,)), ((), ())), preferred_element_type=f32)


def systems_body(*refs, patches, sources, members, region_rows):
    mine, theirs, weights, values, own, to_first, to_second = refs[:7]
    planes, tall_high, tall_low, wide_high, wide_low = refs[7:]
    depth = 3 * BLOCK
    each = 2 * mine.shape[0] // sources
    _, _, core = place()
    ensemble = sources * members
    total = jnp.zeros((depth, LANES), f32)
    for s in range(sources):
        source, row = (mine, theirs)[s % 2], s // 2 * each
        both = source[row + region_rows : row + each, :].astype(f32)
        device = 2 * (s // 2) + (core ^ (s % 2))
        at = pl.multiple_of(device * (members * depth), BLOCK)
        planes[pl.ds(at, members * depth), :] = both
        for b in range(members):
            total += both[b * depth : (b + 1) * depth, :]
    mean = total / ensemble
    for k in range(ensemble):
        planes[k * depth : (k + 1) * depth, :] -= mean
    planes[ensemble * depth : (ensemble + 1) * depth, :] = values[...] - mean
    for k in range(ensemble + 1, ensemble + 8):
        planes[k * depth : (k + 1) * depth, :] = jnp.zeros((depth, LANES), f32)
    for i in range(depth):
        at = slice(i * LANES, (i + 1) * LANES)
        tile = planes[pl.ds(i, ensemble + 8, stride=depth), :]
        high, low = halves(tile)
        wide_high[:, at] = high
        wide_low[:, at] = low
        spread = tile[0:ensemble, :]
        for p in range(3 * patches):
            high, low = halves(spread * weights[p : p + 1, at])
            tall_high[p * ensemble : (p + 1) * ensemble, at] = high
            tall_low[p * ensemble : (p + 1) * ensemble, at] = low
    result = (
        dot_rows(wide_high[...], tall_high[...])
        + dot_rows(wide_low[...], tall_high[...])
        + dot_rows(wide_high[...], tall_low[...])
    )
    count = patches * ensemble // 64
    even = lax.rem(lax.axis_index("tile"), 2) == 0
    found = []
    for n in range(3 * count):
        piece = result[:, n // 2 * LANES : (n // 2 + 1) * LANES] if n // 2 * LANES + LANES <= result.shape[1] else None
        if piece is None:
            piece = jnp.concatenate([result[:, n * 64 :], jnp.zeros((ensemble + 8, 64), f32)], axis=1)
        else:
            if n % 2:
                piece = pltpu.roll(piece, 64, 1)
            piece = jnp.where(iota(piece.shape, 1) < 64, piece, 0.0)
        found.append(piece)
    for i in range(count):
        at = slice(i * LANES, (i + 1) * LANES)
        own[:, at] = found[i]
        for_south, for_north = found[count + i], found[2 * count + i]
        to_first[:, at] = jnp.where(even, for_north, for_south)
        to_second[:, at] = jnp.where(even, for_south, for_north)


def analysis_body(*refs, patches, sources, members, region_rows):
    mine, theirs, own, first, second = refs[:5]
    send, centred, factors = refs[5:]
    each = 2 * mine.shape[0] // sources
    _, _, core = place()
    ensemble = sources * members
    hits = region_rows // members
    total = jnp.zeros((hits, LANES), f32)
    for s in range(sources):
        source, row = (mine, theirs)[s % 2], s // 2 * each
        device = 2 * (s // 2) + (core ^ (s % 2))
        part = source[row : row + region_rows, :].astype(f32)
        for b in range(members):
            one = part[b * hits : (b + 1) * hits, :]
            centred[device * members + b] = one
            total += one
    mean = total / ensemble
    for k in range(ensemble):
        centred[k] -= mean

    count = patches * ensemble // 64
    group = 64 // ensemble
    row = iota((ensemble + 8, LANES), 0)
    lane = iota((ensemble + 8, LANES), 1)
    within = lane & (ensemble - 1)
    start = jnp.where(
        (row == within) & (row < ensemble), jnp.where(lane < 64, ensemble - 1.0, 1.0), 0.0
    )
    lane8 = iota((BLOCK, LANES), 1)
    group_start = (lane8 & 63) & ~(ensemble - 1)
    transforms = []
    for i in range(count):
        at = slice(i * LANES, (i + 1) * LANES)
        state = own[:, at] + first[:, at] + second[:, at] + start
        pivots = jnp.ones((ensemble, LANES), f32)
        for k in range(ensemble):
            column = pick_lanes(state, group_start + k)
            pivot = column[k : k + 1, :]
            scaled = state[k : k + 1, :] / pivot
            state = state - jnp.where(row > k, column, 0.0) * scaled
            pivots = jnp.where(row[0:ensemble] == k, pivot, pivots)
        inverse = state[0:ensemble, :] * lax.rsqrt(pivots)
        mean_weight = -state[ensemble : ensemble + 1, :]
        unit = jnp.where(row[0:ensemble] == within[0:ensemble], 1.0, 0.0)
        transforms.append(mean_weight + (ensemble - 1.0) ** 0.5 * inverse - unit)

    side_lanes = 32
    patch = (lane8 // (2 * side_lanes)) * 2 + (lane8 & (side_lanes - 1)) // PATCH
    inside = 64 + (patch & (group - 1)) * ensemble if group > 1 else 64 + 0 * patch
    which = patch // group
    for j in range(ensemble):
        chosen = pick_lanes(transforms[0], inside + j)
        for i in range(1, count):
            other = pick_lanes(transforms[i], inside + j)
            chosen = jnp.where(jnp.broadcast_to(which[0:1] == i, chosen.shape), other, chosen)
        factors[j] = chosen

    for s in range(send.shape[0]):
        for c in (0, 1):
            first_member = (2 * s + c) * members
            totals = [jnp.zeros((hits, LANES), f32) for _ in range(members)]
            for j in range(ensemble):
                centred_j = centred[j]
                for b in range(members):
                    totals[b] += factors[j, first_member + b : first_member + b + 1, :] * centred_j
            at = slice(c * region_rows, (c + 1) * region_rows)
            send[s, at, :] = jnp.concatenate(totals, axis=0).astype(bf16)


def output_body(forecast, mine, theirs, analysis, ordered):
    members, levels, side, width = forecast.shape
    _, _, core = place()
    rows = ordered.shape[1]
    for s in range(mine.shape[0] // rows):
        at = slice(s * rows, (s + 1) * rows)
        ordered[2 * s + core] = mine[at, :].astype(f32)
        ordered[2 * s + (core ^ 1)] = theirs[at, :].astype(f32)
    for q in range(width // LANES):
        parts = [ordered[4 * q + c] for c in range(4)]
        at = slice(q * LANES, (q + 1) * LANES)
        for r, part in enumerate(transpose_chunks(parts)):
            rows = slice(r * BLOCK, (r + 1) * BLOCK)
            analysis[:, :, rows, at] = forecast[:, :, rows, at] + part.reshape(
                members, levels, BLOCK, LANES
            )


def shards(member_concentration, courant_pairs, obs_cell, obs_value, obs_error, obs_list):
    members, levels, side, width = member_concentration.shape
    blocks = lax.axis_size("member")
    tiles = lax.axis_size("tile")
    height = side * tiles
    ensemble = members * blocks
    per_side = side // PATCH
    patches = per_side * per_side
    slots = obs_list.shape[2]
    region_rows = members * levels * BLOCK
    depth = 3 * BLOCK
    all_rows = region_rows + members * depth
    chips = blocks // 2
    chip_rows = 2 * region_rows + members * 4 * BLOCK
    edge_rows = -(-(24 + patches * slots // width) // 8) * 8
    edge_shape = (members, levels, BLOCK, width)
    rate_shape = (2, levels, BLOCK, width)

    to_first, to_second = call(
        pack_edges,
        [((edge_rows, width), f32)] * 2,
        [
            pltpu.VMEM(edge_shape, f32),
            pltpu.VMEM(edge_shape, f32),
            pltpu.VMEM(rate_shape, f32),
            pltpu.VMEM(rate_shape, f32),
            pltpu.VMEM(obs_list.shape, jnp.int32),
            pltpu.SemaphoreType.DMA((5,)),
        ],
        specs=[pl.BlockSpec(memory_space=pltpu.HBM)] * 3,
        vmem=63,
    )(member_concentration, courant_pairs, obs_list)
    first, second = swap(to_first, to_second, tiles)

    flat = lambda array: array.reshape(-1, LANES)
    cell = flat(obs_cell)
    cell_row = lax.dynamic_index_in_dim(
        cell.reshape(blocks, tiles, BLOCK, LANES), lax.axis_index("tile"), 1, False
    )
    forecast, chunks = call(
        functools.partial(forecast_body, tiles=tiles, height=height),
        [(member_concentration.shape, f32), ((chips, chip_rows, LANES), bf16)],
        [
            pltpu.VMEM((blocks, region_rows, LANES), f32),
        ],
    )(
        member_concentration,
        courant_pairs,
        first,
        second,
        cell_row,
    )
    received = exchange(chunks)
    weights, values = call(
        functools.partial(
            weights_body, tiles=tiles, blocks=blocks, height=height, width=width, side=side
        ),
        [((16, depth * LANES), f32), ((depth, LANES), f32)],
        [pltpu.VMEM((16 * depth, LANES), f32)],
        flops=100_000_000,
    )(obs_list, first, second, cell, flat(obs_value), flat(obs_error))

    sizes = dict(patches=patches, sources=blocks, members=members, region_rows=region_rows)
    share = functools.partial(share_body, region_rows=region_rows)
    mine, theirs = call(share, [((chips * all_rows, LANES), bf16)] * 2)(received, values)
    theirs = swap_cores(theirs)

    tall = 3 * patches * ensemble
    system_shape = (ensemble + 8, patches * ensemble // 64 * LANES)
    own, to_first, to_second = call(
        functools.partial(systems_body, **sizes),
        [(system_shape, f32)] * 3,
        [
            pltpu.VMEM(((ensemble + 8) * depth, LANES), f32),
            pltpu.VMEM((tall, depth * LANES), bf16),
            pltpu.VMEM((tall, depth * LANES), bf16),
            pltpu.VMEM((ensemble + 8, depth * LANES), bf16),
            pltpu.VMEM((ensemble + 8, depth * LANES), bf16),
        ],
    )(mine, theirs, weights, values)
    first, second = swap(to_first, to_second, tiles)

    (changes,) = call(
        functools.partial(analysis_body, **sizes),
        [((chips, 2 * region_rows, LANES), bf16)],
        [
            pltpu.VMEM((ensemble, levels * BLOCK, LANES), f32),
            pltpu.VMEM((ensemble, ensemble, LANES), f32),
        ],
    )(mine, theirs, own, first, second)
    returned = exchange(changes)
    mine, theirs = call(share, [((chips * region_rows, LANES), bf16)] * 2)(returned, forecast)
    theirs = swap_cores(theirs)
    (analysis,) = call(
        output_body, [(forecast.shape, f32)], [pltpu.VMEM((blocks, region_rows, LANES), f32)]
    )(forecast, mine, theirs)
    return analysis


def solution(mesh):
    return jax.shard_map(
        shards,
        mesh=mesh,
        in_specs=(
            P("member", None, "tile", None),
            P(None, None, "tile", None),
            P(),
            P(),
            P(),
            P("tile", "member", None),
        ),
        out_specs=P("member", None, "tile", None),
        check_vma=False,
    )
```

```python
import functools

import jax
import jax.numpy as jnp
from jax import lax
from jax.experimental import pallas as pl
from jax.experimental.pallas import tpu as pltpu
from jax.sharding import PartitionSpec as P

PATCH = 16
LOC_LEN = 16
DIFFUSION = 0.05
LANES = 128
BLOCK = 8

f32 = jnp.float32
bf16 = jnp.bfloat16


def call(body, outs, scratch=(), flops=1_000_000, moved=1_000_000, specs=None, vmem=48):
    specs = {} if specs is None else {"in_specs": specs}
    return pl.pallas_call(
        body,
        **specs,
        out_shape=[jax.ShapeDtypeStruct(shape, kind) for shape, kind in outs],
        scratch_shapes=list(scratch),
        compiler_params=pltpu.CompilerParams(vmem_limit_bytes=vmem * 1024 * 1024),
        cost_estimate=pl.CostEstimate(flops=flops, bytes_accessed=moved, transcendentals=0),
    )


def split(number, size):
    if size & (size - 1) == 0:
        return number >> (size.bit_length() - 1), number & (size - 1)
    quotient = number // size
    return quotient, number - quotient * size


def wrapped(number, size):
    if size & (size - 1) == 0:
        return number & (size - 1)
    return lax.rem(number + size, size)


def iota(shape, axis):
    return lax.broadcasted_iota(jnp.int32, shape, axis)


def pick_lanes(values, index):
    rows = [
        jnp.take_along_axis(values[r : r + BLOCK], index, axis=1, mode="promise_in_bounds")
        for r in range(0, values.shape[0], BLOCK)
    ]
    return rows[0] if len(rows) == 1 else jnp.concatenate(rows, axis=0)


def transpose_chunks(parts):
    lane = iota(parts[0].shape, 1)
    low = lane < 64
    even = (lane & 32) == 0
    parts = list(parts)
    for i in (0, 1):
        a, b = parts[i], parts[i + 2]
        parts[i] = jnp.where(low, a, pltpu.roll(b, 64, 1))
        parts[i + 2] = jnp.where(low, pltpu.roll(a, 64, 1), b)
    for i in (0, 2):
        a, b = parts[i], parts[i + 1]
        parts[i] = jnp.where(even, a, pltpu.roll(b, 32, 1))
        parts[i + 1] = jnp.where(even, pltpu.roll(a, 96, 1), b)
    return parts


def pack_edges(
    tracer, courant, lists, to_first, to_second, first, last, first_rates, last_rates, numbers, arrived
):
    members, levels, side, width = tracer.shape
    copies = [
        pltpu.make_async_copy(source, target, arrived.at[i])
        for i, (source, target) in enumerate(
            (
                (tracer.at[:, :, 0:BLOCK, :], first),
                (tracer.at[:, :, side - BLOCK : side, :], last),
                (courant.at[:, :, 0:BLOCK, :], first_rates),
                (courant.at[:, :, side - BLOCK : side, :], last_rates),
                (lists, numbers),
            )
        )
    ]
    for copy in copies:
        copy.start()
    for copy in copies:
        copy.wait()
    even = lax.rem(lax.axis_index("tile"), 2) == 0

    def put(row, low, high):
        to_first[row : row + 1, :] = jnp.where(even, high, low)
        to_second[row : row + 1, :] = jnp.where(even, low, high)

    end = BLOCK - 1
    for b in range(members):
        for l in range(levels):
            row = b * levels + l
            put(row, first[b, l, 0:1, :], last[b, l, end : end + 1, :])
            put(8 + row, first[b, l, 1:2, :], last[b, l, end - 1 : end, :])
    for c in range(2):
        for l in range(levels):
            put(16 + c * levels + l, first_rates[c, l, 0:1, :], last_rates[c, l, end : end + 1, :])
    row = 24
    for a in range(numbers.shape[0]):
        for b in range(numbers.shape[1]):
            for s in range(0, numbers.shape[2], width):
                part = numbers[a, b : b + 1, s : s + width].astype(f32)
                to_first[row : row + 1, :] = part
                to_second[row : row + 1, :] = part
                row += 1


def coefficients(meridional, zonal):
    return (
        (1.0 - 4.0 * DIFFUSION) - jnp.abs(zonal) - jnp.abs(meridional),
        DIFFUSION + jnp.maximum(zonal, 0.0),
        DIFFUSION - jnp.minimum(zonal, 0.0),
        DIFFUSION + jnp.maximum(meridional, 0.0),
        DIFFUSION - jnp.minimum(meridional, 0.0),
    )


def stencil(current, south, north, factors):
    width = current.shape[1]
    centre, from_west, from_east, from_south, from_north = factors
    west = pltpu.roll(current, 1, 1)
    east = pltpu.roll(current, width - 1, 1)
    return (
        centre * current
        + from_west * west
        + from_east * east
        + from_south * south
        + from_north * north
    )


def beside(first, second, tile):
    even = lax.rem(tile, 2) == 0
    return jnp.where(even, second, first), jnp.where(even, first, second)


def swap(first, second, tiles):
    pairs = lambda start: [
        pair for i in range(start, tiles - 1, 2) for pair in ((i, i + 1), (i + 1, i))
    ]
    return lax.ppermute(first, "tile", pairs(0)), lax.ppermute(second, "tile", pairs(1))


def exchange(chunks):
    chips = len(chunks)
    device = lambda chip, core: 2 * chip + core
    swaps = lambda s: [(device(i, c), device(i ^ s, c)) for i in range(chips) for c in (0, 1)]
    received = {s: lax.ppermute(chunks[s], "member", swaps(s)) for s in range(chips - 1, 0, -1)}
    return [chunks[0]] + [received[s] for s in range(1, chips)]


def swap_cores(array):
    return lax.ppermute(array, "member", [(i, i ^ 1) for i in range(lax.axis_size("member"))])


def place():
    block = lax.axis_index("member")
    core = lax.rem(block, 2)
    return block, (block - core) // 2, core


def share_body(*refs, region_rows):
    chunks, (own, other) = refs[:-3], refs[-2:]
    _, _, core = place()
    first = core == 0
    each = own.shape[0] // len(chunks)
    half = chunks[0].shape[0] - 2 * region_rows
    lines = half // 2
    for s, chunk in enumerate(chunks):
        low, high = chunk[0:region_rows, :], chunk[region_rows : 2 * region_rows, :]
        row = s * each
        own[row : row + region_rows, :] = jnp.where(first, low, high)
        other[row : row + region_rows, :] = jnp.where(first, high, low)
        if each == region_rows:
            continue
        seen = chunk[2 * region_rows :, :].astype(f32)
        west = jnp.concatenate([seen[0 : lines - 8], seen[lines : 2 * lines - 8]], axis=0)
        east = jnp.concatenate([seen[8:lines], seen[lines + 8 : 2 * lines]], axis=0)
        own[row + region_rows : row + each, :] = jnp.where(first, west, east).astype(bf16)
        other[row + region_rows : row + each, :] = jnp.where(first, east, west).astype(bf16)


def forecast_body(
    tracer, courant, first, second, cell, forecast, *rest, tiles, height
):
    *chunks, send, table = rest
    members, levels, side, width = tracer.shape
    blocks = width // side
    tile = lax.axis_index("tile")
    planes = members * levels

    south, north = beside(first[0:24, :], second[0:24, :], tile)
    own = lambda at: jnp.concatenate(
        [tracer[b, l, at : at + 1, :] for b in range(members) for l in range(levels)], axis=0
    )
    inside_south, inside_north = tile > 0, tile < tiles - 1
    low, lowest = south[0:planes], south[8 : 8 + planes]
    high, highest = north[0:planes], north[8 : 8 + planes]

    def edge(source):
        twice = lambda at: jnp.concatenate([source[at : at + levels]] * members, axis=0)
        return coefficients(twice(16), twice(16 + levels))

    below = stencil(low, lowest, own(0), edge(south))
    above = stencil(high, own(side - 1), highest, edge(north))
    below = jnp.where(inside_south, below, 0.0)
    above = jnp.where(inside_north, above, 0.0)
    row = iota((side, width), 0)
    for l in range(levels):
        factors = coefficients(courant[0, l], courant[1, l])
        for b in range(members):
            plane = b * levels + l
            current = tracer[b, l]
            for under, over in ((low, high), (below, above)):
                under, over = under[plane : plane + 1, :], over[plane : plane + 1, :]
                lower = jnp.where(row == 0, under, pltpu.roll(current, 1, 0))
                upper = jnp.where(row == side - 1, over, pltpu.roll(current, side - 1, 0))
                current = stencil(current, lower, upper, factors)
            forecast[b, l] = current

    region_rows = planes * BLOCK
    for q in range(width // LANES):
        parts = [
            forecast[:, :, r : r + BLOCK, q * LANES : (q + 1) * LANES].reshape(region_rows, LANES)
            for r in range(0, side, BLOCK)
        ]
        for i, part in enumerate(transpose_chunks(parts)):
            c = 4 * q + i
            rounded = part.astype(bf16)
            send[c // 2, c % 2 * region_rows : (c % 2 + 1) * region_rows, :] = rounded
            table[c] = rounded.astype(f32)

    hits = levels * BLOCK
    observed = []
    for c in range(blocks):
        cells = cell[c]
        above_row, column = split(cells, width)
        level, grid_row = split(above_row, height)
        _, local_row = split(grid_row, side)
        _, local_column = split(column, side)
        band, sub_row = split(local_row, BLOCK)
        high = level * BLOCK + sub_row
        low = band * side + local_column
        mine = [jnp.zeros((BLOCK, LANES), f32) for _ in range(members)]
        for h in range(hits):
            here = high == h
            for b in range(members):
                line = table[c, b * hits + h : b * hits + h + 1, :]
                line = jnp.broadcast_to(line, (BLOCK, LANES))
                mine[b] = jnp.where(here, pick_lanes(line, low), mine[b])
        observed.append(mine)
    for chip in range(blocks // 2):
        rows = [
            observed[(2 * chip + r - 1) % blocks][b] for b in range(members) for r in range(4)
        ]
        for i in range(0, len(rows), 2):
            at = 2 * region_rows + i * BLOCK
            send[chip, at : at + 2 * BLOCK, :] = jnp.concatenate(rows[i : i + 2], axis=0).astype(
                bf16
            )
    _, chip, _ = place()
    for s, chunk in enumerate(chunks):
        chunk[...] = send[chip ^ s]


def weights_body(
    lists, first, second, cell, value, variance, weights, values, planes, *, tiles, blocks, height, width, side
):
    tile = lax.axis_index("tile")
    block = lax.axis_index("member")
    own_lists = slice(24, 24 + lists.shape[0] * lists.shape[1] * lists.shape[2] // width)
    south, north = beside(first[own_lists, :], second[own_lists, :], tile)
    per_side = side // PATCH
    patches = per_side * per_side
    slots = lists.shape[2]
    depth = 3 * BLOCK
    rows, columns, sizes = [], [], []
    for r in range(3):
        column_block = wrapped(block + (r - 1), blocks)
        first = pl.multiple_of((column_block * tiles + tile) * BLOCK, BLOCK)
        cells = cell[pl.ds(first, BLOCK), :]
        above_row, column = split(cells, width)
        _, grid_row = split(above_row, height)
        rows.append(grid_row)
        columns.append(column)
        sizes.append(variance[pl.ds(first, BLOCK), :])
        values[r * BLOCK : (r + 1) * BLOCK, :] = value[pl.ds(first, BLOCK), :]
    grid_row = jnp.concatenate(rows, axis=0)
    column = jnp.concatenate(columns, axis=0)
    size = jnp.concatenate(sizes, axis=0)

    def pieces(dt, p):
        if dt == 0:
            return [lists[p // per_side, p % per_side : p % per_side + 1, :]]
        source = south if dt < 0 else north
        each = slots // width
        return [
            source[p * each + i : p * each + i + 1].astype(jnp.int32) for i in range(each)
        ]

    index = 0
    for dt in (0, -1, 1):
        for p in range(patches):
            count = jnp.zeros((depth, LANES), f32)
            for part in pieces(dt, p):
                length = part.shape[1]
                region, within = split(part, BLOCK * LANES)
                region_column, region_row = split(region, tiles)
                line, lane = split(within, LANES)
                near = wrapped(region_column - block + 1, blocks)
                fits = (part >= 0) & (region_row == tile) & (near < 3)
                line = jnp.where(fits, near * BLOCK + line, -1)
                one = (iota((depth, length), 0) == line).astype(f32).astype(bf16)
                other = (iota((LANES, length), 0) == lane).astype(f32).astype(bf16)
                count += lax.dot_general(
                    one, other, (((1,), (1,)), ((), ())), preferred_element_type=f32
                )
            patch_row = (tile + dt) * per_side + p // per_side
            patch_column = block * per_side + p % per_side
            row_gap = (grid_row - patch_row * PATCH - PATCH // 2).astype(f32) + 0.5
            turned = column - patch_column * PATCH - PATCH // 2 + width // 2
            column_gap = (wrapped(turned, width) - width // 2).astype(f32) + 0.5
            near = jnp.exp(
                -(row_gap * row_gap + column_gap * column_gap) / (2.0 * LOC_LEN * LOC_LEN)
            )
            planes[index * depth : (index + 1) * depth, :] = count * (near / size)
            index += 1
    for extra in range(index, 16):
        planes[extra * depth : (extra + 1) * depth, :] = jnp.zeros((depth, LANES), f32)
    for i in range(depth):
        weights[:, i * LANES : (i + 1) * LANES] = planes[pl.ds(i, 16, stride=depth), :]


def halves(values):
    high = values.astype(bf16)
    return high, (values - high.astype(f32)).astype(bf16)


def dot_rows(left, right):
    return lax.dot_general(left, right, (((1,), (1,)), ((), ())), preferred_element_type=f32)


def systems_body(*refs, patches, sources, members, region_rows):
    mine, theirs, weights, values, own, to_first, to_second = refs[:7]
    planes, tall_high, tall_low, wide_high, wide_low = refs[7:]
    depth = 3 * BLOCK
    each = 2 * mine.shape[0] // sources
    _, chip, core = place()
    ensemble = sources * members
    total = jnp.zeros((depth, LANES), f32)
    for s in range(sources):
        source, row = (mine, theirs)[s % 2], s // 2 * each
        both = source[row + region_rows : row + each, :].astype(f32)
        device = 2 * (chip ^ (s // 2)) + (core ^ (s % 2))
        at = pl.multiple_of(device * (members * depth), BLOCK)
        planes[pl.ds(at, members * depth), :] = both
        for b in range(members):
            total += both[b * depth : (b + 1) * depth, :]
    mean = total / ensemble
    for k in range(ensemble):
        planes[k * depth : (k + 1) * depth, :] -= mean
    planes[ensemble * depth : (ensemble + 1) * depth, :] = values[...] - mean
    for k in range(ensemble + 1, ensemble + 8):
        planes[k * depth : (k + 1) * depth, :] = jnp.zeros((depth, LANES), f32)
    for i in range(depth):
        at = slice(i * LANES, (i + 1) * LANES)
        tile = planes[pl.ds(i, ensemble + 8, stride=depth), :]
        high, low = halves(tile)
        wide_high[:, at] = high
        wide_low[:, at] = low
        spread = tile[0:ensemble, :]
        for p in range(3 * patches):
            high, low = halves(spread * weights[p : p + 1, at])
            tall_high[p * ensemble : (p + 1) * ensemble, at] = high
            tall_low[p * ensemble : (p + 1) * ensemble, at] = low
    result = (
        dot_rows(wide_high[...], tall_high[...])
        + dot_rows(wide_low[...], tall_high[...])
        + dot_rows(wide_high[...], tall_low[...])
    )
    count = patches * ensemble // 64
    even = lax.rem(lax.axis_index("tile"), 2) == 0
    found = []
    for n in range(3 * count):
        piece = result[:, n // 2 * LANES : (n // 2 + 1) * LANES] if n // 2 * LANES + LANES <= result.shape[1] else None
        if piece is None:
            piece = jnp.concatenate([result[:, n * 64 :], jnp.zeros((ensemble + 8, 64), f32)], axis=1)
        else:
            if n % 2:
                piece = pltpu.roll(piece, 64, 1)
            piece = jnp.where(iota(piece.shape, 1) < 64, piece, 0.0)
        found.append(piece)
    for i in range(count):
        at = slice(i * LANES, (i + 1) * LANES)
        own[:, at] = found[i]
        for_south, for_north = found[count + i], found[2 * count + i]
        to_first[:, at] = jnp.where(even, for_north, for_south)
        to_second[:, at] = jnp.where(even, for_south, for_north)


def analysis_body(*refs, patches, sources, members, region_rows):
    mine, theirs, own, first, second = refs[:5]
    chunks, (centred, factors) = refs[5:-2], refs[-2:]
    each = 2 * mine.shape[0] // sources
    _, chip, core = place()
    ensemble = sources * members
    hits = region_rows // members
    total = jnp.zeros((hits, LANES), f32)
    for s in range(sources):
        source, row = (mine, theirs)[s % 2], s // 2 * each
        device = 2 * (chip ^ (s // 2)) + (core ^ (s % 2))
        part = source[row : row + region_rows, :].astype(f32)
        for b in range(members):
            one = part[b * hits : (b + 1) * hits, :]
            centred[device * members + b] = one
            total += one
    mean = total / ensemble
    for k in range(ensemble):
        centred[k] -= mean

    count = patches * ensemble // 64
    group = 64 // ensemble
    row = iota((ensemble + 8, LANES), 0)
    lane = iota((ensemble + 8, LANES), 1)
    within = lane & (ensemble - 1)
    start = jnp.where(
        (row == within) & (row < ensemble), jnp.where(lane < 64, ensemble - 1.0, 1.0), 0.0
    )
    lane8 = iota((BLOCK, LANES), 1)
    group_start = (lane8 & 63) & ~(ensemble - 1)
    transforms = []
    for i in range(count):
        at = slice(i * LANES, (i + 1) * LANES)
        state = own[:, at] + first[:, at] + second[:, at] + start
        columns = [pick_lanes(state, group_start + k) for k in range(ensemble)]
        pivots = jnp.ones((ensemble, LANES), f32)
        for k in range(ensemble):
            pivot = columns[k][k : k + 1, :]
            factor = jnp.where(row > k, columns[k], 0.0) / pivot
            for j in range(k + 1, ensemble):
                columns[j] = columns[j] - factor * columns[j][k : k + 1, :]
            state = state - factor * state[k : k + 1, :]
            pivots = jnp.where(row[0:ensemble] == k, pivot, pivots)
        inverse = state[0:ensemble, :] * lax.rsqrt(pivots)
        mean_weight = -state[ensemble : ensemble + 1, :]
        unit = jnp.where(row[0:ensemble] == within[0:ensemble], 1.0, 0.0)
        transforms.append(mean_weight + (ensemble - 1.0) ** 0.5 * inverse - unit)

    side_lanes = 32
    patch = (lane8 // (2 * side_lanes)) * 2 + (lane8 & (side_lanes - 1)) // PATCH
    inside = 64 + (patch & (group - 1)) * ensemble if group > 1 else 64 + 0 * patch
    which = patch // group
    for j in range(ensemble):
        chosen = pick_lanes(transforms[0], inside + j)
        for i in range(1, count):
            other = pick_lanes(transforms[i], inside + j)
            chosen = jnp.where(jnp.broadcast_to(which[0:1] == i, chosen.shape), other, chosen)
        factors[j] = chosen

    for s, chunk in enumerate(chunks):
        for c in (0, 1):
            first_member = (2 * (chip ^ s) + c) * members
            totals = [jnp.zeros((hits, LANES), f32) for _ in range(members)]
            for j in range(ensemble):
                centred_j = centred[j]
                for b in range(members):
                    totals[b] += factors[j, pl.ds(first_member + b, 1), :] * centred_j
            at = slice(c * region_rows, (c + 1) * region_rows)
            chunk[at, :] = jnp.concatenate(totals, axis=0).astype(bf16)


def output_body(forecast, mine, theirs, analysis, ordered):
    members, levels, side, width = forecast.shape
    _, chip, core = place()
    rows = ordered.shape[1]
    for s in range(mine.shape[0] // rows):
        at = slice(s * rows, (s + 1) * rows)
        ordered[2 * (chip ^ s) + core] = mine[at, :].astype(f32)
        ordered[2 * (chip ^ s) + (core ^ 1)] = theirs[at, :].astype(f32)
    for q in range(width // LANES):
        parts = [ordered[4 * q + c] for c in range(4)]
        at = slice(q * LANES, (q + 1) * LANES)
        for r, part in enumerate(transpose_chunks(parts)):
            rows = slice(r * BLOCK, (r + 1) * BLOCK)
            analysis[:, :, rows, at] = forecast[:, :, rows, at] + part.reshape(
                members, levels, BLOCK, LANES
            )


def shards(member_concentration, courant_pairs, obs_cell, obs_value, obs_error, obs_list):
    members, levels, side, width = member_concentration.shape
    blocks = lax.axis_size("member")
    tiles = lax.axis_size("tile")
    height = side * tiles
    ensemble = members * blocks
    per_side = side // PATCH
    patches = per_side * per_side
    slots = obs_list.shape[2]
    region_rows = members * levels * BLOCK
    depth = 3 * BLOCK
    all_rows = region_rows + members * depth
    chips = blocks // 2
    chip_rows = 2 * region_rows + members * 4 * BLOCK
    edge_rows = -(-(24 + patches * slots // width) // 8) * 8
    edge_shape = (members, levels, BLOCK, width)
    rate_shape = (2, levels, BLOCK, width)

    to_first, to_second = call(
        pack_edges,
        [((edge_rows, width), f32)] * 2,
        [
            pltpu.VMEM(edge_shape, f32),
            pltpu.VMEM(edge_shape, f32),
            pltpu.VMEM(rate_shape, f32),
            pltpu.VMEM(rate_shape, f32),
            pltpu.VMEM(obs_list.shape, jnp.int32),
            pltpu.SemaphoreType.DMA((5,)),
        ],
        specs=[pl.BlockSpec(memory_space=pltpu.HBM)] * 3,
        vmem=63,
    )(member_concentration, courant_pairs, obs_list)
    first, second = swap(to_first, to_second, tiles)

    flat = lambda array: array.reshape(-1, LANES)
    cell = flat(obs_cell)
    cell_row = lax.dynamic_index_in_dim(
        cell.reshape(blocks, tiles, BLOCK, LANES), lax.axis_index("tile"), 1, False
    )
    forecast, *chunks = call(
        functools.partial(forecast_body, tiles=tiles, height=height),
        [(member_concentration.shape, f32)] + [((chip_rows, LANES), bf16)] * chips,
        [
            pltpu.VMEM((chips, chip_rows, LANES), bf16),
            pltpu.VMEM((blocks, region_rows, LANES), f32),
        ],
    )(
        member_concentration,
        courant_pairs,
        first,
        second,
        cell_row,
    )
    received = exchange(chunks)
    weights, values = call(
        functools.partial(
            weights_body, tiles=tiles, blocks=blocks, height=height, width=width, side=side
        ),
        [((16, depth * LANES), f32), ((depth, LANES), f32)],
        [pltpu.VMEM((16 * depth, LANES), f32)],
        flops=100_000_000,
    )(obs_list, first, second, cell, flat(obs_value), flat(obs_error))

    sizes = dict(patches=patches, sources=blocks, members=members, region_rows=region_rows)
    share = functools.partial(share_body, region_rows=region_rows)
    mine, theirs = call(share, [((chips * all_rows, LANES), bf16)] * 2)(*received, values)
    theirs = swap_cores(theirs)

    tall = 3 * patches * ensemble
    system_shape = (ensemble + 8, patches * ensemble // 64 * LANES)
    own, to_first, to_second = call(
        functools.partial(systems_body, **sizes),
        [(system_shape, f32)] * 3,
        [
            pltpu.VMEM(((ensemble + 8) * depth, LANES), f32),
            pltpu.VMEM((tall, depth * LANES), bf16),
            pltpu.VMEM((tall, depth * LANES), bf16),
            pltpu.VMEM((ensemble + 8, depth * LANES), bf16),
            pltpu.VMEM((ensemble + 8, depth * LANES), bf16),
        ],
    )(mine, theirs, weights, values)
    first, second = swap(to_first, to_second, tiles)

    changes = call(
        functools.partial(analysis_body, **sizes),
        [((2 * region_rows, LANES), bf16)] * chips,
        [
            pltpu.VMEM((ensemble, levels * BLOCK, LANES), f32),
            pltpu.VMEM((ensemble, ensemble, LANES), f32),
        ],
    )(mine, theirs, own, first, second)
    returned = exchange(changes)
    mine, theirs = call(share, [((chips * region_rows, LANES), bf16)] * 2)(*returned, forecast)
    theirs = swap_cores(theirs)
    (analysis,) = call(
        output_body, [(forecast.shape, f32)], [pltpu.VMEM((blocks, region_rows, LANES), f32)]
    )(forecast, mine, theirs)
    return analysis


def solution(mesh):
    return jax.shard_map(
        shards,
        mesh=mesh,
        in_specs=(
            P("member", None, "tile", None),
            P(None, None, "tile", None),
            P(),
            P(),
            P(),
            P("tile", "member", None),
        ),
        out_specs=P("member", None, "tile", None),
        check_vma=False,
    )
```

```python
import functools

import jax
import jax.numpy as jnp
from jax import lax
from jax.experimental import pallas as pl
from jax.experimental.pallas import tpu as pltpu
from jax.sharding import PartitionSpec as P

PATCH = 16
LOC_LEN = 16
DIFFUSION = 0.05
LANES = 128
BLOCK = 8

f32 = jnp.float32
bf16 = jnp.bfloat16


def call(body, outs, scratch=(), flops=1_000_000, moved=1_000_000, specs=None, vmem=48):
    specs = {} if specs is None else {"in_specs": specs}
    return pl.pallas_call(
        body,
        **specs,
        out_shape=[jax.ShapeDtypeStruct(shape, kind) for shape, kind in outs],
        scratch_shapes=list(scratch),
        compiler_params=pltpu.CompilerParams(vmem_limit_bytes=vmem * 1024 * 1024),
        cost_estimate=pl.CostEstimate(flops=flops, bytes_accessed=moved, transcendentals=0),
    )


def split(number, size):
    if size & (size - 1) == 0:
        return number >> (size.bit_length() - 1), number & (size - 1)
    quotient = number // size
    return quotient, number - quotient * size


def wrapped(number, size):
    if size & (size - 1) == 0:
        return number & (size - 1)
    return lax.rem(number + size, size)


def iota(shape, axis):
    return lax.broadcasted_iota(jnp.int32, shape, axis)


def pick_lanes(values, index):
    rows = [
        jnp.take_along_axis(values[r : r + BLOCK], index, axis=1, mode="promise_in_bounds")
        for r in range(0, values.shape[0], BLOCK)
    ]
    return rows[0] if len(rows) == 1 else jnp.concatenate(rows, axis=0)


def transpose_chunks(parts):
    lane = iota(parts[0].shape, 1)
    low = lane < 64
    even = (lane & 32) == 0
    parts = list(parts)
    for i in (0, 1):
        a, b = parts[i], parts[i + 2]
        parts[i] = jnp.where(low, a, pltpu.roll(b, 64, 1))
        parts[i + 2] = jnp.where(low, pltpu.roll(a, 64, 1), b)
    for i in (0, 2):
        a, b = parts[i], parts[i + 1]
        parts[i] = jnp.where(even, a, pltpu.roll(b, 32, 1))
        parts[i + 1] = jnp.where(even, pltpu.roll(a, 96, 1), b)
    return parts


def pack_edges(
    tracer, courant, lists, to_first, to_second, first, last, first_rates, last_rates, numbers, arrived
):
    members, levels, side, width = tracer.shape
    copies = [
        pltpu.make_async_copy(source, target, arrived.at[i])
        for i, (source, target) in enumerate(
            (
                (tracer.at[:, :, 0:BLOCK, :], first),
                (tracer.at[:, :, side - BLOCK : side, :], last),
                (courant.at[:, :, 0:BLOCK, :], first_rates),
                (courant.at[:, :, side - BLOCK : side, :], last_rates),
                (lists, numbers),
            )
        )
    ]
    for copy in copies:
        copy.start()
    for copy in copies:
        copy.wait()
    even = lax.rem(lax.axis_index("tile"), 2) == 0

    def put(row, low, high):
        to_first[row : row + 1, :] = jnp.where(even, high, low)
        to_second[row : row + 1, :] = jnp.where(even, low, high)

    end = BLOCK - 1
    for b in range(members):
        for l in range(levels):
            row = b * levels + l
            put(row, first[b, l, 0:1, :], last[b, l, end : end + 1, :])
            put(8 + row, first[b, l, 1:2, :], last[b, l, end - 1 : end, :])
    for c in range(2):
        for l in range(levels):
            put(16 + c * levels + l, first_rates[c, l, 0:1, :], last_rates[c, l, end : end + 1, :])
    row = 24
    for a in range(numbers.shape[0]):
        for b in range(numbers.shape[1]):
            for s in range(0, numbers.shape[2], width):
                part = numbers[a, b : b + 1, s : s + width].astype(f32)
                to_first[row : row + 1, :] = part
                to_second[row : row + 1, :] = part
                row += 1


def coefficients(meridional, zonal):
    return (
        (1.0 - 4.0 * DIFFUSION) - jnp.abs(zonal) - jnp.abs(meridional),
        DIFFUSION + jnp.maximum(zonal, 0.0),
        DIFFUSION - jnp.minimum(zonal, 0.0),
        DIFFUSION + jnp.maximum(meridional, 0.0),
        DIFFUSION - jnp.minimum(meridional, 0.0),
    )


def stencil(current, south, north, factors):
    width = current.shape[1]
    centre, from_west, from_east, from_south, from_north = factors
    west = pltpu.roll(current, 1, 1)
    east = pltpu.roll(current, width - 1, 1)
    return (
        centre * current
        + from_west * west
        + from_east * east
        + from_south * south
        + from_north * north
    )


def beside(first, second, tile):
    even = lax.rem(tile, 2) == 0
    return jnp.where(even, second, first), jnp.where(even, first, second)


def swap(first, second, tiles):
    pairs = lambda start: [
        pair for i in range(start, tiles - 1, 2) for pair in ((i, i + 1), (i + 1, i))
    ]
    return lax.ppermute(first, "tile", pairs(0)), lax.ppermute(second, "tile", pairs(1))


def turn(s, chips):
    return (chips - s) % chips


def exchange(chunks):
    chips = len(chunks)
    device = lambda chip, core: 2 * chip + core
    swaps = lambda s: [
        (device(i, c), device(i ^ turn(s, chips), c)) for i in range(chips) for c in (0, 1)
    ]
    return [chunks[0]] + [lax.ppermute(chunks[s], "member", swaps(s)) for s in range(1, chips)]


def swap_cores(array):
    return lax.ppermute(array, "member", [(i, i ^ 1) for i in range(lax.axis_size("member"))])


def place():
    block = lax.axis_index("member")
    core = lax.rem(block, 2)
    return block, (block - core) // 2, core


def share_body(*refs, region_rows):
    chunks, (own, other) = refs[:-3], refs[-2:]
    _, _, core = place()
    first = core == 0
    each = own.shape[0] // len(chunks)
    half = chunks[0].shape[0] - 2 * region_rows
    lines = half // 2
    for s, chunk in enumerate(chunks):
        low, high = chunk[0:region_rows, :], chunk[region_rows : 2 * region_rows, :]
        row = s * each
        own[row : row + region_rows, :] = jnp.where(first, low, high)
        other[row : row + region_rows, :] = jnp.where(first, high, low)
        if each == region_rows:
            continue
        seen = chunk[2 * region_rows :, :].astype(f32)
        west = jnp.concatenate([seen[0 : lines - 8], seen[lines : 2 * lines - 8]], axis=0)
        east = jnp.concatenate([seen[8:lines], seen[lines + 8 : 2 * lines]], axis=0)
        own[row + region_rows : row + each, :] = jnp.where(first, west, east).astype(bf16)
        other[row + region_rows : row + each, :] = jnp.where(first, east, west).astype(bf16)


def forecast_body(
    tracer, courant, first, second, cell, forecast, *rest, tiles, height
):
    *chunks, send, table = rest
    members, levels, side, width = tracer.shape
    blocks = width // side
    tile = lax.axis_index("tile")
    planes = members * levels

    south, north = beside(first[0:24, :], second[0:24, :], tile)
    own = lambda at: jnp.concatenate(
        [tracer[b, l, at : at + 1, :] for b in range(members) for l in range(levels)], axis=0
    )
    inside_south, inside_north = tile > 0, tile < tiles - 1
    low, lowest = south[0:planes], south[8 : 8 + planes]
    high, highest = north[0:planes], north[8 : 8 + planes]

    def edge(source):
        twice = lambda at: jnp.concatenate([source[at : at + levels]] * members, axis=0)
        return coefficients(twice(16), twice(16 + levels))

    below = stencil(low, lowest, own(0), edge(south))
    above = stencil(high, own(side - 1), highest, edge(north))
    below = jnp.where(inside_south, below, 0.0)
    above = jnp.where(inside_north, above, 0.0)
    row = iota((side, width), 0)
    for l in range(levels):
        factors = coefficients(courant[0, l], courant[1, l])
        for b in range(members):
            plane = b * levels + l
            current = tracer[b, l]
            for under, over in ((low, high), (below, above)):
                under, over = under[plane : plane + 1, :], over[plane : plane + 1, :]
                lower = jnp.where(row == 0, under, pltpu.roll(current, 1, 0))
                upper = jnp.where(row == side - 1, over, pltpu.roll(current, side - 1, 0))
                current = stencil(current, lower, upper, factors)
            forecast[b, l] = current

    region_rows = planes * BLOCK
    for q in range(width // LANES):
        parts = [
            forecast[:, :, r : r + BLOCK, q * LANES : (q + 1) * LANES].reshape(region_rows, LANES)
            for r in range(0, side, BLOCK)
        ]
        for i, part in enumerate(transpose_chunks(parts)):
            c = 4 * q + i
            rounded = part.astype(bf16)
            send[c // 2, c % 2 * region_rows : (c % 2 + 1) * region_rows, :] = rounded
            table[c] = rounded.astype(f32)

    hits = levels * BLOCK
    observed = []
    for c in range(blocks):
        cells = cell[c]
        above_row, column = split(cells, width)
        level, grid_row = split(above_row, height)
        _, local_row = split(grid_row, side)
        _, local_column = split(column, side)
        band, sub_row = split(local_row, BLOCK)
        high = level * BLOCK + sub_row
        low = band * side + local_column
        mine = [jnp.zeros((BLOCK, LANES), f32) for _ in range(members)]
        for h in range(hits):
            here = high == h
            for b in range(members):
                line = table[c, b * hits + h : b * hits + h + 1, :]
                line = jnp.broadcast_to(line, (BLOCK, LANES))
                mine[b] = jnp.where(here, pick_lanes(line, low), mine[b])
        observed.append(mine)
    for chip in range(blocks // 2):
        rows = [
            observed[(2 * chip + r - 1) % blocks][b] for b in range(members) for r in range(4)
        ]
        for i in range(0, len(rows), 2):
            at = 2 * region_rows + i * BLOCK
            send[chip, at : at + 2 * BLOCK, :] = jnp.concatenate(rows[i : i + 2], axis=0).astype(
                bf16
            )
    _, chip, _ = place()
    for s, chunk in enumerate(chunks):
        chunk[...] = send[chip ^ turn(s, len(chunks))]


def weights_body(
    lists, first, second, cell, value, variance, weights, values, planes, *, tiles, blocks, height, width, side
):
    tile = lax.axis_index("tile")
    block = lax.axis_index("member")
    own_lists = slice(24, 24 + lists.shape[0] * lists.shape[1] * lists.shape[2] // width)
    south, north = beside(first[own_lists, :], second[own_lists, :], tile)
    per_side = side // PATCH
    patches = per_side * per_side
    slots = lists.shape[2]
    depth = 3 * BLOCK
    rows, columns, sizes = [], [], []
    for r in range(3):
        column_block = wrapped(block + (r - 1), blocks)
        first = pl.multiple_of((column_block * tiles + tile) * BLOCK, BLOCK)
        cells = cell[pl.ds(first, BLOCK), :]
        above_row, column = split(cells, width)
        _, grid_row = split(above_row, height)
        rows.append(grid_row)
        columns.append(column)
        sizes.append(variance[pl.ds(first, BLOCK), :])
        values[r * BLOCK : (r + 1) * BLOCK, :] = value[pl.ds(first, BLOCK), :]
    grid_row = jnp.concatenate(rows, axis=0)
    column = jnp.concatenate(columns, axis=0)
    size = jnp.concatenate(sizes, axis=0)

    def pieces(dt, p):
        if dt == 0:
            return [lists[p // per_side, p % per_side : p % per_side + 1, :]]
        source = south if dt < 0 else north
        each = slots // width
        return [
            source[p * each + i : p * each + i + 1].astype(jnp.int32) for i in range(each)
        ]

    index = 0
    for dt in (0, -1, 1):
        for p in range(patches):
            count = jnp.zeros((depth, LANES), f32)
            for part in pieces(dt, p):
                length = part.shape[1]
                region, within = split(part, BLOCK * LANES)
                region_column, region_row = split(region, tiles)
                line, lane = split(within, LANES)
                near = wrapped(region_column - block + 1, blocks)
                fits = (part >= 0) & (region_row == tile) & (near < 3)
                line = jnp.where(fits, near * BLOCK + line, -1)
                one = (iota((depth, length), 0) == line).astype(f32).astype(bf16)
                other = (iota((LANES, length), 0) == lane).astype(f32).astype(bf16)
                count += lax.dot_general(
                    one, other, (((1,), (1,)), ((), ())), preferred_element_type=f32
                )
            patch_row = (tile + dt) * per_side + p // per_side
            patch_column = block * per_side + p % per_side
            row_gap = (grid_row - patch_row * PATCH - PATCH // 2).astype(f32) + 0.5
            turned = column - patch_column * PATCH - PATCH // 2 + width // 2
            column_gap = (wrapped(turned, width) - width // 2).astype(f32) + 0.5
            near = jnp.exp(
                -(row_gap * row_gap + column_gap * column_gap) / (2.0 * LOC_LEN * LOC_LEN)
            )
            planes[index * depth : (index + 1) * depth, :] = count * (near / size)
            index += 1
    for extra in range(index, 16):
        planes[extra * depth : (extra + 1) * depth, :] = jnp.zeros((depth, LANES), f32)
    for i in range(depth):
        weights[:, i * LANES : (i + 1) * LANES] = planes[pl.ds(i, 16, stride=depth), :]


def halves(values):
    high = values.astype(bf16)
    return high, (values - high.astype(f32)).astype(bf16)


def dot_rows(left, right):
    return lax.dot_general(left, right, (((1,), (1,)), ((), ())), preferred_element_type=f32)


def scale(spread, weights, tall_high, tall_low, at, first):
    ensemble = spread.shape[0]
    for p in range(tall_high.shape[0] // ensemble):
        high, low = halves(spread * weights[first + p : first + p + 1, at])
        tall_high[p * ensemble : (p + 1) * ensemble, at] = high
        tall_low[p * ensemble : (p + 1) * ensemble, at] = low


def products(wide, tall_high, tall_low):
    rows = wide.shape[0] // 2
    both = dot_rows(wide[...], tall_high[...])
    result = both[0:rows] + both[rows:] + dot_rows(wide[0:rows, :], tall_low[...])
    count = result.shape[1] // 64
    if count % 2:
        result = jnp.concatenate([result, jnp.zeros((rows, 64), f32)], axis=1)
    found = []
    for n in range(count):
        piece = result[:, n // 2 * LANES : (n // 2 + 1) * LANES]
        if n % 2:
            piece = pltpu.roll(piece, 64, 1)
        found.append(jnp.where(iota(piece.shape, 1) < 64, piece, 0.0))
    return found


def neighbours_body(
    mine, theirs, weights, values, to_first, to_second, wide, planes, tall_high, tall_low, *, sources, members, region_rows
):
    depth = 3 * BLOCK
    each = 2 * mine.shape[0] // sources
    _, chip, core = place()
    ensemble = sources * members
    total = jnp.zeros((depth, LANES), f32)
    for s in range(sources):
        source, row = (mine, theirs)[s % 2], s // 2 * each
        both = source[row + region_rows : row + each, :].astype(f32)
        device = 2 * (chip ^ turn(s // 2, sources // 2)) + (core ^ (s % 2))
        at = pl.multiple_of(device * (members * depth), BLOCK)
        planes[pl.ds(at, members * depth), :] = both
        for b in range(members):
            total += both[b * depth : (b + 1) * depth, :]
    mean = total / ensemble
    for k in range(ensemble):
        planes[k * depth : (k + 1) * depth, :] -= mean
    planes[ensemble * depth : (ensemble + 1) * depth, :] = values[...] - mean
    for k in range(ensemble + 1, ensemble + 8):
        planes[k * depth : (k + 1) * depth, :] = jnp.zeros((depth, LANES), f32)
    rows = ensemble + 8
    patches = tall_high.shape[0] // (2 * ensemble)
    for i in range(depth):
        at = slice(i * LANES, (i + 1) * LANES)
        tile = planes[pl.ds(i, rows, stride=depth), :]
        high, low = halves(tile)
        wide[0:rows, at] = high
        wide[rows : 2 * rows, at] = low
        scale(tile[0:ensemble, :], weights, tall_high, tall_low, at, patches)
    found = products(wide, tall_high, tall_low)
    odd = lax.rem(lax.axis_index("tile"), 2) == 1
    count = len(found) // 2
    for i in range(count):
        at = slice(i * LANES, (i + 1) * LANES)
        for_south, for_north = found[i], found[count + i]
        to_first[:, at] = jnp.where(odd, for_south, for_north)
        to_second[:, at] = jnp.where(odd, for_north, for_south)


def own_body(
    mine, theirs, weights, wide, own, centred, tall_high, tall_low, *, sources, members, region_rows
):
    _, chip, core = place()
    each = 2 * mine.shape[0] // sources
    ensemble = sources * members
    hits = region_rows // members
    total = jnp.zeros((hits, LANES), f32)
    for s in range(sources):
        source, row = (mine, theirs)[s % 2], s // 2 * each
        device = 2 * (chip ^ turn(s // 2, sources // 2)) + (core ^ (s % 2))
        part = source[row : row + region_rows, :].astype(f32)
        for b in range(members):
            one = part[b * hits : (b + 1) * hits, :]
            centred[device * members + b] = one
            total += one
    mean = total / ensemble
    for k in range(ensemble):
        centred[k] -= mean
    rows = ensemble + 8
    for i in range(0, wide.shape[1], LANES):
        at = slice(i, i + LANES)
        spread = wide[0:ensemble, at].astype(f32) + wide[rows : rows + ensemble, at].astype(f32)
        scale(spread, weights, tall_high, tall_low, at, 0)
    for i, piece in enumerate(products(wide, tall_high, tall_low)):
        own[:, i * LANES : (i + 1) * LANES] = piece


def analysis_body(own, first, second, centred, *refs, patches, sources, members, region_rows):
    chunks, factors = refs[:-1], refs[-1]
    _, chip, _ = place()
    ensemble = sources * members
    hits = region_rows // members
    count = patches * ensemble // 64
    group = 64 // ensemble
    row = iota((ensemble + 8, LANES), 0)
    lane = iota((ensemble + 8, LANES), 1)
    within = lane & (ensemble - 1)
    start = jnp.where(
        (row == within) & (row < ensemble), jnp.where(lane < 64, ensemble - 1.0, 1.0), 0.0
    )
    lane8 = iota((BLOCK, LANES), 1)
    group_start = (lane8 & 63) & ~(ensemble - 1)
    transforms = []
    for i in range(count):
        at = slice(i * LANES, (i + 1) * LANES)
        state = own[:, at] + first[:, at] + second[:, at] + start
        columns = [pick_lanes(state, group_start + k) for k in range(ensemble)]
        pivots = jnp.ones((ensemble, LANES), f32)
        for k in range(ensemble):
            pivot = columns[k][k : k + 1, :]
            factor = jnp.where(row > k, columns[k], 0.0) / pivot
            for j in range(k + 1, ensemble):
                columns[j] = columns[j] - factor * columns[j][k : k + 1, :]
            state = state - factor * state[k : k + 1, :]
            pivots = jnp.where(row[0:ensemble] == k, pivot, pivots)
        inverse = state[0:ensemble, :] * lax.rsqrt(pivots)
        mean_weight = -state[ensemble : ensemble + 1, :]
        unit = jnp.where(row[0:ensemble] == within[0:ensemble], 1.0, 0.0)
        transforms.append(mean_weight + (ensemble - 1.0) ** 0.5 * inverse - unit)

    side_lanes = 32
    patch = (lane8 // (2 * side_lanes)) * 2 + (lane8 & (side_lanes - 1)) // PATCH
    inside = 64 + (patch & (group - 1)) * ensemble if group > 1 else 64 + 0 * patch
    which = patch // group
    for j in range(ensemble):
        chosen = pick_lanes(transforms[0], inside + j)
        for i in range(1, count):
            other = pick_lanes(transforms[i], inside + j)
            chosen = jnp.where(jnp.broadcast_to(which[0:1] == i, chosen.shape), other, chosen)
        factors[j] = chosen

    for s, chunk in enumerate(chunks):
        for c in (0, 1):
            first_member = (2 * (chip ^ turn(s, len(chunks))) + c) * members
            totals = [jnp.zeros((hits, LANES), f32) for _ in range(members)]
            for j in range(ensemble):
                centred_j = centred[j]
                for b in range(members):
                    totals[b] += factors[j, pl.ds(first_member + b, 1), :] * centred_j
            at = slice(c * region_rows, (c + 1) * region_rows)
            chunk[at, :] = jnp.concatenate(totals, axis=0).astype(bf16)


def output_body(forecast, mine, theirs, analysis, ordered):
    members, levels, side, width = forecast.shape
    _, chip, core = place()
    rows = ordered.shape[1]
    chips = mine.shape[0] // rows
    for s in range(chips):
        at = slice(s * rows, (s + 1) * rows)
        source = 2 * (chip ^ turn(s, chips))
        ordered[source + core] = mine[at, :].astype(f32)
        ordered[source + (core ^ 1)] = theirs[at, :].astype(f32)
    for q in range(width // LANES):
        parts = [ordered[4 * q + c] for c in range(4)]
        at = slice(q * LANES, (q + 1) * LANES)
        for r, part in enumerate(transpose_chunks(parts)):
            rows = slice(r * BLOCK, (r + 1) * BLOCK)
            analysis[:, :, rows, at] = forecast[:, :, rows, at] + part.reshape(
                members, levels, BLOCK, LANES
            )


def shards(member_concentration, courant_pairs, obs_cell, obs_value, obs_error, obs_list):
    members, levels, side, width = member_concentration.shape
    blocks = lax.axis_size("member")
    tiles = lax.axis_size("tile")
    height = side * tiles
    ensemble = members * blocks
    per_side = side // PATCH
    patches = per_side * per_side
    slots = obs_list.shape[2]
    region_rows = members * levels * BLOCK
    depth = 3 * BLOCK
    all_rows = region_rows + members * depth
    chips = blocks // 2
    chip_rows = 2 * region_rows + members * 4 * BLOCK
    edge_rows = -(-(24 + patches * slots // width) // 8) * 8
    edge_shape = (members, levels, BLOCK, width)
    rate_shape = (2, levels, BLOCK, width)

    to_first, to_second = call(
        pack_edges,
        [((edge_rows, width), f32)] * 2,
        [
            pltpu.VMEM(edge_shape, f32),
            pltpu.VMEM(edge_shape, f32),
            pltpu.VMEM(rate_shape, f32),
            pltpu.VMEM(rate_shape, f32),
            pltpu.VMEM(obs_list.shape, jnp.int32),
            pltpu.SemaphoreType.DMA((5,)),
        ],
        specs=[pl.BlockSpec(memory_space=pltpu.HBM)] * 3,
        vmem=63,
    )(member_concentration, courant_pairs, obs_list)
    first, second = swap(to_first, to_second, tiles)

    flat = lambda array: array.reshape(-1, LANES)
    cell = flat(obs_cell)
    cell_row = lax.dynamic_index_in_dim(
        cell.reshape(blocks, tiles, BLOCK, LANES), lax.axis_index("tile"), 1, False
    )
    forecast, *chunks = call(
        functools.partial(forecast_body, tiles=tiles, height=height),
        [(member_concentration.shape, f32)] + [((chip_rows, LANES), bf16)] * chips,
        [
            pltpu.VMEM((chips, chip_rows, LANES), bf16),
            pltpu.VMEM((blocks, region_rows, LANES), f32),
        ],
    )(
        member_concentration,
        courant_pairs,
        first,
        second,
        cell_row,
    )
    received = exchange(chunks)
    weights, values = call(
        functools.partial(
            weights_body, tiles=tiles, blocks=blocks, height=height, width=width, side=side
        ),
        [((16, depth * LANES), f32), ((depth, LANES), f32)],
        [pltpu.VMEM((16 * depth, LANES), f32)],
        flops=100_000_000,
    )(obs_list, first, second, cell, flat(obs_value), flat(obs_error))

    sizes = dict(sources=blocks, members=members, region_rows=region_rows)
    tall = patches * ensemble
    length = depth * LANES
    system_shape = (ensemble + 8, tall // 64 * LANES)
    wide_shape = (2 * (ensemble + 8), length)
    centred_shape = (ensemble, levels * BLOCK, LANES)
    share = functools.partial(share_body, region_rows=region_rows)
    mine, theirs = call(share, [((chips * all_rows, LANES), bf16)] * 2)(*received, values)
    theirs = swap_cores(theirs)
    to_first, to_second, wide = call(
        functools.partial(neighbours_body, **sizes),
        [(system_shape, f32), (system_shape, f32), (wide_shape, bf16)],
        [
            pltpu.VMEM(((ensemble + 8) * depth, LANES), f32),
            pltpu.VMEM((2 * tall, length), bf16),
            pltpu.VMEM((2 * tall, length), bf16),
        ],
    )(mine, theirs, weights, values)
    first, second = swap(to_first, to_second, tiles)
    own, centred = call(
        functools.partial(own_body, **sizes),
        [(system_shape, f32), (centred_shape, f32)],
        [pltpu.VMEM((tall, length), bf16), pltpu.VMEM((tall, length), bf16)],
        flops=50_000_000,
    )(mine, theirs, weights, wide)

    changes = call(
        functools.partial(analysis_body, patches=patches, **sizes),
        [((2 * region_rows, LANES), bf16)] * chips,
        [pltpu.VMEM((ensemble, ensemble, LANES), f32)],
    )(own, first, second, centred)
    returned = exchange(changes)
    mine, theirs = call(share, [((chips * region_rows, LANES), bf16)] * 2)(*returned, forecast)
    theirs = swap_cores(theirs)
    (analysis,) = call(
        output_body, [(forecast.shape, f32)], [pltpu.VMEM((blocks, region_rows, LANES), f32)]
    )(forecast, mine, theirs)
    return analysis


def solution(mesh):
    return jax.shard_map(
        shards,
        mesh=mesh,
        in_specs=(
            P("member", None, "tile", None),
            P(None, None, "tile", None),
            P(),
            P(),
            P(),
            P("tile", "member", None),
        ),
        out_specs=P("member", None, "tile", None),
        check_vma=False,
    )
```

```python
import functools

import jax
import jax.numpy as jnp
from jax import lax
from jax.experimental import pallas as pl
from jax.experimental.pallas import tpu as pltpu
from jax.sharding import PartitionSpec as P

PATCH = 16
LOC_LEN = 16
DIFFUSION = 0.05
LANES = 128
BLOCK = 8

f32 = jnp.float32
bf16 = jnp.bfloat16


def call(body, outs, scratch=(), flops=1_000_000, moved=1_000_000, specs=None, vmem=48):
    specs = {} if specs is None else {"in_specs": specs}
    return pl.pallas_call(
        body,
        **specs,
        out_shape=[jax.ShapeDtypeStruct(shape, kind) for shape, kind in outs],
        scratch_shapes=list(scratch),
        compiler_params=pltpu.CompilerParams(vmem_limit_bytes=vmem * 1024 * 1024),
        cost_estimate=pl.CostEstimate(flops=flops, bytes_accessed=moved, transcendentals=0),
    )


def split(number, size):
    if size & (size - 1) == 0:
        return number >> (size.bit_length() - 1), number & (size - 1)
    quotient = number // size
    return quotient, number - quotient * size


def wrapped(number, size):
    if size & (size - 1) == 0:
        return number & (size - 1)
    return lax.rem(number + size, size)


def iota(shape, axis):
    return lax.broadcasted_iota(jnp.int32, shape, axis)


def pick_lanes(values, index):
    rows = [
        jnp.take_along_axis(values[r : r + BLOCK], index, axis=1, mode="promise_in_bounds")
        for r in range(0, values.shape[0], BLOCK)
    ]
    return rows[0] if len(rows) == 1 else jnp.concatenate(rows, axis=0)


def transpose_chunks(parts):
    lane = iota(parts[0].shape, 1)
    low = lane < 64
    even = (lane & 32) == 0
    parts = list(parts)
    for i in (0, 1):
        a, b = parts[i], parts[i + 2]
        parts[i] = jnp.where(low, a, pltpu.roll(b, 64, 1))
        parts[i + 2] = jnp.where(low, pltpu.roll(a, 64, 1), b)
    for i in (0, 2):
        a, b = parts[i], parts[i + 1]
        parts[i] = jnp.where(even, a, pltpu.roll(b, 32, 1))
        parts[i + 1] = jnp.where(even, pltpu.roll(a, 96, 1), b)
    return parts


def pack_edges(
    tracer, courant, lists, to_first, to_second, first, last, first_rates, last_rates, numbers, arrived
):
    members, levels, side, width = tracer.shape
    copies = [
        pltpu.make_async_copy(source, target, arrived.at[i])
        for i, (source, target) in enumerate(
            (
                (tracer.at[:, :, 0:BLOCK, :], first),
                (tracer.at[:, :, side - BLOCK : side, :], last),
                (courant.at[:, :, 0:BLOCK, :], first_rates),
                (courant.at[:, :, side - BLOCK : side, :], last_rates),
                (lists, numbers),
            )
        )
    ]
    for copy in copies:
        copy.start()
    for copy in copies:
        copy.wait()
    even = lax.rem(lax.axis_index("tile"), 2) == 0

    def put(row, low, high):
        to_first[row : row + 1, :] = jnp.where(even, high, low)
        to_second[row : row + 1, :] = jnp.where(even, low, high)

    end = BLOCK - 1
    for b in range(members):
        for l in range(levels):
            row = b * levels + l
            put(row, first[b, l, 0:1, :], last[b, l, end : end + 1, :])
            put(8 + row, first[b, l, 1:2, :], last[b, l, end - 1 : end, :])
    for c in range(2):
        for l in range(levels):
            put(16 + c * levels + l, first_rates[c, l, 0:1, :], last_rates[c, l, end : end + 1, :])
    row = 24
    for a in range(numbers.shape[0]):
        for b in range(numbers.shape[1]):
            for s in range(0, numbers.shape[2], width):
                part = numbers[a, b : b + 1, s : s + width].astype(f32)
                to_first[row : row + 1, :] = part
                to_second[row : row + 1, :] = part
                row += 1


def coefficients(meridional, zonal):
    return (
        (1.0 - 4.0 * DIFFUSION) - jnp.abs(zonal) - jnp.abs(meridional),
        DIFFUSION + jnp.maximum(zonal, 0.0),
        DIFFUSION - jnp.minimum(zonal, 0.0),
        DIFFUSION + jnp.maximum(meridional, 0.0),
        DIFFUSION - jnp.minimum(meridional, 0.0),
    )


def stencil(current, south, north, factors):
    width = current.shape[1]
    centre, from_west, from_east, from_south, from_north = factors
    west = pltpu.roll(current, 1, 1)
    east = pltpu.roll(current, width - 1, 1)
    return (
        centre * current
        + from_west * west
        + from_east * east
        + from_south * south
        + from_north * north
    )


def beside(first, second, tile):
    even = lax.rem(tile, 2) == 0
    return jnp.where(even, second, first), jnp.where(even, first, second)


def swap(first, second, tiles):
    pairs = lambda start: [
        pair for i in range(start, tiles - 1, 2) for pair in ((i, i + 1), (i + 1, i))
    ]
    return lax.ppermute(first, "tile", pairs(0)), lax.ppermute(second, "tile", pairs(1))


def turn(s, chips):
    return (chips - s) % chips


def exchange(chunks):
    chips = len(chunks)
    device = lambda chip, core: 2 * chip + core
    swaps = lambda s: [
        (device(i, c), device(i ^ turn(s, chips), c)) for i in range(chips) for c in (0, 1)
    ]
    return [chunks[0]] + [lax.ppermute(chunks[s], "member", swaps(s)) for s in range(1, chips)]


def swap_cores(array):
    return lax.ppermute(array, "member", [(i, i ^ 1) for i in range(lax.axis_size("member"))])


def place():
    block = lax.axis_index("member")
    core = lax.rem(block, 2)
    return block, (block - core) // 2, core


def share_body(*refs, region_rows):
    chunks, (own, other) = refs[:-3], refs[-2:]
    _, _, core = place()
    first = core == 0
    each = own.shape[0] // len(chunks)
    half = chunks[0].shape[0] - 2 * region_rows
    lines = half // 2
    for s, chunk in enumerate(chunks):
        low, high = chunk[0:region_rows, :], chunk[region_rows : 2 * region_rows, :]
        row = s * each
        own[row : row + region_rows, :] = jnp.where(first, low, high)
        other[row : row + region_rows, :] = jnp.where(first, high, low)
        if each == region_rows:
            continue
        seen = chunk[2 * region_rows :, :].astype(f32)
        west = jnp.concatenate([seen[0 : lines - 8], seen[lines : 2 * lines - 8]], axis=0)
        east = jnp.concatenate([seen[8:lines], seen[lines + 8 : 2 * lines]], axis=0)
        own[row + region_rows : row + each, :] = jnp.where(first, west, east).astype(bf16)
        other[row + region_rows : row + each, :] = jnp.where(first, east, west).astype(bf16)


def pack(forecast):
    members, levels, side, width = forecast.shape
    for q in range(width // LANES):
        parts = [
            forecast[:, :, r : r + BLOCK, q * LANES : (q + 1) * LANES].reshape(-1, LANES)
            for r in range(0, side, BLOCK)
        ]
        for i, part in enumerate(transpose_chunks(parts)):
            yield 4 * q + i, part.astype(bf16)


def observe(cell, table, observed, rows, levels, side, width, height):
    members = len(observed[0])
    hits = levels * BLOCK
    for c in range(cell.shape[0]):
        above_row, column = split(cell[c], width)
        level, grid_row = split(above_row, height)
        _, local_row = split(grid_row, side)
        _, local_column = split(column, side)
        band, sub_row = split(local_row, BLOCK)
        high = level * BLOCK + sub_row
        low = band * side + local_column
        for h in [l * BLOCK + r for l in range(levels) for r in rows]:
            here = high == h
            for b in range(members):
                line = table[c, b * hits + h : b * hits + h + 1, :]
                line = jnp.broadcast_to(line, (BLOCK, LANES))
                observed[c][b] = jnp.where(here, pick_lanes(line, low), observed[c][b])


def draft_body(tracer, courant, cell, _, forecast, seen, table, *, height):
    members, levels, side, width = tracer.shape
    for l in range(levels):
        factors = coefficients(courant[0, l], courant[1, l])
        for b in range(members):
            current = tracer[b, l]
            for step in range(2):
                lower = pltpu.roll(current, 1, 0)
                upper = pltpu.roll(current, side - 1, 0)
                current = stencil(current, lower, upper, factors)
            forecast[b, l] = current
    for c, rounded in pack(forecast):
        table[c] = rounded.astype(f32)
    blocks = cell.shape[0]
    observed = [[jnp.zeros((BLOCK, LANES), f32) for _ in range(members)] for _ in range(blocks)]
    observe(cell, table, observed, range(BLOCK), levels, side, width, height)
    for c in range(blocks):
        for b in range(members):
            seen[c, b] = observed[c][b]


def forecast_body(
    tracer, courant, draft, seen, first, second, cell, forecast, *rest, tiles, height
):
    *chunks, send, table = rest
    members, levels, side, width = tracer.shape
    blocks = width // side
    tile = lax.axis_index("tile")
    planes = members * levels
    region_rows = planes * BLOCK
    south, north = beside(first[0:24, :], second[0:24, :], tile)
    own = lambda at: jnp.concatenate(
        [tracer[b, l, at : at + 1, :] for b in range(members) for l in range(levels)], axis=0
    )
    rates = lambda part, at: jnp.concatenate(
        [courant[part, l, at : at + 1, :] for l in range(levels)] * members, axis=0
    )
    here = lambda at: coefficients(rates(0, at), rates(1, at))

    def there(source):
        twice = lambda at: jnp.concatenate([source[at : at + levels]] * members, axis=0)
        return coefficients(twice(16), twice(16 + levels))

    forecast[...] = draft[...]
    for other, inside, at, toward in (
        (south, tile > 0, 0, 1),
        (north, tile < tiles - 1, side - 1, -1),
    ):
        order = lambda outer, inner: (outer, inner) if toward == 1 else (inner, outer)
        rows = [own(at + toward * i) for i in range(4)]
        factors = [here(at + toward * i) for i in range(3)]
        near, far = other[0:planes], other[8 : 8 + planes]
        outside = jnp.where(inside, stencil(near, *order(far, rows[0]), there(other)), 0.0)
        outer = [near, rows[0], rows[1]]
        once = [stencil(rows[i], *order(outer[i], rows[i + 1]), factors[i]) for i in range(3)]
        final = (
            stencil(once[0], *order(outside, once[1]), factors[0]),
            stencil(once[1], *order(once[0], once[2]), factors[1]),
        )
        for i, values in enumerate(final):
            row = at + toward * i
            for b in range(members):
                for l in range(levels):
                    plane = b * levels + l
                    forecast[b, l, row : row + 1, :] = values[plane : plane + 1, :]

    for c, rounded in pack(forecast):
        send[c // 2, c % 2 * region_rows : (c % 2 + 1) * region_rows, :] = rounded
        table[c] = rounded.astype(f32)
    observed = [[seen[c, b] for b in range(members)] for c in range(blocks)]
    edge = (0, 1, BLOCK - 2, BLOCK - 1)
    observe(cell, table, observed, edge, levels, side, width, height)
    for chip in range(blocks // 2):
        lines = [
            observed[(2 * chip + r - 1) % blocks][b] for b in range(members) for r in range(4)
        ]
        for i in range(0, len(lines), 2):
            at = 2 * region_rows + i * BLOCK
            send[chip, at : at + 2 * BLOCK, :] = jnp.concatenate(lines[i : i + 2], axis=0).astype(
                bf16
            )
    _, chip, _ = place()
    for s, chunk in enumerate(chunks):
        chunk[...] = send[chip ^ turn(s, len(chunks))]


def weights_body(
    lists, first, second, cell, value, variance, weights, values, planes, *, tiles, blocks, height, width, side
):
    tile = lax.axis_index("tile")
    block = lax.axis_index("member")
    own_lists = slice(24, 24 + lists.shape[0] * lists.shape[1] * lists.shape[2] // width)
    south, north = beside(first[own_lists, :], second[own_lists, :], tile)
    per_side = side // PATCH
    patches = per_side * per_side
    slots = lists.shape[2]
    depth = 3 * BLOCK
    rows, columns, sizes = [], [], []
    for r in range(3):
        column_block = wrapped(block + (r - 1), blocks)
        first = pl.multiple_of((column_block * tiles + tile) * BLOCK, BLOCK)
        cells = cell[pl.ds(first, BLOCK), :]
        above_row, column = split(cells, width)
        _, grid_row = split(above_row, height)
        rows.append(grid_row)
        columns.append(column)
        sizes.append(variance[pl.ds(first, BLOCK), :])
        values[r * BLOCK : (r + 1) * BLOCK, :] = value[pl.ds(first, BLOCK), :]
    grid_row = jnp.concatenate(rows, axis=0)
    column = jnp.concatenate(columns, axis=0)
    size = jnp.concatenate(sizes, axis=0)

    def pieces(dt, p):
        if dt == 0:
            return [lists[p // per_side, p % per_side : p % per_side + 1, :]]
        source = south if dt < 0 else north
        each = slots // width
        return [
            source[p * each + i : p * each + i + 1].astype(jnp.int32) for i in range(each)
        ]

    index = 0
    for dt in (0, -1, 1):
        for p in range(patches):
            count = jnp.zeros((depth, LANES), f32)
            for part in pieces(dt, p):
                length = part.shape[1]
                region, within = split(part, BLOCK * LANES)
                region_column, region_row = split(region, tiles)
                line, lane = split(within, LANES)
                near = wrapped(region_column - block + 1, blocks)
                fits = (part >= 0) & (region_row == tile) & (near < 3)
                line = jnp.where(fits, near * BLOCK + line, -1)
                one = (iota((depth, length), 0) == line).astype(f32).astype(bf16)
                other = (iota((LANES, length), 0) == lane).astype(f32).astype(bf16)
                count += lax.dot_general(
                    one, other, (((1,), (1,)), ((), ())), preferred_element_type=f32
                )
            patch_row = (tile + dt) * per_side + p // per_side
            patch_column = block * per_side + p % per_side
            row_gap = (grid_row - patch_row * PATCH - PATCH // 2).astype(f32) + 0.5
            turned = column - patch_column * PATCH - PATCH // 2 + width // 2
            column_gap = (wrapped(turned, width) - width // 2).astype(f32) + 0.5
            near = jnp.exp(
                -(row_gap * row_gap + column_gap * column_gap) / (2.0 * LOC_LEN * LOC_LEN)
            )
            planes[index * depth : (index + 1) * depth, :] = count * (near / size)
            index += 1
    for extra in range(index, 16):
        planes[extra * depth : (extra + 1) * depth, :] = jnp.zeros((depth, LANES), f32)
    for i in range(depth):
        weights[:, i * LANES : (i + 1) * LANES] = planes[pl.ds(i, 16, stride=depth), :]


def halves(values):
    high = values.astype(bf16)
    return high, (values - high.astype(f32)).astype(bf16)


def dot_rows(left, right):
    return lax.dot_general(left, right, (((1,), (1,)), ((), ())), preferred_element_type=f32)


def scale(spread, weights, tall_high, tall_low, at, first):
    ensemble = spread.shape[0]
    for p in range(tall_high.shape[0] // ensemble):
        high, low = halves(spread * weights[first + p : first + p + 1, at])
        tall_high[p * ensemble : (p + 1) * ensemble, at] = high
        tall_low[p * ensemble : (p + 1) * ensemble, at] = low


def products(wide, tall_high, tall_low):
    rows = wide.shape[0] // 2
    both = dot_rows(wide[...], tall_high[...])
    result = both[0:rows] + both[rows:] + dot_rows(wide[0:rows, :], tall_low[...])
    count = result.shape[1] // 64
    if count % 2:
        result = jnp.concatenate([result, jnp.zeros((rows, 64), f32)], axis=1)
    found = []
    for n in range(count):
        piece = result[:, n // 2 * LANES : (n // 2 + 1) * LANES]
        if n % 2:
            piece = pltpu.roll(piece, 64, 1)
        found.append(jnp.where(iota(piece.shape, 1) < 64, piece, 0.0))
    return found


def neighbours_body(
    mine, theirs, weights, values, to_first, to_second, wide, planes, tall_high, tall_low, *, sources, members, region_rows
):
    depth = 3 * BLOCK
    each = 2 * mine.shape[0] // sources
    _, chip, core = place()
    ensemble = sources * members
    total = jnp.zeros((depth, LANES), f32)
    for s in range(sources):
        source, row = (mine, theirs)[s % 2], s // 2 * each
        both = source[row + region_rows : row + each, :].astype(f32)
        device = 2 * (chip ^ turn(s // 2, sources // 2)) + (core ^ (s % 2))
        at = pl.multiple_of(device * (members * depth), BLOCK)
        planes[pl.ds(at, members * depth), :] = both
        for b in range(members):
            total += both[b * depth : (b + 1) * depth, :]
    mean = total / ensemble
    for k in range(ensemble):
        planes[k * depth : (k + 1) * depth, :] -= mean
    planes[ensemble * depth : (ensemble + 1) * depth, :] = values[...] - mean
    for k in range(ensemble + 1, ensemble + 8):
        planes[k * depth : (k + 1) * depth, :] = jnp.zeros((depth, LANES), f32)
    rows = ensemble + 8
    patches = tall_high.shape[0] // (2 * ensemble)
    for i in range(depth):
        at = slice(i * LANES, (i + 1) * LANES)
        tile = planes[pl.ds(i, rows, stride=depth), :]
        high, low = halves(tile)
        wide[0:rows, at] = high
        wide[rows : 2 * rows, at] = low
        scale(tile[0:ensemble, :], weights, tall_high, tall_low, at, patches)
    found = products(wide, tall_high, tall_low)
    odd = lax.rem(lax.axis_index("tile"), 2) == 1
    count = len(found) // 2
    for i in range(count):
        at = slice(i * LANES, (i + 1) * LANES)
        for_south, for_north = found[i], found[count + i]
        to_first[:, at] = jnp.where(odd, for_south, for_north)
        to_second[:, at] = jnp.where(odd, for_north, for_south)


def own_body(
    mine, theirs, weights, wide, own, centred, tall_high, tall_low, *, sources, members, region_rows
):
    _, chip, core = place()
    each = 2 * mine.shape[0] // sources
    ensemble = sources * members
    hits = region_rows // members
    total = jnp.zeros((hits, LANES), f32)
    for s in range(sources):
        source, row = (mine, theirs)[s % 2], s // 2 * each
        device = 2 * (chip ^ turn(s // 2, sources // 2)) + (core ^ (s % 2))
        part = source[row : row + region_rows, :].astype(f32)
        for b in range(members):
            one = part[b * hits : (b + 1) * hits, :]
            centred[device * members + b] = one
            total += one
    mean = total / ensemble
    for k in range(ensemble):
        centred[k] -= mean
    rows = ensemble + 8
    for i in range(0, wide.shape[1], LANES):
        at = slice(i, i + LANES)
        spread = wide[0:ensemble, at].astype(f32) + wide[rows : rows + ensemble, at].astype(f32)
        scale(spread, weights, tall_high, tall_low, at, 0)
    for i, piece in enumerate(products(wide, tall_high, tall_low)):
        own[:, i * LANES : (i + 1) * LANES] = piece


def analysis_body(own, first, second, centred, *refs, patches, sources, members, region_rows):
    chunks, factors = refs[:-1], refs[-1]
    _, chip, _ = place()
    ensemble = sources * members
    hits = region_rows // members
    count = patches * ensemble // 64
    group = 64 // ensemble
    row = iota((ensemble + 8, LANES), 0)
    lane = iota((ensemble + 8, LANES), 1)
    within = lane & (ensemble - 1)
    start = jnp.where(
        (row == within) & (row < ensemble), jnp.where(lane < 64, ensemble - 1.0, 1.0), 0.0
    )
    lane8 = iota((BLOCK, LANES), 1)
    group_start = (lane8 & 63) & ~(ensemble - 1)
    transforms = []
    for i in range(count):
        at = slice(i * LANES, (i + 1) * LANES)
        state = own[:, at] + first[:, at] + second[:, at] + start
        columns = [pick_lanes(state, group_start + k) for k in range(ensemble)]
        pivots = jnp.ones((ensemble, LANES), f32)
        for k in range(ensemble):
            pivot = columns[k][k : k + 1, :]
            factor = jnp.where(row > k, columns[k], 0.0) / pivot
            for j in range(k + 1, ensemble):
                columns[j] = columns[j] - factor * columns[j][k : k + 1, :]
            state = state - factor * state[k : k + 1, :]
            pivots = jnp.where(row[0:ensemble] == k, pivot, pivots)
        inverse = state[0:ensemble, :] * lax.rsqrt(pivots)
        mean_weight = -state[ensemble : ensemble + 1, :]
        unit = jnp.where(row[0:ensemble] == within[0:ensemble], 1.0, 0.0)
        transforms.append(mean_weight + (ensemble - 1.0) ** 0.5 * inverse - unit)

    side_lanes = 32
    patch = (lane8 // (2 * side_lanes)) * 2 + (lane8 & (side_lanes - 1)) // PATCH
    inside = 64 + (patch & (group - 1)) * ensemble if group > 1 else 64 + 0 * patch
    which = patch // group
    for j in range(ensemble):
        chosen = pick_lanes(transforms[0], inside + j)
        for i in range(1, count):
            other = pick_lanes(transforms[i], inside + j)
            chosen = jnp.where(jnp.broadcast_to(which[0:1] == i, chosen.shape), other, chosen)
        factors[j] = chosen

    for s, chunk in enumerate(chunks):
        for c in (0, 1):
            first_member = (2 * (chip ^ turn(s, len(chunks))) + c) * members
            totals = [jnp.zeros((hits, LANES), f32) for _ in range(members)]
            for j in range(ensemble):
                centred_j = centred[j]
                for b in range(members):
                    totals[b] += factors[j, pl.ds(first_member + b, 1), :] * centred_j
            at = slice(c * region_rows, (c + 1) * region_rows)
            chunk[at, :] = jnp.concatenate(totals, axis=0).astype(bf16)


def output_body(forecast, mine, theirs, analysis, ordered):
    members, levels, side, width = forecast.shape
    _, chip, core = place()
    rows = ordered.shape[1]
    chips = mine.shape[0] // rows
    for s in range(chips):
        at = slice(s * rows, (s + 1) * rows)
        source = 2 * (chip ^ turn(s, chips))
        ordered[source + core] = mine[at, :].astype(f32)
        ordered[source + (core ^ 1)] = theirs[at, :].astype(f32)
    for q in range(width // LANES):
        parts = [ordered[4 * q + c] for c in range(4)]
        at = slice(q * LANES, (q + 1) * LANES)
        for r, part in enumerate(transpose_chunks(parts)):
            rows = slice(r * BLOCK, (r + 1) * BLOCK)
            analysis[:, :, rows, at] = forecast[:, :, rows, at] + part.reshape(
                members, levels, BLOCK, LANES
            )


def shards(member_concentration, courant_pairs, obs_cell, obs_value, obs_error, obs_list):
    members, levels, side, width = member_concentration.shape
    blocks = lax.axis_size("member")
    tiles = lax.axis_size("tile")
    height = side * tiles
    ensemble = members * blocks
    per_side = side // PATCH
    patches = per_side * per_side
    slots = obs_list.shape[2]
    region_rows = members * levels * BLOCK
    depth = 3 * BLOCK
    all_rows = region_rows + members * depth
    chips = blocks // 2
    chip_rows = 2 * region_rows + members * 4 * BLOCK
    edge_rows = -(-(24 + patches * slots // width) // 8) * 8
    edge_shape = (members, levels, BLOCK, width)
    rate_shape = (2, levels, BLOCK, width)

    to_first, to_second = call(
        pack_edges,
        [((edge_rows, width), f32)] * 2,
        [
            pltpu.VMEM(edge_shape, f32),
            pltpu.VMEM(edge_shape, f32),
            pltpu.VMEM(rate_shape, f32),
            pltpu.VMEM(rate_shape, f32),
            pltpu.VMEM(obs_list.shape, jnp.int32),
            pltpu.SemaphoreType.DMA((5,)),
        ],
        specs=[pl.BlockSpec(memory_space=pltpu.HBM)] * 3,
        vmem=63,
    )(member_concentration, courant_pairs, obs_list)
    first, second = swap(to_first, to_second, tiles)

    whole = pl.BlockSpec(memory_space=pltpu.VMEM)
    flat = lambda array: array.reshape(-1, LANES)
    cell = flat(obs_cell)
    cell_row = lax.dynamic_index_in_dim(
        cell.reshape(blocks, tiles, BLOCK, LANES), lax.axis_index("tile"), 1, False
    )
    draft, seen = call(
        functools.partial(draft_body, height=height),
        [(member_concentration.shape, f32), ((blocks, members, BLOCK, LANES), f32)],
        [pltpu.VMEM((blocks, region_rows, LANES), f32)],
        flops=50_000_000,
        specs=[whole, whole, whole, pl.BlockSpec(memory_space=pltpu.HBM)],
    )(member_concentration, courant_pairs, cell_row, to_second)
    forecast, *chunks = call(
        functools.partial(forecast_body, tiles=tiles, height=height),
        [(member_concentration.shape, f32)] + [((chip_rows, LANES), bf16)] * chips,
        [
            pltpu.VMEM((chips, chip_rows, LANES), bf16),
            pltpu.VMEM((blocks, region_rows, LANES), f32),
        ],
    )(
        member_concentration,
        courant_pairs,
        draft,
        seen,
        first,
        second,
        cell_row,
    )
    received = exchange(chunks)
    weights, values = call(
        functools.partial(
            weights_body, tiles=tiles, blocks=blocks, height=height, width=width, side=side
        ),
        [((16, depth * LANES), f32), ((depth, LANES), f32)],
        [pltpu.VMEM((16 * depth, LANES), f32)],
        flops=100_000_000,
    )(obs_list, first, second, cell, flat(obs_value), flat(obs_error))

    sizes = dict(sources=blocks, members=members, region_rows=region_rows)
    tall = patches * ensemble
    length = depth * LANES
    system_shape = (ensemble + 8, tall // 64 * LANES)
    wide_shape = (2 * (ensemble + 8), length)
    centred_shape = (ensemble, levels * BLOCK, LANES)
    share = functools.partial(share_body, region_rows=region_rows)
    mine, theirs = call(share, [((chips * all_rows, LANES), bf16)] * 2)(*received, values)
    theirs = swap_cores(theirs)
    to_first, to_second, wide = call(
        functools.partial(neighbours_body, **sizes),
        [(system_shape, f32), (system_shape, f32), (wide_shape, bf16)],
        [
            pltpu.VMEM(((ensemble + 8) * depth, LANES), f32),
            pltpu.VMEM((2 * tall, length), bf16),
            pltpu.VMEM((2 * tall, length), bf16),
        ],
    )(mine, theirs, weights, values)
    first, second = swap(to_first, to_second, tiles)
    own, centred = call(
        functools.partial(own_body, **sizes),
        [(system_shape, f32), (centred_shape, f32)],
        [pltpu.VMEM((tall, length), bf16), pltpu.VMEM((tall, length), bf16)],
        flops=50_000_000,
    )(mine, theirs, weights, wide)

    changes = call(
        functools.partial(analysis_body, patches=patches, **sizes),
        [((2 * region_rows, LANES), bf16)] * chips,
        [pltpu.VMEM((ensemble, ensemble, LANES), f32)],
    )(own, first, second, centred)
    returned = exchange(changes)
    mine, theirs = call(share, [((chips * region_rows, LANES), bf16)] * 2)(*returned, forecast)
    theirs = swap_cores(theirs)
    (analysis,) = call(
        output_body, [(forecast.shape, f32)], [pltpu.VMEM((blocks, region_rows, LANES), f32)]
    )(forecast, mine, theirs)
    return analysis


def solution(mesh):
    return jax.shard_map(
        shards,
        mesh=mesh,
        in_specs=(
            P("member", None, "tile", None),
            P(None, None, "tile", None),
            P(),
            P(),
            P(),
            P("tile", "member", None),
        ),
        out_specs=P("member", None, "tile", None),
        check_vma=False,
    )
```

```python
import functools

import jax
import jax.numpy as jnp
from jax import lax
from jax.experimental import pallas as pl
from jax.experimental.pallas import tpu as pltpu
from jax.sharding import PartitionSpec as P

PATCH = 16
LOC_LEN = 16
DIFFUSION = 0.05
LANES = 128
BLOCK = 8

f32 = jnp.float32
bf16 = jnp.bfloat16


def call(body, outs, scratch=(), flops=1_000_000, moved=1_000_000, specs=None, vmem=48):
    specs = {} if specs is None else {"in_specs": specs}
    return pl.pallas_call(
        body,
        **specs,
        out_shape=[jax.ShapeDtypeStruct(shape, kind) for shape, kind in outs],
        scratch_shapes=list(scratch),
        compiler_params=pltpu.CompilerParams(vmem_limit_bytes=vmem * 1024 * 1024),
        cost_estimate=pl.CostEstimate(flops=flops, bytes_accessed=moved, transcendentals=0),
    )


def split(number, size):
    if size & (size - 1) == 0:
        return number >> (size.bit_length() - 1), number & (size - 1)
    quotient = number // size
    return quotient, number - quotient * size


def wrapped(number, size):
    if size & (size - 1) == 0:
        return number & (size - 1)
    return lax.rem(number + size, size)


def iota(shape, axis):
    return lax.broadcasted_iota(jnp.int32, shape, axis)


def pick_lanes(values, index):
    rows = [
        jnp.take_along_axis(values[r : r + BLOCK], index, axis=1, mode="promise_in_bounds")
        for r in range(0, values.shape[0], BLOCK)
    ]
    return rows[0] if len(rows) == 1 else jnp.concatenate(rows, axis=0)


def transpose_chunks(parts):
    lane = iota(parts[0].shape, 1)
    low = lane < 64
    even = (lane & 32) == 0
    parts = list(parts)
    for i in (0, 1):
        a, b = parts[i], parts[i + 2]
        parts[i] = jnp.where(low, a, pltpu.roll(b, 64, 1))
        parts[i + 2] = jnp.where(low, pltpu.roll(a, 64, 1), b)
    for i in (0, 2):
        a, b = parts[i], parts[i + 1]
        parts[i] = jnp.where(even, a, pltpu.roll(b, 32, 1))
        parts[i + 1] = jnp.where(even, pltpu.roll(a, 96, 1), b)
    return parts


def pack_edges(
    tracer, courant, lists, to_first, to_second, first, last, first_rates, last_rates, numbers, arrived
):
    members, levels, side, width = tracer.shape
    copies = [
        pltpu.make_async_copy(source, target, arrived.at[i])
        for i, (source, target) in enumerate(
            (
                (tracer.at[:, :, 0:BLOCK, :], first),
                (tracer.at[:, :, side - BLOCK : side, :], last),
                (courant.at[:, :, 0:BLOCK, :], first_rates),
                (courant.at[:, :, side - BLOCK : side, :], last_rates),
                (lists, numbers),
            )
        )
    ]
    for copy in copies:
        copy.start()
    for copy in copies:
        copy.wait()
    odd = lax.rem(lax.axis_index("tile"), 2) == 1

    def put(row, low, high):
        to_first[row : row + 1, :] = jnp.where(odd, high, low)
        to_second[row : row + 1, :] = jnp.where(odd, low, high)

    end = BLOCK - 1
    for b in range(members):
        for l in range(levels):
            row = b * levels + l
            put(row, first[b, l, 0:1, :], last[b, l, end : end + 1, :])
            put(8 + row, first[b, l, 1:2, :], last[b, l, end - 1 : end, :])
    for c in range(2):
        for l in range(levels):
            put(16 + c * levels + l, first_rates[c, l, 0:1, :], last_rates[c, l, end : end + 1, :])
    row = 24
    for a in range(numbers.shape[0]):
        for b in range(numbers.shape[1]):
            for s in range(0, numbers.shape[2], width):
                part = numbers[a, b : b + 1, s : s + width].astype(f32)
                to_first[row : row + 1, :] = part
                to_second[row : row + 1, :] = part
                row += 1


def coefficients(meridional, zonal):
    return (
        (1.0 - 4.0 * DIFFUSION) - jnp.abs(zonal) - jnp.abs(meridional),
        DIFFUSION + jnp.maximum(zonal, 0.0),
        DIFFUSION - jnp.minimum(zonal, 0.0),
        DIFFUSION + jnp.maximum(meridional, 0.0),
        DIFFUSION - jnp.minimum(meridional, 0.0),
    )


def stencil(current, south, north, factors):
    width = current.shape[1]
    centre, from_west, from_east, from_south, from_north = factors
    west = pltpu.roll(current, 1, 1)
    east = pltpu.roll(current, width - 1, 1)
    return (
        centre * current
        + from_west * west
        + from_east * east
        + from_south * south
        + from_north * north
    )


def beside(first, second, tile):
    odd = lax.rem(tile, 2) == 1
    return jnp.where(odd, second, first), jnp.where(odd, first, second)


def swap(first, second, tiles, lead):
    pairs = lambda start: [
        pair for i in range(start, tiles - 1, 2) for pair in ((i, i + 1), (i + 1, i))
    ]
    return (
        lax.ppermute(first, "tile", pairs(lead)),
        lax.ppermute(second, "tile", pairs(1 - lead)),
    )


def turn(s, chips):
    return (chips - s) % chips


def exchange(chunks):
    chips = len(chunks)
    device = lambda chip, core: 2 * chip + core
    swaps = lambda s: [
        (device(i, c), device(i ^ turn(s, chips), c)) for i in range(chips) for c in (0, 1)
    ]
    return [chunks[0]] + [lax.ppermute(chunks[s], "member", swaps(s)) for s in range(1, chips)]


def swap_cores(array):
    return lax.ppermute(array, "member", [(i, i ^ 1) for i in range(lax.axis_size("member"))])


def place():
    block = lax.axis_index("member")
    core = lax.rem(block, 2)
    return block, (block - core) // 2, core


def share_body(*refs, region_rows):
    chunks, (own, other) = refs[:-3], refs[-2:]
    _, _, core = place()
    first = core == 0
    each = own.shape[0] // len(chunks)
    half = chunks[0].shape[0] - 2 * region_rows
    lines = half // 2
    for s, chunk in enumerate(chunks):
        low, high = chunk[0:region_rows, :], chunk[region_rows : 2 * region_rows, :]
        row = s * each
        own[row : row + region_rows, :] = jnp.where(first, low, high)
        other[row : row + region_rows, :] = jnp.where(first, high, low)
        if each == region_rows:
            continue
        seen = chunk[2 * region_rows :, :].astype(f32)
        west = jnp.concatenate([seen[0 : lines - 8], seen[lines : 2 * lines - 8]], axis=0)
        east = jnp.concatenate([seen[8:lines], seen[lines + 8 : 2 * lines]], axis=0)
        own[row + region_rows : row + each, :] = jnp.where(first, west, east).astype(bf16)
        other[row + region_rows : row + each, :] = jnp.where(first, east, west).astype(bf16)


def pack(forecast):
    members, levels, side, width = forecast.shape
    for q in range(width // LANES):
        parts = [
            forecast[:, :, r : r + BLOCK, q * LANES : (q + 1) * LANES].reshape(-1, LANES)
            for r in range(0, side, BLOCK)
        ]
        for i, part in enumerate(transpose_chunks(parts)):
            yield 4 * q + i, part.astype(bf16)


def observe(cell, table, observed, rows, levels, side, width, height):
    members = len(observed[0])
    hits = levels * BLOCK
    for c in range(cell.shape[0]):
        above_row, column = split(cell[c], width)
        level, grid_row = split(above_row, height)
        _, local_row = split(grid_row, side)
        _, local_column = split(column, side)
        band, sub_row = split(local_row, BLOCK)
        high = level * BLOCK + sub_row
        low = band * side + local_column
        for h in [l * BLOCK + r for l in range(levels) for r in rows]:
            here = high == h
            for b in range(members):
                line = table[c, b * hits + h : b * hits + h + 1, :]
                line = jnp.broadcast_to(line, (BLOCK, LANES))
                observed[c][b] = jnp.where(here, pick_lanes(line, low), observed[c][b])


def draft_body(tracer, courant, cell, _, forecast, seen, table, *, height):
    members, levels, side, width = tracer.shape
    for l in range(levels):
        factors = coefficients(courant[0, l], courant[1, l])
        for b in range(members):
            current = tracer[b, l]
            for step in range(2):
                lower = pltpu.roll(current, 1, 0)
                upper = pltpu.roll(current, side - 1, 0)
                current = stencil(current, lower, upper, factors)
            forecast[b, l] = current
    for c, rounded in pack(forecast):
        table[c] = rounded.astype(f32)
    blocks = cell.shape[0]
    observed = [[jnp.zeros((BLOCK, LANES), f32) for _ in range(members)] for _ in range(blocks)]
    observe(cell, table, observed, range(BLOCK), levels, side, width, height)
    for c in range(blocks):
        for b in range(members):
            seen[c, b] = observed[c][b]


def forecast_body(
    tracer, courant, draft, seen, first, second, cell, forecast, *rest, tiles, height
):
    *chunks, send, table = rest
    members, levels, side, width = tracer.shape
    blocks = width // side
    tile = lax.axis_index("tile")
    planes = members * levels
    region_rows = planes * BLOCK
    south, north = beside(first[0:24, :], second[0:24, :], tile)
    own = lambda at: jnp.concatenate(
        [tracer[b, l, at : at + 1, :] for b in range(members) for l in range(levels)], axis=0
    )
    rates = lambda part, at: jnp.concatenate(
        [courant[part, l, at : at + 1, :] for l in range(levels)] * members, axis=0
    )
    here = lambda at: coefficients(rates(0, at), rates(1, at))

    def there(source):
        twice = lambda at: jnp.concatenate([source[at : at + levels]] * members, axis=0)
        return coefficients(twice(16), twice(16 + levels))

    forecast[...] = draft[...]
    for other, inside, at, toward in (
        (south, tile > 0, 0, 1),
        (north, tile < tiles - 1, side - 1, -1),
    ):
        order = lambda outer, inner: (outer, inner) if toward == 1 else (inner, outer)
        rows = [own(at + toward * i) for i in range(4)]
        factors = [here(at + toward * i) for i in range(3)]
        near, far = other[0:planes], other[8 : 8 + planes]
        outside = jnp.where(inside, stencil(near, *order(far, rows[0]), there(other)), 0.0)
        outer = [near, rows[0], rows[1]]
        once = [stencil(rows[i], *order(outer[i], rows[i + 1]), factors[i]) for i in range(3)]
        final = (
            stencil(once[0], *order(outside, once[1]), factors[0]),
            stencil(once[1], *order(once[0], once[2]), factors[1]),
        )
        for i, values in enumerate(final):
            row = at + toward * i
            for b in range(members):
                for l in range(levels):
                    plane = b * levels + l
                    forecast[b, l, row : row + 1, :] = values[plane : plane + 1, :]

    for c, rounded in pack(forecast):
        send[c // 2, c % 2 * region_rows : (c % 2 + 1) * region_rows, :] = rounded
        table[c] = rounded.astype(f32)
    observed = [[seen[c, b] for b in range(members)] for c in range(blocks)]
    edge = (0, 1, BLOCK - 2, BLOCK - 1)
    observe(cell, table, observed, edge, levels, side, width, height)
    for chip in range(blocks // 2):
        lines = [
            observed[(2 * chip + r - 1) % blocks][b] for b in range(members) for r in range(4)
        ]
        for i in range(0, len(lines), 2):
            at = 2 * region_rows + i * BLOCK
            send[chip, at : at + 2 * BLOCK, :] = jnp.concatenate(lines[i : i + 2], axis=0).astype(
                bf16
            )
    _, chip, _ = place()
    for s, chunk in enumerate(chunks):
        chunk[...] = send[chip ^ turn(s, len(chunks))]


def weights_body(
    lists, first, second, cell, value, variance, weights, values, planes, *, tiles, blocks, height, width, side
):
    tile = lax.axis_index("tile")
    block = lax.axis_index("member")
    own_lists = slice(24, 24 + lists.shape[0] * lists.shape[1] * lists.shape[2] // width)
    south, north = beside(first[own_lists, :], second[own_lists, :], tile)
    per_side = side // PATCH
    patches = per_side * per_side
    slots = lists.shape[2]
    depth = 3 * BLOCK
    rows, columns, sizes = [], [], []
    for r in range(3):
        column_block = wrapped(block + (r - 1), blocks)
        first = pl.multiple_of((column_block * tiles + tile) * BLOCK, BLOCK)
        cells = cell[pl.ds(first, BLOCK), :]
        above_row, column = split(cells, width)
        _, grid_row = split(above_row, height)
        rows.append(grid_row)
        columns.append(column)
        sizes.append(variance[pl.ds(first, BLOCK), :])
        values[r * BLOCK : (r + 1) * BLOCK, :] = value[pl.ds(first, BLOCK), :]
    grid_row = jnp.concatenate(rows, axis=0)
    column = jnp.concatenate(columns, axis=0)
    size = jnp.concatenate(sizes, axis=0)

    def pieces(dt, p):
        if dt == 0:
            return [lists[p // per_side, p % per_side : p % per_side + 1, :]]
        source = south if dt < 0 else north
        each = slots // width
        return [
            source[p * each + i : p * each + i + 1].astype(jnp.int32) for i in range(each)
        ]

    index = 0
    for dt in (0, -1, 1):
        for p in range(patches):
            count = jnp.zeros((depth, LANES), f32)
            for part in pieces(dt, p):
                length = part.shape[1]
                region, within = split(part, BLOCK * LANES)
                region_column, region_row = split(region, tiles)
                line, lane = split(within, LANES)
                near = wrapped(region_column - block + 1, blocks)
                fits = (part >= 0) & (region_row == tile) & (near < 3)
                line = jnp.where(fits, near * BLOCK + line, -1)
                one = (iota((depth, length), 0) == line).astype(f32).astype(bf16)
                other = (iota((LANES, length), 0) == lane).astype(f32).astype(bf16)
                count += lax.dot_general(
                    one, other, (((1,), (1,)), ((), ())), preferred_element_type=f32
                )
            patch_row = (tile + dt) * per_side + p // per_side
            patch_column = block * per_side + p % per_side
            row_gap = (grid_row - patch_row * PATCH - PATCH // 2).astype(f32) + 0.5
            turned = column - patch_column * PATCH - PATCH // 2 + width // 2
            column_gap = (wrapped(turned, width) - width // 2).astype(f32) + 0.5
            near = jnp.exp(
                -(row_gap * row_gap + column_gap * column_gap) / (2.0 * LOC_LEN * LOC_LEN)
            )
            planes[index * depth : (index + 1) * depth, :] = count * (near / size)
            index += 1
    for extra in range(index, 16):
        planes[extra * depth : (extra + 1) * depth, :] = jnp.zeros((depth, LANES), f32)
    for i in range(depth):
        weights[:, i * LANES : (i + 1) * LANES] = planes[pl.ds(i, 16, stride=depth), :]


def halves(values):
    high = values.astype(bf16)
    return high, (values - high.astype(f32)).astype(bf16)


def dot_rows(left, right):
    return lax.dot_general(left, right, (((1,), (1,)), ((), ())), preferred_element_type=f32)


def scale(spread, weights, tall_high, tall_low, at, first):
    ensemble = spread.shape[0]
    for p in range(tall_high.shape[0] // ensemble):
        high, low = halves(spread * weights[first + p : first + p + 1, at])
        tall_high[p * ensemble : (p + 1) * ensemble, at] = high
        tall_low[p * ensemble : (p + 1) * ensemble, at] = low


def products(wide, tall_high, tall_low):
    rows = wide.shape[0] // 2
    both = dot_rows(wide[...], tall_high[...])
    result = both[0:rows] + both[rows:] + dot_rows(wide[0:rows, :], tall_low[...])
    count = result.shape[1] // 64
    if count % 2:
        result = jnp.concatenate([result, jnp.zeros((rows, 64), f32)], axis=1)
    found = []
    for n in range(count):
        piece = result[:, n // 2 * LANES : (n // 2 + 1) * LANES]
        if n % 2:
            piece = pltpu.roll(piece, 64, 1)
        found.append(jnp.where(iota(piece.shape, 1) < 64, piece, 0.0))
    return found


def neighbours_body(
    mine, theirs, weights, values, to_first, to_second, wide, planes, tall_high, tall_low, *, sources, members, region_rows
):
    depth = 3 * BLOCK
    each = 2 * mine.shape[0] // sources
    _, chip, core = place()
    ensemble = sources * members
    total = jnp.zeros((depth, LANES), f32)
    for s in range(sources):
        source, row = (mine, theirs)[s % 2], s // 2 * each
        both = source[row + region_rows : row + each, :].astype(f32)
        device = 2 * (chip ^ turn(s // 2, sources // 2)) + (core ^ (s % 2))
        at = pl.multiple_of(device * (members * depth), BLOCK)
        planes[pl.ds(at, members * depth), :] = both
        for b in range(members):
            total += both[b * depth : (b + 1) * depth, :]
    mean = total / ensemble
    for k in range(ensemble):
        planes[k * depth : (k + 1) * depth, :] -= mean
    planes[ensemble * depth : (ensemble + 1) * depth, :] = values[...] - mean
    for k in range(ensemble + 1, ensemble + 8):
        planes[k * depth : (k + 1) * depth, :] = jnp.zeros((depth, LANES), f32)
    rows = ensemble + 8
    patches = tall_high.shape[0] // (2 * ensemble)
    for i in range(depth):
        at = slice(i * LANES, (i + 1) * LANES)
        tile = planes[pl.ds(i, rows, stride=depth), :]
        high, low = halves(tile)
        wide[0:rows, at] = high
        wide[rows : 2 * rows, at] = low
        scale(tile[0:ensemble, :], weights, tall_high, tall_low, at, patches)
    found = products(wide, tall_high, tall_low)
    odd = lax.rem(lax.axis_index("tile"), 2) == 1
    count = len(found) // 2
    for i in range(count):
        at = slice(i * LANES, (i + 1) * LANES)
        for_south, for_north = found[i], found[count + i]
        to_first[:, at] = jnp.where(odd, for_south, for_north)
        to_second[:, at] = jnp.where(odd, for_north, for_south)


def own_body(
    mine, theirs, weights, wide, own, centred, tall_high, tall_low, *, sources, members, region_rows
):
    _, chip, core = place()
    each = 2 * mine.shape[0] // sources
    ensemble = sources * members
    hits = region_rows // members
    total = jnp.zeros((hits, LANES), f32)
    for s in range(sources):
        source, row = (mine, theirs)[s % 2], s // 2 * each
        device = 2 * (chip ^ turn(s // 2, sources // 2)) + (core ^ (s % 2))
        part = source[row : row + region_rows, :].astype(f32)
        for b in range(members):
            one = part[b * hits : (b + 1) * hits, :]
            centred[device * members + b] = one
            total += one
    mean = total / ensemble
    for k in range(ensemble):
        centred[k] -= mean
    rows = ensemble + 8
    for i in range(0, wide.shape[1], LANES):
        at = slice(i, i + LANES)
        spread = wide[0:ensemble, at].astype(f32) + wide[rows : rows + ensemble, at].astype(f32)
        scale(spread, weights, tall_high, tall_low, at, 0)
    for i, piece in enumerate(products(wide, tall_high, tall_low)):
        own[:, i * LANES : (i + 1) * LANES] = piece


def analysis_body(own, first, second, centred, *refs, patches, sources, members, region_rows):
    chunks, factors = refs[:-1], refs[-1]
    _, chip, _ = place()
    ensemble = sources * members
    hits = region_rows // members
    count = patches * ensemble // 64
    group = 64 // ensemble
    row = iota((ensemble + 8, LANES), 0)
    lane = iota((ensemble + 8, LANES), 1)
    within = lane & (ensemble - 1)
    start = jnp.where(
        (row == within) & (row < ensemble), jnp.where(lane < 64, ensemble - 1.0, 1.0), 0.0
    )
    lane8 = iota((BLOCK, LANES), 1)
    group_start = (lane8 & 63) & ~(ensemble - 1)
    transforms = []
    for i in range(count):
        at = slice(i * LANES, (i + 1) * LANES)
        state = own[:, at] + first[:, at] + second[:, at] + start
        columns = [pick_lanes(state, group_start + k) for k in range(ensemble)]
        pivots = jnp.ones((ensemble, LANES), f32)
        for k in range(ensemble):
            pivot = columns[k][k : k + 1, :]
            factor = jnp.where(row > k, columns[k], 0.0) / pivot
            for j in range(k + 1, ensemble):
                columns[j] = columns[j] - factor * columns[j][k : k + 1, :]
            state = state - factor * state[k : k + 1, :]
            pivots = jnp.where(row[0:ensemble] == k, pivot, pivots)
        inverse = state[0:ensemble, :] * lax.rsqrt(pivots)
        mean_weight = -state[ensemble : ensemble + 1, :]
        unit = jnp.where(row[0:ensemble] == within[0:ensemble], 1.0, 0.0)
        transforms.append(mean_weight + (ensemble - 1.0) ** 0.5 * inverse - unit)

    side_lanes = 32
    patch = (lane8 // (2 * side_lanes)) * 2 + (lane8 & (side_lanes - 1)) // PATCH
    inside = 64 + (patch & (group - 1)) * ensemble if group > 1 else 64 + 0 * patch
    which = patch // group
    for j in range(ensemble):
        chosen = pick_lanes(transforms[0], inside + j)
        for i in range(1, count):
            other = pick_lanes(transforms[i], inside + j)
            chosen = jnp.where(jnp.broadcast_to(which[0:1] == i, chosen.shape), other, chosen)
        factors[j] = chosen

    for s, chunk in enumerate(chunks):
        for c in (0, 1):
            first_member = (2 * (chip ^ turn(s, len(chunks))) + c) * members
            totals = [jnp.zeros((hits, LANES), f32) for _ in range(members)]
            for j in range(ensemble):
                centred_j = centred[j]
                for b in range(members):
                    totals[b] += factors[j, pl.ds(first_member + b, 1), :] * centred_j
            at = slice(c * region_rows, (c + 1) * region_rows)
            chunk[at, :] = jnp.concatenate(totals, axis=0).astype(bf16)


def output_body(forecast, mine, theirs, analysis, ordered):
    members, levels, side, width = forecast.shape
    _, chip, core = place()
    rows = ordered.shape[1]
    chips = mine.shape[0] // rows
    for s in range(chips):
        at = slice(s * rows, (s + 1) * rows)
        source = 2 * (chip ^ turn(s, chips))
        ordered[source + core] = mine[at, :].astype(f32)
        ordered[source + (core ^ 1)] = theirs[at, :].astype(f32)
    for q in range(width // LANES):
        parts = [ordered[4 * q + c] for c in range(4)]
        at = slice(q * LANES, (q + 1) * LANES)
        for r, part in enumerate(transpose_chunks(parts)):
            rows = slice(r * BLOCK, (r + 1) * BLOCK)
            analysis[:, :, rows, at] = forecast[:, :, rows, at] + part.reshape(
                members, levels, BLOCK, LANES
            )


def shards(member_concentration, courant_pairs, obs_cell, obs_value, obs_error, obs_list):
    members, levels, side, width = member_concentration.shape
    blocks = lax.axis_size("member")
    tiles = lax.axis_size("tile")
    height = side * tiles
    ensemble = members * blocks
    per_side = side // PATCH
    patches = per_side * per_side
    slots = obs_list.shape[2]
    region_rows = members * levels * BLOCK
    depth = 3 * BLOCK
    all_rows = region_rows + members * depth
    chips = blocks // 2
    chip_rows = 2 * region_rows + members * 4 * BLOCK
    edge_rows = -(-(24 + patches * slots // width) // 8) * 8
    edge_shape = (members, levels, BLOCK, width)
    rate_shape = (2, levels, BLOCK, width)

    to_first, to_second = call(
        pack_edges,
        [((edge_rows, width), f32)] * 2,
        [
            pltpu.VMEM(edge_shape, f32),
            pltpu.VMEM(edge_shape, f32),
            pltpu.VMEM(rate_shape, f32),
            pltpu.VMEM(rate_shape, f32),
            pltpu.VMEM(obs_list.shape, jnp.int32),
            pltpu.SemaphoreType.DMA((5,)),
        ],
        specs=[pl.BlockSpec(memory_space=pltpu.HBM)] * 3,
        vmem=63,
    )(member_concentration, courant_pairs, obs_list)
    first, second = swap(to_first, to_second, tiles, 1)

    whole = pl.BlockSpec(memory_space=pltpu.VMEM)
    flat = lambda array: array.reshape(-1, LANES)
    cell = flat(obs_cell)
    cell_row = lax.dynamic_index_in_dim(
        cell.reshape(blocks, tiles, BLOCK, LANES), lax.axis_index("tile"), 1, False
    )
    draft, seen = call(
        functools.partial(draft_body, height=height),
        [(member_concentration.shape, f32), ((blocks, members, BLOCK, LANES), f32)],
        [pltpu.VMEM((blocks, region_rows, LANES), f32)],
        flops=50_000_000,
        specs=[whole, whole, whole, pl.BlockSpec(memory_space=pltpu.HBM)],
    )(member_concentration, courant_pairs, cell_row, to_second)
    forecast, *chunks = call(
        functools.partial(forecast_body, tiles=tiles, height=height),
        [(member_concentration.shape, f32)] + [((chip_rows, LANES), bf16)] * chips,
        [
            pltpu.VMEM((chips, chip_rows, LANES), bf16),
            pltpu.VMEM((blocks, region_rows, LANES), f32),
        ],
    )(
        member_concentration,
        courant_pairs,
        draft,
        seen,
        first,
        second,
        cell_row,
    )
    received = exchange(chunks)
    weights, values = call(
        functools.partial(
            weights_body, tiles=tiles, blocks=blocks, height=height, width=width, side=side
        ),
        [((16, depth * LANES), f32), ((depth, LANES), f32)],
        [pltpu.VMEM((16 * depth, LANES), f32)],
        flops=100_000_000,
    )(obs_list, first, second, cell, flat(obs_value), flat(obs_error))

    sizes = dict(sources=blocks, members=members, region_rows=region_rows)
    tall = patches * ensemble
    length = depth * LANES
    system_shape = (ensemble + 8, tall // 64 * LANES)
    wide_shape = (2 * (ensemble + 8), length)
    centred_shape = (ensemble, levels * BLOCK, LANES)
    share = functools.partial(share_body, region_rows=region_rows)
    mine, theirs = call(share, [((chips * all_rows, LANES), bf16)] * 2)(*received, values)
    theirs = swap_cores(theirs)
    to_first, to_second, wide = call(
        functools.partial(neighbours_body, **sizes),
        [(system_shape, f32), (system_shape, f32), (wide_shape, bf16)],
        [
            pltpu.VMEM(((ensemble + 8) * depth, LANES), f32),
            pltpu.VMEM((2 * tall, length), bf16),
            pltpu.VMEM((2 * tall, length), bf16),
        ],
    )(mine, theirs, weights, values)
    first, second = swap(to_first, to_second, tiles, 0)
    own, centred = call(
        functools.partial(own_body, **sizes),
        [(system_shape, f32), (centred_shape, f32)],
        [pltpu.VMEM((tall, length), bf16), pltpu.VMEM((tall, length), bf16)],
        flops=50_000_000,
    )(mine, theirs, weights, wide)

    changes = call(
        functools.partial(analysis_body, patches=patches, **sizes),
        [((2 * region_rows, LANES), bf16)] * chips,
        [pltpu.VMEM((ensemble, ensemble, LANES), f32)],
    )(own, first, second, centred)
    returned = exchange(changes)
    mine, theirs = call(share, [((chips * region_rows, LANES), bf16)] * 2)(*returned, forecast)
    theirs = swap_cores(theirs)
    (analysis,) = call(
        output_body, [(forecast.shape, f32)], [pltpu.VMEM((blocks, region_rows, LANES), f32)]
    )(forecast, mine, theirs)
    return analysis


def solution(mesh):
    return jax.shard_map(
        shards,
        mesh=mesh,
        in_specs=(
            P("member", None, "tile", None),
            P(None, None, "tile", None),
            P(),
            P(),
            P(),
            P("tile", "member", None),
        ),
        out_specs=P("member", None, "tile", None),
        check_vma=False,
    )
```

```python
import functools

import jax
import jax.numpy as jnp
from jax import lax
from jax.experimental import pallas as pl
from jax.experimental.pallas import tpu as pltpu
from jax.sharding import PartitionSpec as P

PATCH = 16
LOC_LEN = 16
DIFFUSION = 0.05
LANES = 128
BLOCK = 8

f32 = jnp.float32
bf16 = jnp.bfloat16


def call(body, outs, scratch=(), flops=1_000_000, moved=1_000_000, specs=None, vmem=48):
    specs = {} if specs is None else {"in_specs": specs}
    return pl.pallas_call(
        body,
        **specs,
        out_shape=[jax.ShapeDtypeStruct(shape, kind) for shape, kind in outs],
        scratch_shapes=list(scratch),
        compiler_params=pltpu.CompilerParams(vmem_limit_bytes=vmem * 1024 * 1024),
        cost_estimate=pl.CostEstimate(flops=flops, bytes_accessed=moved, transcendentals=0),
    )


def split(number, size):
    if size & (size - 1) == 0:
        return number >> (size.bit_length() - 1), number & (size - 1)
    quotient = number // size
    return quotient, number - quotient * size


def wrapped(number, size):
    if size & (size - 1) == 0:
        return number & (size - 1)
    return lax.rem(number + size, size)


def iota(shape, axis):
    return lax.broadcasted_iota(jnp.int32, shape, axis)


def pick_lanes(values, index):
    rows = [
        jnp.take_along_axis(values[r : r + BLOCK], index, axis=1, mode="promise_in_bounds")
        for r in range(0, values.shape[0], BLOCK)
    ]
    return rows[0] if len(rows) == 1 else jnp.concatenate(rows, axis=0)


def transpose_chunks(parts):
    lane = iota(parts[0].shape, 1)
    low = lane < 64
    even = (lane & 32) == 0
    parts = list(parts)
    for i in (0, 1):
        a, b = parts[i], parts[i + 2]
        parts[i] = jnp.where(low, a, pltpu.roll(b, 64, 1))
        parts[i + 2] = jnp.where(low, pltpu.roll(a, 64, 1), b)
    for i in (0, 2):
        a, b = parts[i], parts[i + 1]
        parts[i] = jnp.where(even, a, pltpu.roll(b, 32, 1))
        parts[i + 1] = jnp.where(even, pltpu.roll(a, 96, 1), b)
    return parts


def pack_edges(
    tracer, courant, lists, to_first, to_second, first, last, first_rates, last_rates, numbers, arrived
):
    members, levels, side, width = tracer.shape
    copies = [
        pltpu.make_async_copy(source, target, arrived.at[i])
        for i, (source, target) in enumerate(
            (
                (tracer.at[:, :, 0:BLOCK, :], first),
                (tracer.at[:, :, side - BLOCK : side, :], last),
                (courant.at[:, :, 0:BLOCK, :], first_rates),
                (courant.at[:, :, side - BLOCK : side, :], last_rates),
                (lists, numbers),
            )
        )
    ]
    for copy in copies:
        copy.start()
    for copy in copies:
        copy.wait()
    even = lax.rem(lax.axis_index("tile"), 2) == 0

    def put(row, low, high):
        to_first[row : row + 1, :] = jnp.where(even, high, low)
        to_second[row : row + 1, :] = jnp.where(even, low, high)

    end = BLOCK - 1
    for b in range(members):
        for l in range(levels):
            row = b * levels + l
            put(row, first[b, l, 0:1, :], last[b, l, end : end + 1, :])
            put(8 + row, first[b, l, 1:2, :], last[b, l, end - 1 : end, :])
    for c in range(2):
        for l in range(levels):
            put(16 + c * levels + l, first_rates[c, l, 0:1, :], last_rates[c, l, end : end + 1, :])
    row = 24
    for a in range(numbers.shape[0]):
        for b in range(numbers.shape[1]):
            for s in range(0, numbers.shape[2], width):
                part = numbers[a, b : b + 1, s : s + width].astype(f32)
                to_first[row : row + 1, :] = part
                to_second[row : row + 1, :] = part
                row += 1


def coefficients(meridional, zonal):
    return (
        (1.0 - 4.0 * DIFFUSION) - jnp.abs(zonal) - jnp.abs(meridional),
        DIFFUSION + jnp.maximum(zonal, 0.0),
        DIFFUSION - jnp.minimum(zonal, 0.0),
        DIFFUSION + jnp.maximum(meridional, 0.0),
        DIFFUSION - jnp.minimum(meridional, 0.0),
    )


def stencil(current, south, north, factors):
    width = current.shape[1]
    centre, from_west, from_east, from_south, from_north = factors
    west = pltpu.roll(current, 1, 1)
    east = pltpu.roll(current, width - 1, 1)
    return (
        centre * current
        + from_west * west
        + from_east * east
        + from_south * south
        + from_north * north
    )


def beside(first, second, tile):
    even = lax.rem(tile, 2) == 0
    return jnp.where(even, second, first), jnp.where(even, first, second)


def swap(first, second, tiles):
    pairs = lambda start: [
        pair for i in range(start, tiles - 1, 2) for pair in ((i, i + 1), (i + 1, i))
    ]
    return lax.ppermute(first, "tile", pairs(0)), lax.ppermute(second, "tile", pairs(1))


def turn(s, chips):
    return (chips - s) % chips


def exchange(chunks):
    chips = len(chunks)
    device = lambda chip, core: 2 * chip + core
    swaps = lambda s: [
        (device(i, c), device(i ^ turn(s, chips), c)) for i in range(chips) for c in (0, 1)
    ]
    return [chunks[0]] + [lax.ppermute(chunks[s], "member", swaps(s)) for s in range(1, chips)]


def gather_body(*refs, places, outputs):
    inputs, targets = refs[:-outputs], refs[-outputs:]
    for target, parts in zip(targets, places):
        rows = target.shape[0] // len(parts)
        for i, (source, at) in enumerate(parts):
            target[i * rows : (i + 1) * rows, :] = inputs[source][at * rows : (at + 1) * rows, :]


def regroup(slots, groups):
    arrays = []
    for group in groups:
        for array, _ in (slots[d] for d in group):
            if not any(array is other for other in arrays):
                arrays.append(array)
    find = lambda array: [array is other for other in arrays].index(True)
    places = [[(find(slots[d][0]), slots[d][1]) for d in group] for group in groups]
    rows = slots[0][0].shape[0]
    return call(
        functools.partial(gather_body, places=places, outputs=len(groups)),
        [((rows * len(group), LANES), bf16) for group in groups],
    )(*arrays)


def exchange_by_bits(chunks):
    chips = len(chunks)
    slots = {turn(s, chips): (chunk, 0) for s, chunk in enumerate(chunks)}
    bit = 1
    while bit < chips:
        moving = [d for d in range(chips) if d & bit]
        (packed,) = regroup(slots, [moving])
        pairs = [(i, i ^ (2 * bit)) for i in range(2 * chips)]
        arrived = lax.ppermute(packed, "member", pairs)
        for i, d in enumerate(moving):
            slots[d] = (arrived, i)
        bit *= 2
    return regroup(slots, [[turn(s, chips)] for s in range(chips)])


def swap_cores(array):
    return lax.ppermute(array, "member", [(i, i ^ 1) for i in range(lax.axis_size("member"))])


def place():
    block = lax.axis_index("member")
    core = lax.rem(block, 2)
    return block, (block - core) // 2, core


def share_body(*refs, region_rows):
    chunks, (own, other) = refs[:-3], refs[-2:]
    _, _, core = place()
    first = core == 0
    each = own.shape[0] // len(chunks)
    half = chunks[0].shape[0] - 2 * region_rows
    lines = half // 2
    for s, chunk in enumerate(chunks):
        low, high = chunk[0:region_rows, :], chunk[region_rows : 2 * region_rows, :]
        row = s * each
        own[row : row + region_rows, :] = jnp.where(first, low, high)
        other[row : row + region_rows, :] = jnp.where(first, high, low)
        if each == region_rows:
            continue
        seen = chunk[2 * region_rows :, :].astype(f32)
        west = jnp.concatenate([seen[0 : lines - 8], seen[lines : 2 * lines - 8]], axis=0)
        east = jnp.concatenate([seen[8:lines], seen[lines + 8 : 2 * lines]], axis=0)
        own[row + region_rows : row + each, :] = jnp.where(first, west, east).astype(bf16)
        other[row + region_rows : row + each, :] = jnp.where(first, east, west).astype(bf16)


def pack(forecast):
    members, levels, side, width = forecast.shape
    for q in range(width // LANES):
        parts = [
            forecast[:, :, r : r + BLOCK, q * LANES : (q + 1) * LANES].reshape(-1, LANES)
            for r in range(0, side, BLOCK)
        ]
        for i, part in enumerate(transpose_chunks(parts)):
            yield 4 * q + i, part.astype(bf16)


def observe(cell, table, observed, rows, levels, side, width, height):
    members = len(observed[0])
    hits = levels * BLOCK
    for c in range(cell.shape[0]):
        above_row, column = split(cell[c], width)
        level, grid_row = split(above_row, height)
        _, local_row = split(grid_row, side)
        _, local_column = split(column, side)
        band, sub_row = split(local_row, BLOCK)
        high = level * BLOCK + sub_row
        low = band * side + local_column
        for h in [l * BLOCK + r for l in range(levels) for r in rows]:
            here = high == h
            for b in range(members):
                line = table[c, b * hits + h : b * hits + h + 1, :]
                line = jnp.broadcast_to(line, (BLOCK, LANES))
                observed[c][b] = jnp.where(here, pick_lanes(line, low), observed[c][b])


def draft_body(tracer, courant, cell, _, forecast, seen, table, *, height):
    members, levels, side, width = tracer.shape
    for l in range(levels):
        factors = coefficients(courant[0, l], courant[1, l])
        for b in range(members):
            current = tracer[b, l]
            for step in range(2):
                lower = pltpu.roll(current, 1, 0)
                upper = pltpu.roll(current, side - 1, 0)
                current = stencil(current, lower, upper, factors)
            forecast[b, l] = current
    for c, rounded in pack(forecast):
        table[c] = rounded.astype(f32)
    blocks = cell.shape[0]
    observed = [[jnp.zeros((BLOCK, LANES), f32) for _ in range(members)] for _ in range(blocks)]
    observe(cell, table, observed, range(BLOCK), levels, side, width, height)
    for c in range(blocks):
        for b in range(members):
            seen[c, b] = observed[c][b]


def forecast_body(
    tracer, courant, draft, seen, first, second, cell, forecast, *rest, tiles, height
):
    *chunks, send, table = rest
    members, levels, side, width = tracer.shape
    blocks = width // side
    tile = lax.axis_index("tile")
    planes = members * levels
    region_rows = planes * BLOCK
    south, north = beside(first[0:24, :], second[0:24, :], tile)
    own = lambda at: jnp.concatenate(
        [tracer[b, l, at : at + 1, :] for b in range(members) for l in range(levels)], axis=0
    )
    rates = lambda part, at: jnp.concatenate(
        [courant[part, l, at : at + 1, :] for l in range(levels)] * members, axis=0
    )
    here = lambda at: coefficients(rates(0, at), rates(1, at))

    def there(source):
        twice = lambda at: jnp.concatenate([source[at : at + levels]] * members, axis=0)
        return coefficients(twice(16), twice(16 + levels))

    forecast[...] = draft[...]
    for other, inside, at, toward in (
        (south, tile > 0, 0, 1),
        (north, tile < tiles - 1, side - 1, -1),
    ):
        order = lambda outer, inner: (outer, inner) if toward == 1 else (inner, outer)
        rows = [own(at + toward * i) for i in range(4)]
        factors = [here(at + toward * i) for i in range(3)]
        near, far = other[0:planes], other[8 : 8 + planes]
        outside = jnp.where(inside, stencil(near, *order(far, rows[0]), there(other)), 0.0)
        outer = [near, rows[0], rows[1]]
        once = [stencil(rows[i], *order(outer[i], rows[i + 1]), factors[i]) for i in range(3)]
        final = (
            stencil(once[0], *order(outside, once[1]), factors[0]),
            stencil(once[1], *order(once[0], once[2]), factors[1]),
        )
        for i, values in enumerate(final):
            row = at + toward * i
            for b in range(members):
                for l in range(levels):
                    plane = b * levels + l
                    forecast[b, l, row : row + 1, :] = values[plane : plane + 1, :]

    for c, rounded in pack(forecast):
        send[c // 2, c % 2 * region_rows : (c % 2 + 1) * region_rows, :] = rounded
        table[c] = rounded.astype(f32)
    observed = [[seen[c, b] for b in range(members)] for c in range(blocks)]
    edge = (0, 1, BLOCK - 2, BLOCK - 1)
    observe(cell, table, observed, edge, levels, side, width, height)
    for chip in range(blocks // 2):
        lines = [
            observed[(2 * chip + r - 1) % blocks][b] for b in range(members) for r in range(4)
        ]
        for i in range(0, len(lines), 2):
            at = 2 * region_rows + i * BLOCK
            send[chip, at : at + 2 * BLOCK, :] = jnp.concatenate(lines[i : i + 2], axis=0).astype(
                bf16
            )
    _, chip, _ = place()
    for s, chunk in enumerate(chunks):
        chunk[...] = send[chip ^ turn(s, len(chunks))]


def weights_body(
    lists, first, second, cell, value, variance, weights, values, planes, *, tiles, blocks, height, width, side
):
    tile = lax.axis_index("tile")
    block = lax.axis_index("member")
    own_lists = slice(24, 24 + lists.shape[0] * lists.shape[1] * lists.shape[2] // width)
    south, north = beside(first[own_lists, :], second[own_lists, :], tile)
    per_side = side // PATCH
    patches = per_side * per_side
    slots = lists.shape[2]
    depth = 3 * BLOCK
    rows, columns, sizes = [], [], []
    for r in range(3):
        column_block = wrapped(block + (r - 1), blocks)
        first = pl.multiple_of((column_block * tiles + tile) * BLOCK, BLOCK)
        cells = cell[pl.ds(first, BLOCK), :]
        above_row, column = split(cells, width)
        _, grid_row = split(above_row, height)
        rows.append(grid_row)
        columns.append(column)
        sizes.append(variance[pl.ds(first, BLOCK), :])
        values[r * BLOCK : (r + 1) * BLOCK, :] = value[pl.ds(first, BLOCK), :]
    grid_row = jnp.concatenate(rows, axis=0)
    column = jnp.concatenate(columns, axis=0)
    size = jnp.concatenate(sizes, axis=0)

    def pieces(dt, p):
        if dt == 0:
            return [lists[p // per_side, p % per_side : p % per_side + 1, :]]
        source = south if dt < 0 else north
        each = slots // width
        return [
            source[p * each + i : p * each + i + 1].astype(jnp.int32) for i in range(each)
        ]

    index = 0
    for dt in (0, -1, 1):
        for p in range(patches):
            count = jnp.zeros((depth, LANES), f32)
            for part in pieces(dt, p):
                length = part.shape[1]
                region, within = split(part, BLOCK * LANES)
                region_column, region_row = split(region, tiles)
                line, lane = split(within, LANES)
                near = wrapped(region_column - block + 1, blocks)
                fits = (part >= 0) & (region_row == tile) & (near < 3)
                line = jnp.where(fits, near * BLOCK + line, -1)
                one = (iota((depth, length), 0) == line).astype(f32).astype(bf16)
                other = (iota((LANES, length), 0) == lane).astype(f32).astype(bf16)
                count += lax.dot_general(
                    one, other, (((1,), (1,)), ((), ())), preferred_element_type=f32
                )
            patch_row = (tile + dt) * per_side + p // per_side
            patch_column = block * per_side + p % per_side
            row_gap = (grid_row - patch_row * PATCH - PATCH // 2).astype(f32) + 0.5
            turned = column - patch_column * PATCH - PATCH // 2 + width // 2
            column_gap = (wrapped(turned, width) - width // 2).astype(f32) + 0.5
            near = jnp.exp(
                -(row_gap * row_gap + column_gap * column_gap) / (2.0 * LOC_LEN * LOC_LEN)
            )
            planes[index * depth : (index + 1) * depth, :] = count * (near / size)
            index += 1
    for extra in range(index, 16):
        planes[extra * depth : (extra + 1) * depth, :] = jnp.zeros((depth, LANES), f32)
    for i in range(depth):
        weights[:, i * LANES : (i + 1) * LANES] = planes[pl.ds(i, 16, stride=depth), :]


def halves(values):
    high = values.astype(bf16)
    return high, (values - high.astype(f32)).astype(bf16)


def dot_rows(left, right):
    return lax.dot_general(left, right, (((1,), (1,)), ((), ())), preferred_element_type=f32)


def scale(spread, weights, tall_high, tall_low, at, first):
    ensemble = spread.shape[0]
    for p in range(tall_high.shape[0] // ensemble):
        high, low = halves(spread * weights[first + p : first + p + 1, at])
        tall_high[p * ensemble : (p + 1) * ensemble, at] = high
        tall_low[p * ensemble : (p + 1) * ensemble, at] = low


def products(wide, tall_high, tall_low):
    rows = wide.shape[0] // 2
    both = dot_rows(wide[...], tall_high[...])
    result = both[0:rows] + both[rows:] + dot_rows(wide[0:rows, :], tall_low[...])
    count = result.shape[1] // 64
    if count % 2:
        result = jnp.concatenate([result, jnp.zeros((rows, 64), f32)], axis=1)
    found = []
    for n in range(count):
        piece = result[:, n // 2 * LANES : (n // 2 + 1) * LANES]
        if n % 2:
            piece = pltpu.roll(piece, 64, 1)
        found.append(jnp.where(iota(piece.shape, 1) < 64, piece, 0.0))
    return found


def neighbours_body(
    mine, theirs, weights, values, to_first, to_second, wide, planes, tall_high, tall_low, *, sources, members, region_rows
):
    depth = 3 * BLOCK
    each = 2 * mine.shape[0] // sources
    _, chip, core = place()
    ensemble = sources * members
    total = jnp.zeros((depth, LANES), f32)
    for s in range(sources):
        source, row = (mine, theirs)[s % 2], s // 2 * each
        both = source[row + region_rows : row + each, :].astype(f32)
        device = 2 * (chip ^ turn(s // 2, sources // 2)) + (core ^ (s % 2))
        at = pl.multiple_of(device * (members * depth), BLOCK)
        planes[pl.ds(at, members * depth), :] = both
        for b in range(members):
            total += both[b * depth : (b + 1) * depth, :]
    mean = total / ensemble
    for k in range(ensemble):
        planes[k * depth : (k + 1) * depth, :] -= mean
    planes[ensemble * depth : (ensemble + 1) * depth, :] = values[...] - mean
    for k in range(ensemble + 1, ensemble + 8):
        planes[k * depth : (k + 1) * depth, :] = jnp.zeros((depth, LANES), f32)
    rows = ensemble + 8
    patches = tall_high.shape[0] // (2 * ensemble)
    for i in range(depth):
        at = slice(i * LANES, (i + 1) * LANES)
        tile = planes[pl.ds(i, rows, stride=depth), :]
        high, low = halves(tile)
        wide[0:rows, at] = high
        wide[rows : 2 * rows, at] = low
        scale(tile[0:ensemble, :], weights, tall_high, tall_low, at, patches)
    found = products(wide, tall_high, tall_low)
    odd = lax.rem(lax.axis_index("tile"), 2) == 1
    count = len(found) // 2
    for i in range(count):
        at = slice(i * LANES, (i + 1) * LANES)
        for_south, for_north = found[i], found[count + i]
        to_first[:, at] = jnp.where(odd, for_south, for_north)
        to_second[:, at] = jnp.where(odd, for_north, for_south)


def own_body(
    mine, theirs, weights, wide, own, centred, tall_high, tall_low, *, sources, members, region_rows
):
    _, chip, core = place()
    each = 2 * mine.shape[0] // sources
    ensemble = sources * members
    hits = region_rows // members
    total = jnp.zeros((hits, LANES), f32)
    for s in range(sources):
        source, row = (mine, theirs)[s % 2], s // 2 * each
        device = 2 * (chip ^ turn(s // 2, sources // 2)) + (core ^ (s % 2))
        part = source[row : row + region_rows, :].astype(f32)
        for b in range(members):
            one = part[b * hits : (b + 1) * hits, :]
            centred[device * members + b] = one
            total += one
    mean = total / ensemble
    for k in range(ensemble):
        centred[k] -= mean
    rows = ensemble + 8
    for i in range(0, wide.shape[1], LANES):
        at = slice(i, i + LANES)
        spread = wide[0:ensemble, at].astype(f32) + wide[rows : rows + ensemble, at].astype(f32)
        scale(spread, weights, tall_high, tall_low, at, 0)
    for i, piece in enumerate(products(wide, tall_high, tall_low)):
        own[:, i * LANES : (i + 1) * LANES] = piece


def analysis_body(own, first, second, centred, *refs, patches, sources, members, region_rows):
    chunks, factors = refs[:-1], refs[-1]
    _, chip, _ = place()
    ensemble = sources * members
    hits = region_rows // members
    count = patches * ensemble // 64
    group = 64 // ensemble
    row = iota((ensemble + 8, LANES), 0)
    lane = iota((ensemble + 8, LANES), 1)
    within = lane & (ensemble - 1)
    start = jnp.where(
        (row == within) & (row < ensemble), jnp.where(lane < 64, ensemble - 1.0, 1.0), 0.0
    )
    lane8 = iota((BLOCK, LANES), 1)
    group_start = (lane8 & 63) & ~(ensemble - 1)
    transforms = []
    for i in range(count):
        at = slice(i * LANES, (i + 1) * LANES)
        state = own[:, at] + first[:, at] + second[:, at] + start
        columns = [pick_lanes(state, group_start + k) for k in range(ensemble)]
        pivots = jnp.ones((ensemble, LANES), f32)
        for k in range(ensemble):
            pivot = columns[k][k : k + 1, :]
            factor = jnp.where(row > k, columns[k], 0.0) / pivot
            for j in range(k + 1, ensemble):
                columns[j] = columns[j] - factor * columns[j][k : k + 1, :]
            state = state - factor * state[k : k + 1, :]
            pivots = jnp.where(row[0:ensemble] == k, pivot, pivots)
        inverse = state[0:ensemble, :] * lax.rsqrt(pivots)
        mean_weight = -state[ensemble : ensemble + 1, :]
        unit = jnp.where(row[0:ensemble] == within[0:ensemble], 1.0, 0.0)
        transforms.append(mean_weight + (ensemble - 1.0) ** 0.5 * inverse - unit)

    side_lanes = 32
    patch = (lane8 // (2 * side_lanes)) * 2 + (lane8 & (side_lanes - 1)) // PATCH
    inside = 64 + (patch & (group - 1)) * ensemble if group > 1 else 64 + 0 * patch
    which = patch // group
    for j in range(ensemble):
        chosen = pick_lanes(transforms[0], inside + j)
        for i in range(1, count):
            other = pick_lanes(transforms[i], inside + j)
            chosen = jnp.where(jnp.broadcast_to(which[0:1] == i, chosen.shape), other, chosen)
        factors[j] = chosen

    for s, chunk in enumerate(chunks):
        for c in (0, 1):
            first_member = (2 * (chip ^ turn(s, len(chunks))) + c) * members
            totals = [jnp.zeros((hits, LANES), f32) for _ in range(members)]
            for j in range(ensemble):
                centred_j = centred[j]
                for b in range(members):
                    totals[b] += factors[j, pl.ds(first_member + b, 1), :] * centred_j
            at = slice(c * region_rows, (c + 1) * region_rows)
            chunk[at, :] = jnp.concatenate(totals, axis=0).astype(bf16)


def output_body(forecast, mine, theirs, analysis, ordered):
    members, levels, side, width = forecast.shape
    _, chip, core = place()
    rows = ordered.shape[1]
    chips = mine.shape[0] // rows
    for s in range(chips):
        at = slice(s * rows, (s + 1) * rows)
        source = 2 * (chip ^ turn(s, chips))
        ordered[source + core] = mine[at, :].astype(f32)
        ordered[source + (core ^ 1)] = theirs[at, :].astype(f32)
    for q in range(width // LANES):
        parts = [ordered[4 * q + c] for c in range(4)]
        at = slice(q * LANES, (q + 1) * LANES)
        for r, part in enumerate(transpose_chunks(parts)):
            rows = slice(r * BLOCK, (r + 1) * BLOCK)
            analysis[:, :, rows, at] = forecast[:, :, rows, at] + part.reshape(
                members, levels, BLOCK, LANES
            )


def shards(member_concentration, courant_pairs, obs_cell, obs_value, obs_error, obs_list):
    members, levels, side, width = member_concentration.shape
    blocks = lax.axis_size("member")
    tiles = lax.axis_size("tile")
    height = side * tiles
    ensemble = members * blocks
    per_side = side // PATCH
    patches = per_side * per_side
    slots = obs_list.shape[2]
    region_rows = members * levels * BLOCK
    depth = 3 * BLOCK
    all_rows = region_rows + members * depth
    chips = blocks // 2
    chip_rows = 2 * region_rows + members * 4 * BLOCK
    edge_rows = -(-(24 + patches * slots // width) // 8) * 8
    edge_shape = (members, levels, BLOCK, width)
    rate_shape = (2, levels, BLOCK, width)

    to_first, to_second = call(
        pack_edges,
        [((edge_rows, width), f32)] * 2,
        [
            pltpu.VMEM(edge_shape, f32),
            pltpu.VMEM(edge_shape, f32),
            pltpu.VMEM(rate_shape, f32),
            pltpu.VMEM(rate_shape, f32),
            pltpu.VMEM(obs_list.shape, jnp.int32),
            pltpu.SemaphoreType.DMA((5,)),
        ],
        specs=[pl.BlockSpec(memory_space=pltpu.HBM)] * 3,
        vmem=63,
    )(member_concentration, courant_pairs, obs_list)
    first, second = swap(to_first, to_second, tiles)

    whole = pl.BlockSpec(memory_space=pltpu.VMEM)
    flat = lambda array: array.reshape(-1, LANES)
    cell = flat(obs_cell)
    cell_row = lax.dynamic_index_in_dim(
        cell.reshape(blocks, tiles, BLOCK, LANES), lax.axis_index("tile"), 1, False
    )
    draft, seen = call(
        functools.partial(draft_body, height=height),
        [(member_concentration.shape, f32), ((blocks, members, BLOCK, LANES), f32)],
        [pltpu.VMEM((blocks, region_rows, LANES), f32)],
        flops=50_000_000,
        specs=[whole, whole, whole, pl.BlockSpec(memory_space=pltpu.HBM)],
    )(member_concentration, courant_pairs, cell_row, to_second)
    forecast, *chunks = call(
        functools.partial(forecast_body, tiles=tiles, height=height),
        [(member_concentration.shape, f32)] + [((chip_rows, LANES), bf16)] * chips,
        [
            pltpu.VMEM((chips, chip_rows, LANES), bf16),
            pltpu.VMEM((blocks, region_rows, LANES), f32),
        ],
    )(
        member_concentration,
        courant_pairs,
        draft,
        seen,
        first,
        second,
        cell_row,
    )
    received = exchange(chunks)
    weights, values = call(
        functools.partial(
            weights_body, tiles=tiles, blocks=blocks, height=height, width=width, side=side
        ),
        [((16, depth * LANES), f32), ((depth, LANES), f32)],
        [pltpu.VMEM((16 * depth, LANES), f32)],
        flops=100_000_000,
    )(obs_list, first, second, cell, flat(obs_value), flat(obs_error))

    sizes = dict(sources=blocks, members=members, region_rows=region_rows)
    tall = patches * ensemble
    length = depth * LANES
    system_shape = (ensemble + 8, tall // 64 * LANES)
    wide_shape = (2 * (ensemble + 8), length)
    centred_shape = (ensemble, levels * BLOCK, LANES)
    share = functools.partial(share_body, region_rows=region_rows)
    mine, theirs = call(share, [((chips * all_rows, LANES), bf16)] * 2)(*received, values)
    theirs = swap_cores(theirs)
    to_first, to_second, wide = call(
        functools.partial(neighbours_body, **sizes),
        [(system_shape, f32), (system_shape, f32), (wide_shape, bf16)],
        [
            pltpu.VMEM(((ensemble + 8) * depth, LANES), f32),
            pltpu.VMEM((2 * tall, length), bf16),
            pltpu.VMEM((2 * tall, length), bf16),
        ],
    )(mine, theirs, weights, values)
    first, second = swap(to_first, to_second, tiles)
    own, centred = call(
        functools.partial(own_body, **sizes),
        [(system_shape, f32), (centred_shape, f32)],
        [pltpu.VMEM((tall, length), bf16), pltpu.VMEM((tall, length), bf16)],
        flops=50_000_000,
    )(mine, theirs, weights, wide)

    changes = call(
        functools.partial(analysis_body, patches=patches, **sizes),
        [((2 * region_rows, LANES), bf16)] * chips,
        [pltpu.VMEM((ensemble, ensemble, LANES), f32)],
    )(own, first, second, centred)
    returned = exchange_by_bits(changes)
    mine, theirs = call(share, [((chips * region_rows, LANES), bf16)] * 2)(*returned, forecast)
    theirs = swap_cores(theirs)
    (analysis,) = call(
        output_body, [(forecast.shape, f32)], [pltpu.VMEM((blocks, region_rows, LANES), f32)]
    )(forecast, mine, theirs)
    return analysis


def solution(mesh):
    return jax.shard_map(
        shards,
        mesh=mesh,
        in_specs=(
            P("member", None, "tile", None),
            P(None, None, "tile", None),
            P(),
            P(),
            P(),
            P("tile", "member", None),
        ),
        out_specs=P("member", None, "tile", None),
        check_vma=False,
    )
```

```python
import functools

import jax
import jax.numpy as jnp
from jax import lax
from jax.experimental import pallas as pl
from jax.experimental.pallas import tpu as pltpu
from jax.sharding import PartitionSpec as P

PATCH = 16
LOC_LEN = 16
DIFFUSION = 0.05
LANES = 128
BLOCK = 8

f32 = jnp.float32
bf16 = jnp.bfloat16


def call(body, outs, scratch=(), flops=1_000_000, moved=1_000_000, specs=None, vmem=48):
    specs = {} if specs is None else {"in_specs": specs}
    return pl.pallas_call(
        body,
        **specs,
        out_shape=[jax.ShapeDtypeStruct(shape, kind) for shape, kind in outs],
        scratch_shapes=list(scratch),
        compiler_params=pltpu.CompilerParams(vmem_limit_bytes=vmem * 1024 * 1024),
        cost_estimate=pl.CostEstimate(flops=flops, bytes_accessed=moved, transcendentals=0),
    )


def split(number, size):
    if size & (size - 1) == 0:
        return number >> (size.bit_length() - 1), number & (size - 1)
    quotient = number // size
    return quotient, number - quotient * size


def wrapped(number, size):
    if size & (size - 1) == 0:
        return number & (size - 1)
    return lax.rem(number + size, size)


def iota(shape, axis):
    return lax.broadcasted_iota(jnp.int32, shape, axis)


def pick_lanes(values, index):
    rows = [
        jnp.take_along_axis(values[r : r + BLOCK], index, axis=1, mode="promise_in_bounds")
        for r in range(0, values.shape[0], BLOCK)
    ]
    return rows[0] if len(rows) == 1 else jnp.concatenate(rows, axis=0)


def transpose_chunks(parts):
    lane = iota(parts[0].shape, 1)
    low = lane < 64
    even = (lane & 32) == 0
    parts = list(parts)
    for i in (0, 1):
        a, b = parts[i], parts[i + 2]
        parts[i] = jnp.where(low, a, pltpu.roll(b, 64, 1))
        parts[i + 2] = jnp.where(low, pltpu.roll(a, 64, 1), b)
    for i in (0, 2):
        a, b = parts[i], parts[i + 1]
        parts[i] = jnp.where(even, a, pltpu.roll(b, 32, 1))
        parts[i + 1] = jnp.where(even, pltpu.roll(a, 96, 1), b)
    return parts


def pack_edges(
    tracer, courant, lists, to_first, to_second, first, last, first_rates, last_rates, numbers, arrived
):
    members, levels, side, width = tracer.shape
    copies = [
        pltpu.make_async_copy(source, target, arrived.at[i])
        for i, (source, target) in enumerate(
            (
                (tracer.at[:, :, 0:BLOCK, :], first),
                (tracer.at[:, :, side - BLOCK : side, :], last),
                (courant.at[:, :, 0:BLOCK, :], first_rates),
                (courant.at[:, :, side - BLOCK : side, :], last_rates),
                (lists, numbers),
            )
        )
    ]
    for copy in copies:
        copy.start()
    for copy in copies:
        copy.wait()
    even = lax.rem(lax.axis_index("tile"), 2) == 0

    def put(row, low, high):
        to_first[row : row + 1, :] = jnp.where(even, high, low)
        to_second[row : row + 1, :] = jnp.where(even, low, high)

    end = BLOCK - 1
    for b in range(members):
        for l in range(levels):
            row = b * levels + l
            put(row, first[b, l, 0:1, :], last[b, l, end : end + 1, :])
            put(8 + row, first[b, l, 1:2, :], last[b, l, end - 1 : end, :])
    for c in range(2):
        for l in range(levels):
            put(16 + c * levels + l, first_rates[c, l, 0:1, :], last_rates[c, l, end : end + 1, :])
    row = 24
    for a in range(numbers.shape[0]):
        for b in range(numbers.shape[1]):
            for s in range(0, numbers.shape[2], width):
                part = numbers[a, b : b + 1, s : s + width].astype(f32)
                to_first[row : row + 1, :] = part
                to_second[row : row + 1, :] = part
                row += 1


def coefficients(meridional, zonal):
    return (
        (1.0 - 4.0 * DIFFUSION) - jnp.abs(zonal) - jnp.abs(meridional),
        DIFFUSION + jnp.maximum(zonal, 0.0),
        DIFFUSION - jnp.minimum(zonal, 0.0),
        DIFFUSION + jnp.maximum(meridional, 0.0),
        DIFFUSION - jnp.minimum(meridional, 0.0),
    )


def stencil(current, south, north, factors):
    width = current.shape[1]
    centre, from_west, from_east, from_south, from_north = factors
    west = pltpu.roll(current, 1, 1)
    east = pltpu.roll(current, width - 1, 1)
    return (
        centre * current
        + from_west * west
        + from_east * east
        + from_south * south
        + from_north * north
    )


def beside(first, second, tile):
    even = lax.rem(tile, 2) == 0
    return jnp.where(even, second, first), jnp.where(even, first, second)


def swap(first, second, tiles):
    pairs = lambda start: [
        pair for i in range(start, tiles - 1, 2) for pair in ((i, i + 1), (i + 1, i))
    ]
    return lax.ppermute(first, "tile", pairs(0)), lax.ppermute(second, "tile", pairs(1))


def turn(s, chips):
    return s % (chips - 1) + 1 if s else 0


def exchange(chunks):
    chips = len(chunks)
    device = lambda chip, core: 2 * chip + core
    swaps = lambda s: [
        (device(i, c), device(i ^ turn(s, chips), c)) for i in range(chips) for c in (0, 1)
    ]
    return [chunks[0]] + [lax.ppermute(chunks[s], "member", swaps(s)) for s in range(1, chips)]


def swap_cores(array):
    return lax.ppermute(array, "member", [(i, i ^ 1) for i in range(lax.axis_size("member"))])


def place():
    block = lax.axis_index("member")
    core = lax.rem(block, 2)
    return block, (block - core) // 2, core


def share_body(*refs, region_rows):
    chunks, (own, other) = refs[:-3], refs[-2:]
    _, _, core = place()
    first = core == 0
    each = own.shape[0] // len(chunks)
    half = chunks[0].shape[0] - 2 * region_rows
    lines = half // 2
    for s, chunk in enumerate(chunks):
        low, high = chunk[0:region_rows, :], chunk[region_rows : 2 * region_rows, :]
        row = s * each
        own[row : row + region_rows, :] = jnp.where(first, low, high)
        other[row : row + region_rows, :] = jnp.where(first, high, low)
        if each == region_rows:
            continue
        seen = chunk[2 * region_rows :, :].astype(f32)
        west = jnp.concatenate([seen[0 : lines - 8], seen[lines : 2 * lines - 8]], axis=0)
        east = jnp.concatenate([seen[8:lines], seen[lines + 8 : 2 * lines]], axis=0)
        own[row + region_rows : row + each, :] = jnp.where(first, west, east).astype(bf16)
        other[row + region_rows : row + each, :] = jnp.where(first, east, west).astype(bf16)


def pack(forecast):
    members, levels, side, width = forecast.shape
    for q in range(width // LANES):
        parts = [
            forecast[:, :, r : r + BLOCK, q * LANES : (q + 1) * LANES].reshape(-1, LANES)
            for r in range(0, side, BLOCK)
        ]
        for i, part in enumerate(transpose_chunks(parts)):
            yield 4 * q + i, part.astype(bf16)


def observe(cell, table, observed, rows, levels, side, width, height):
    members = len(observed[0])
    hits = levels * BLOCK
    for c in range(cell.shape[0]):
        above_row, column = split(cell[c], width)
        level, grid_row = split(above_row, height)
        _, local_row = split(grid_row, side)
        _, local_column = split(column, side)
        band, sub_row = split(local_row, BLOCK)
        high = level * BLOCK + sub_row
        low = band * side + local_column
        for h in [l * BLOCK + r for l in range(levels) for r in rows]:
            here = high == h
            for b in range(members):
                line = table[c, b * hits + h : b * hits + h + 1, :]
                line = jnp.broadcast_to(line, (BLOCK, LANES))
                observed[c][b] = jnp.where(here, pick_lanes(line, low), observed[c][b])


def draft_body(tracer, courant, cell, _, forecast, seen, table, *, height):
    members, levels, side, width = tracer.shape
    for l in range(levels):
        factors = coefficients(courant[0, l], courant[1, l])
        for b in range(members):
            current = tracer[b, l]
            for step in range(2):
                lower = pltpu.roll(current, 1, 0)
                upper = pltpu.roll(current, side - 1, 0)
                current = stencil(current, lower, upper, factors)
            forecast[b, l] = current
    for c, rounded in pack(forecast):
        table[c] = rounded.astype(f32)
    blocks = cell.shape[0]
    observed = [[jnp.zeros((BLOCK, LANES), f32) for _ in range(members)] for _ in range(blocks)]
    observe(cell, table, observed, range(BLOCK), levels, side, width, height)
    for c in range(blocks):
        for b in range(members):
            seen[c, b] = observed[c][b]


def forecast_body(
    tracer, courant, draft, seen, first, second, cell, forecast, *rest, tiles, height
):
    *chunks, send, table = rest
    members, levels, side, width = tracer.shape
    blocks = width // side
    tile = lax.axis_index("tile")
    planes = members * levels
    region_rows = planes * BLOCK
    south, north = beside(first[0:24, :], second[0:24, :], tile)
    own = lambda at: jnp.concatenate(
        [tracer[b, l, at : at + 1, :] for b in range(members) for l in range(levels)], axis=0
    )
    rates = lambda part, at: jnp.concatenate(
        [courant[part, l, at : at + 1, :] for l in range(levels)] * members, axis=0
    )
    here = lambda at: coefficients(rates(0, at), rates(1, at))

    def there(source):
        twice = lambda at: jnp.concatenate([source[at : at + levels]] * members, axis=0)
        return coefficients(twice(16), twice(16 + levels))

    forecast[...] = draft[...]
    for other, inside, at, toward in (
        (south, tile > 0, 0, 1),
        (north, tile < tiles - 1, side - 1, -1),
    ):
        order = lambda outer, inner: (outer, inner) if toward == 1 else (inner, outer)
        rows = [own(at + toward * i) for i in range(4)]
        factors = [here(at + toward * i) for i in range(3)]
        near, far = other[0:planes], other[8 : 8 + planes]
        outside = jnp.where(inside, stencil(near, *order(far, rows[0]), there(other)), 0.0)
        outer = [near, rows[0], rows[1]]
        once = [stencil(rows[i], *order(outer[i], rows[i + 1]), factors[i]) for i in range(3)]
        final = (
            stencil(once[0], *order(outside, once[1]), factors[0]),
            stencil(once[1], *order(once[0], once[2]), factors[1]),
        )
        for i, values in enumerate(final):
            row = at + toward * i
            for b in range(members):
                for l in range(levels):
                    plane = b * levels + l
                    forecast[b, l, row : row + 1, :] = values[plane : plane + 1, :]

    for c, rounded in pack(forecast):
        send[c // 2, c % 2 * region_rows : (c % 2 + 1) * region_rows, :] = rounded
        table[c] = rounded.astype(f32)
    observed = [[seen[c, b] for b in range(members)] for c in range(blocks)]
    edge = (0, 1, BLOCK - 2, BLOCK - 1)
    observe(cell, table, observed, edge, levels, side, width, height)
    for chip in range(blocks // 2):
        lines = [
            observed[(2 * chip + r - 1) % blocks][b] for b in range(members) for r in range(4)
        ]
        for i in range(0, len(lines), 2):
            at = 2 * region_rows + i * BLOCK
            send[chip, at : at + 2 * BLOCK, :] = jnp.concatenate(lines[i : i + 2], axis=0).astype(
                bf16
            )
    _, chip, _ = place()
    for s, chunk in enumerate(chunks):
        chunk[...] = send[chip ^ turn(s, len(chunks))]


def weights_body(
    lists, first, second, cell, value, variance, weights, values, planes, *, tiles, blocks, height, width, side
):
    tile = lax.axis_index("tile")
    block = lax.axis_index("member")
    own_lists = slice(24, 24 + lists.shape[0] * lists.shape[1] * lists.shape[2] // width)
    south, north = beside(first[own_lists, :], second[own_lists, :], tile)
    per_side = side // PATCH
    patches = per_side * per_side
    slots = lists.shape[2]
    depth = 3 * BLOCK
    rows, columns, sizes = [], [], []
    for r in range(3):
        column_block = wrapped(block + (r - 1), blocks)
        first = pl.multiple_of((column_block * tiles + tile) * BLOCK, BLOCK)
        cells = cell[pl.ds(first, BLOCK), :]
        above_row, column = split(cells, width)
        _, grid_row = split(above_row, height)
        rows.append(grid_row)
        columns.append(column)
        sizes.append(variance[pl.ds(first, BLOCK), :])
        values[r * BLOCK : (r + 1) * BLOCK, :] = value[pl.ds(first, BLOCK), :]
    grid_row = jnp.concatenate(rows, axis=0)
    column = jnp.concatenate(columns, axis=0)
    size = jnp.concatenate(sizes, axis=0)

    def pieces(dt, p):
        if dt == 0:
            return [lists[p // per_side, p % per_side : p % per_side + 1, :]]
        source = south if dt < 0 else north
        each = slots // width
        return [
            source[p * each + i : p * each + i + 1].astype(jnp.int32) for i in range(each)
        ]

    index = 0
    for dt in (0, -1, 1):
        for p in range(patches):
            count = jnp.zeros((depth, LANES), f32)
            for part in pieces(dt, p):
                length = part.shape[1]
                region, within = split(part, BLOCK * LANES)
                region_column, region_row = split(region, tiles)
                line, lane = split(within, LANES)
                near = wrapped(region_column - block + 1, blocks)
                fits = (part >= 0) & (region_row == tile) & (near < 3)
                line = jnp.where(fits, near * BLOCK + line, -1)
                one = (iota((depth, length), 0) == line).astype(f32).astype(bf16)
                other = (iota((LANES, length), 0) == lane).astype(f32).astype(bf16)
                count += lax.dot_general(
                    one, other, (((1,), (1,)), ((), ())), preferred_element_type=f32
                )
            patch_row = (tile + dt) * per_side + p // per_side
            patch_column = block * per_side + p % per_side
            row_gap = (grid_row - patch_row * PATCH - PATCH // 2).astype(f32) + 0.5
            turned = column - patch_column * PATCH - PATCH // 2 + width // 2
            column_gap = (wrapped(turned, width) - width // 2).astype(f32) + 0.5
            near = jnp.exp(
                -(row_gap * row_gap + column_gap * column_gap) / (2.0 * LOC_LEN * LOC_LEN)
            )
            planes[index * depth : (index + 1) * depth, :] = count * (near / size)
            index += 1
    for extra in range(index, 16):
        planes[extra * depth : (extra + 1) * depth, :] = jnp.zeros((depth, LANES), f32)
    for i in range(depth):
        weights[:, i * LANES : (i + 1) * LANES] = planes[pl.ds(i, 16, stride=depth), :]


def halves(values):
    high = values.astype(bf16)
    return high, (values - high.astype(f32)).astype(bf16)


def dot_rows(left, right):
    return lax.dot_general(left, right, (((1,), (1,)), ((), ())), preferred_element_type=f32)


def scale(spread, weights, tall_high, tall_low, at, first):
    ensemble = spread.shape[0]
    for p in range(tall_high.shape[0] // ensemble):
        high, low = halves(spread * weights[first + p : first + p + 1, at])
        tall_high[p * ensemble : (p + 1) * ensemble, at] = high
        tall_low[p * ensemble : (p + 1) * ensemble, at] = low


def products(wide, tall_high, tall_low):
    rows = wide.shape[0] // 2
    both = dot_rows(wide[...], tall_high[...])
    result = both[0:rows] + both[rows:] + dot_rows(wide[0:rows, :], tall_low[...])
    count = result.shape[1] // 64
    if count % 2:
        result = jnp.concatenate([result, jnp.zeros((rows, 64), f32)], axis=1)
    found = []
    for n in range(count):
        piece = result[:, n // 2 * LANES : (n // 2 + 1) * LANES]
        if n % 2:
            piece = pltpu.roll(piece, 64, 1)
        found.append(jnp.where(iota(piece.shape, 1) < 64, piece, 0.0))
    return found


def neighbours_body(
    mine, theirs, weights, values, to_first, to_second, wide, planes, tall_high, tall_low, *, sources, members, region_rows
):
    depth = 3 * BLOCK
    each = 2 * mine.shape[0] // sources
    _, chip, core = place()
    ensemble = sources * members
    total = jnp.zeros((depth, LANES), f32)
    for s in range(sources):
        source, row = (mine, theirs)[s % 2], s // 2 * each
        both = source[row + region_rows : row + each, :].astype(f32)
        device = 2 * (chip ^ turn(s // 2, sources // 2)) + (core ^ (s % 2))
        at = pl.multiple_of(device * (members * depth), BLOCK)
        planes[pl.ds(at, members * depth), :] = both
        for b in range(members):
            total += both[b * depth : (b + 1) * depth, :]
    mean = total / ensemble
    for k in range(ensemble):
        planes[k * depth : (k + 1) * depth, :] -= mean
    planes[ensemble * depth : (ensemble + 1) * depth, :] = values[...] - mean
    for k in range(ensemble + 1, ensemble + 8):
        planes[k * depth : (k + 1) * depth, :] = jnp.zeros((depth, LANES), f32)
    rows = ensemble + 8
    patches = tall_high.shape[0] // (2 * ensemble)
    for i in range(depth):
        at = slice(i * LANES, (i + 1) * LANES)
        tile = planes[pl.ds(i, rows, stride=depth), :]
        high, low = halves(tile)
        wide[0:rows, at] = high
        wide[rows : 2 * rows, at] = low
        scale(tile[0:ensemble, :], weights, tall_high, tall_low, at, patches)
    found = products(wide, tall_high, tall_low)
    odd = lax.rem(lax.axis_index("tile"), 2) == 1
    count = len(found) // 2
    for i in range(count):
        at = slice(i * LANES, (i + 1) * LANES)
        for_south, for_north = found[i], found[count + i]
        to_first[:, at] = jnp.where(odd, for_south, for_north)
        to_second[:, at] = jnp.where(odd, for_north, for_south)


def own_body(
    mine, theirs, weights, wide, own, centred, tall_high, tall_low, *, sources, members, region_rows
):
    _, chip, core = place()
    each = 2 * mine.shape[0] // sources
    ensemble = sources * members
    hits = region_rows // members
    total = jnp.zeros((hits, LANES), f32)
    for s in range(sources):
        source, row = (mine, theirs)[s % 2], s // 2 * each
        device = 2 * (chip ^ turn(s // 2, sources // 2)) + (core ^ (s % 2))
        part = source[row : row + region_rows, :].astype(f32)
        for b in range(members):
            one = part[b * hits : (b + 1) * hits, :]
            centred[device * members + b] = one
            total += one
    mean = total / ensemble
    for k in range(ensemble):
        centred[k] -= mean
    rows = ensemble + 8
    for i in range(0, wide.shape[1], LANES):
        at = slice(i, i + LANES)
        spread = wide[0:ensemble, at].astype(f32) + wide[rows : rows + ensemble, at].astype(f32)
        scale(spread, weights, tall_high, tall_low, at, 0)
    for i, piece in enumerate(products(wide, tall_high, tall_low)):
        own[:, i * LANES : (i + 1) * LANES] = piece


def analysis_body(own, first, second, centred, *refs, patches, sources, members, region_rows):
    chunks, factors = refs[:-1], refs[-1]
    _, chip, _ = place()
    ensemble = sources * members
    hits = region_rows // members
    count = patches * ensemble // 64
    group = 64 // ensemble
    row = iota((ensemble + 8, LANES), 0)
    lane = iota((ensemble + 8, LANES), 1)
    within = lane & (ensemble - 1)
    start = jnp.where(
        (row == within) & (row < ensemble), jnp.where(lane < 64, ensemble - 1.0, 1.0), 0.0
    )
    lane8 = iota((BLOCK, LANES), 1)
    group_start = (lane8 & 63) & ~(ensemble - 1)
    transforms = []
    for i in range(count):
        at = slice(i * LANES, (i + 1) * LANES)
        state = own[:, at] + first[:, at] + second[:, at] + start
        columns = [pick_lanes(state, group_start + k) for k in range(ensemble)]
        pivots = jnp.ones((ensemble, LANES), f32)
        for k in range(ensemble):
            pivot = columns[k][k : k + 1, :]
            factor = jnp.where(row > k, columns[k], 0.0) / pivot
            for j in range(k + 1, ensemble):
                columns[j] = columns[j] - factor * columns[j][k : k + 1, :]
            state = state - factor * state[k : k + 1, :]
            pivots = jnp.where(row[0:ensemble] == k, pivot, pivots)
        inverse = state[0:ensemble, :] * lax.rsqrt(pivots)
        mean_weight = -state[ensemble : ensemble + 1, :]
        unit = jnp.where(row[0:ensemble] == within[0:ensemble], 1.0, 0.0)
        transforms.append(mean_weight + (ensemble - 1.0) ** 0.5 * inverse - unit)

    side_lanes = 32
    patch = (lane8 // (2 * side_lanes)) * 2 + (lane8 & (side_lanes - 1)) // PATCH
    inside = 64 + (patch & (group - 1)) * ensemble if group > 1 else 64 + 0 * patch
    which = patch // group
    for j in range(ensemble):
        chosen = pick_lanes(transforms[0], inside + j)
        for i in range(1, count):
            other = pick_lanes(transforms[i], inside + j)
            chosen = jnp.where(jnp.broadcast_to(which[0:1] == i, chosen.shape), other, chosen)
        factors[j] = chosen

    for s, chunk in enumerate(chunks):
        for c in (0, 1):
            first_member = (2 * (chip ^ turn(s, len(chunks))) + c) * members
            totals = [jnp.zeros((hits, LANES), f32) for _ in range(members)]
            for j in range(ensemble):
                centred_j = centred[j]
                for b in range(members):
                    totals[b] += factors[j, pl.ds(first_member + b, 1), :] * centred_j
            at = slice(c * region_rows, (c + 1) * region_rows)
            chunk[at, :] = jnp.concatenate(totals, axis=0).astype(bf16)


def output_body(forecast, mine, theirs, analysis, ordered):
    members, levels, side, width = forecast.shape
    _, chip, core = place()
    rows = ordered.shape[1]
    chips = mine.shape[0] // rows
    for s in range(chips):
        at = slice(s * rows, (s + 1) * rows)
        source = 2 * (chip ^ turn(s, chips))
        ordered[source + core] = mine[at, :].astype(f32)
        ordered[source + (core ^ 1)] = theirs[at, :].astype(f32)
    for q in range(width // LANES):
        parts = [ordered[4 * q + c] for c in range(4)]
        at = slice(q * LANES, (q + 1) * LANES)
        for r, part in enumerate(transpose_chunks(parts)):
            rows = slice(r * BLOCK, (r + 1) * BLOCK)
            analysis[:, :, rows, at] = forecast[:, :, rows, at] + part.reshape(
                members, levels, BLOCK, LANES
            )


def shards(member_concentration, courant_pairs, obs_cell, obs_value, obs_error, obs_list):
    members, levels, side, width = member_concentration.shape
    blocks = lax.axis_size("member")
    tiles = lax.axis_size("tile")
    height = side * tiles
    ensemble = members * blocks
    per_side = side // PATCH
    patches = per_side * per_side
    slots = obs_list.shape[2]
    region_rows = members * levels * BLOCK
    depth = 3 * BLOCK
    all_rows = region_rows + members * depth
    chips = blocks // 2
    chip_rows = 2 * region_rows + members * 4 * BLOCK
    edge_rows = -(-(24 + patches * slots // width) // 8) * 8
    edge_shape = (members, levels, BLOCK, width)
    rate_shape = (2, levels, BLOCK, width)

    to_first, to_second = call(
        pack_edges,
        [((edge_rows, width), f32)] * 2,
        [
            pltpu.VMEM(edge_shape, f32),
            pltpu.VMEM(edge_shape, f32),
            pltpu.VMEM(rate_shape, f32),
            pltpu.VMEM(rate_shape, f32),
            pltpu.VMEM(obs_list.shape, jnp.int32),
            pltpu.SemaphoreType.DMA((5,)),
        ],
        specs=[pl.BlockSpec(memory_space=pltpu.HBM)] * 3,
        vmem=63,
    )(member_concentration, courant_pairs, obs_list)
    first, second = swap(to_first, to_second, tiles)

    whole = pl.BlockSpec(memory_space=pltpu.VMEM)
    flat = lambda array: array.reshape(-1, LANES)
    cell = flat(obs_cell)
    cell_row = lax.dynamic_index_in_dim(
        cell.reshape(blocks, tiles, BLOCK, LANES), lax.axis_index("tile"), 1, False
    )
    draft, seen = call(
        functools.partial(draft_body, height=height),
        [(member_concentration.shape, f32), ((blocks, members, BLOCK, LANES), f32)],
        [pltpu.VMEM((blocks, region_rows, LANES), f32)],
        flops=50_000_000,
        specs=[whole, whole, whole, pl.BlockSpec(memory_space=pltpu.HBM)],
    )(member_concentration, courant_pairs, cell_row, to_second)
    forecast, *chunks = call(
        functools.partial(forecast_body, tiles=tiles, height=height),
        [(member_concentration.shape, f32)] + [((chip_rows, LANES), bf16)] * chips,
        [
            pltpu.VMEM((chips, chip_rows, LANES), bf16),
            pltpu.VMEM((blocks, region_rows, LANES), f32),
        ],
    )(
        member_concentration,
        courant_pairs,
        draft,
        seen,
        first,
        second,
        cell_row,
    )
    received = exchange(chunks)
    weights, values = call(
        functools.partial(
            weights_body, tiles=tiles, blocks=blocks, height=height, width=width, side=side
        ),
        [((16, depth * LANES), f32), ((depth, LANES), f32)],
        [pltpu.VMEM((16 * depth, LANES), f32)],
        flops=100_000_000,
    )(obs_list, first, second, cell, flat(obs_value), flat(obs_error))

    sizes = dict(sources=blocks, members=members, region_rows=region_rows)
    tall = patches * ensemble
    length = depth * LANES
    system_shape = (ensemble + 8, tall // 64 * LANES)
    wide_shape = (2 * (ensemble + 8), length)
    centred_shape = (ensemble, levels * BLOCK, LANES)
    share = functools.partial(share_body, region_rows=region_rows)
    mine, theirs = call(share, [((chips * all_rows, LANES), bf16)] * 2)(*received, values)
    theirs = swap_cores(theirs)
    to_first, to_second, wide = call(
        functools.partial(neighbours_body, **sizes),
        [(system_shape, f32), (system_shape, f32), (wide_shape, bf16)],
        [
            pltpu.VMEM(((ensemble + 8) * depth, LANES), f32),
            pltpu.VMEM((2 * tall, length), bf16),
            pltpu.VMEM((2 * tall, length), bf16),
        ],
    )(mine, theirs, weights, values)
    first, second = swap(to_first, to_second, tiles)
    own, centred = call(
        functools.partial(own_body, **sizes),
        [(system_shape, f32), (centred_shape, f32)],
        [pltpu.VMEM((tall, length), bf16), pltpu.VMEM((tall, length), bf16)],
        flops=50_000_000,
    )(mine, theirs, weights, wide)

    changes = call(
        functools.partial(analysis_body, patches=patches, **sizes),
        [((2 * region_rows, LANES), bf16)] * chips,
        [pltpu.VMEM((ensemble, ensemble, LANES), f32)],
    )(own, first, second, centred)
    returned = exchange(changes)
    mine, theirs = call(share, [((chips * region_rows, LANES), bf16)] * 2)(*returned, forecast)
    theirs = swap_cores(theirs)
    (analysis,) = call(
        output_body, [(forecast.shape, f32)], [pltpu.VMEM((blocks, region_rows, LANES), f32)]
    )(forecast, mine, theirs)
    return analysis


def solution(mesh):
    return jax.shard_map(
        shards,
        mesh=mesh,
        in_specs=(
            P("member", None, "tile", None),
            P(None, None, "tile", None),
            P(),
            P(),
            P(),
            P("tile", "member", None),
        ),
        out_specs=P("member", None, "tile", None),
        check_vma=False,
    )
```

```python
import functools

import jax
import jax.numpy as jnp
from jax import lax
from jax.experimental import pallas as pl
from jax.experimental.pallas import tpu as pltpu
from jax.sharding import PartitionSpec as P

PATCH = 16
LOC_LEN = 16
DIFFUSION = 0.05
LANES = 128
BLOCK = 8

f32 = jnp.float32
bf16 = jnp.bfloat16


def call(body, outs, scratch=(), flops=1_000_000, moved=1_000_000, specs=None, vmem=48):
    specs = {} if specs is None else {"in_specs": specs}
    return pl.pallas_call(
        body,
        **specs,
        out_shape=[jax.ShapeDtypeStruct(shape, kind) for shape, kind in outs],
        scratch_shapes=list(scratch),
        compiler_params=pltpu.CompilerParams(vmem_limit_bytes=vmem * 1024 * 1024),
        cost_estimate=pl.CostEstimate(flops=flops, bytes_accessed=moved, transcendentals=0),
    )


def split(number, size):
    if size & (size - 1) == 0:
        return number >> (size.bit_length() - 1), number & (size - 1)
    quotient = number // size
    return quotient, number - quotient * size


def wrapped(number, size):
    if size & (size - 1) == 0:
        return number & (size - 1)
    return lax.rem(number + size, size)


def iota(shape, axis):
    return lax.broadcasted_iota(jnp.int32, shape, axis)


def pick_lanes(values, index):
    rows = [
        jnp.take_along_axis(values[r : r + BLOCK], index, axis=1, mode="promise_in_bounds")
        for r in range(0, values.shape[0], BLOCK)
    ]
    return rows[0] if len(rows) == 1 else jnp.concatenate(rows, axis=0)


def transpose_chunks(parts):
    lane = iota(parts[0].shape, 1)
    low = lane < 64
    even = (lane & 32) == 0
    parts = list(parts)
    for i in (0, 1):
        a, b = parts[i], parts[i + 2]
        parts[i] = jnp.where(low, a, pltpu.roll(b, 64, 1))
        parts[i + 2] = jnp.where(low, pltpu.roll(a, 64, 1), b)
    for i in (0, 2):
        a, b = parts[i], parts[i + 1]
        parts[i] = jnp.where(even, a, pltpu.roll(b, 32, 1))
        parts[i + 1] = jnp.where(even, pltpu.roll(a, 96, 1), b)
    return parts


def pack_edges(
    tracer, courant, lists, to_first, to_second, first, last, first_rates, last_rates, numbers, arrived
):
    members, levels, side, width = tracer.shape
    copies = [
        pltpu.make_async_copy(source, target, arrived.at[i])
        for i, (source, target) in enumerate(
            (
                (tracer.at[:, :, 0:BLOCK, :], first),
                (tracer.at[:, :, side - BLOCK : side, :], last),
                (courant.at[:, :, 0:BLOCK, :], first_rates),
                (courant.at[:, :, side - BLOCK : side, :], last_rates),
                (lists, numbers),
            )
        )
    ]
    for copy in copies:
        copy.start()
    for copy in copies:
        copy.wait()
    even = lax.rem(lax.axis_index("tile"), 2) == 0

    def put(row, low, high):
        to_first[row : row + 1, :] = jnp.where(even, high, low)
        to_second[row : row + 1, :] = jnp.where(even, low, high)

    end = BLOCK - 1
    for b in range(members):
        for l in range(levels):
            row = b * levels + l
            put(row, first[b, l, 0:1, :], last[b, l, end : end + 1, :])
            put(8 + row, first[b, l, 1:2, :], last[b, l, end - 1 : end, :])
    for c in range(2):
        for l in range(levels):
            put(16 + c * levels + l, first_rates[c, l, 0:1, :], last_rates[c, l, end : end + 1, :])
    row = 24
    for a in range(numbers.shape[0]):
        for b in range(numbers.shape[1]):
            for s in range(0, numbers.shape[2], width):
                part = numbers[a, b : b + 1, s : s + width].astype(f32)
                to_first[row : row + 1, :] = part
                to_second[row : row + 1, :] = part
                row += 1


def coefficients(meridional, zonal):
    return (
        (1.0 - 4.0 * DIFFUSION) - jnp.abs(zonal) - jnp.abs(meridional),
        DIFFUSION + jnp.maximum(zonal, 0.0),
        DIFFUSION - jnp.minimum(zonal, 0.0),
        DIFFUSION + jnp.maximum(meridional, 0.0),
        DIFFUSION - jnp.minimum(meridional, 0.0),
    )


def stencil(current, south, north, factors):
    width = current.shape[1]
    centre, from_west, from_east, from_south, from_north = factors
    west = pltpu.roll(current, 1, 1)
    east = pltpu.roll(current, width - 1, 1)
    return (
        centre * current
        + from_west * west
        + from_east * east
        + from_south * south
        + from_north * north
    )


def beside(first, second, tile):
    even = lax.rem(tile, 2) == 0
    return jnp.where(even, second, first), jnp.where(even, first, second)


def swap(first, second, tiles):
    pairs = lambda start: [
        pair for i in range(start, tiles - 1, 2) for pair in ((i, i + 1), (i + 1, i))
    ]
    return lax.ppermute(first, "tile", pairs(0)), lax.ppermute(second, "tile", pairs(1))


def turn(s, chips):
    return (chips - s) % chips


def exchange(chunks):
    chips = len(chunks)
    device = lambda chip, core: 2 * chip + core
    swaps = lambda s: [
        (device(i, c), device(i ^ turn(s, chips), c)) for i in range(chips) for c in (0, 1)
    ]
    return [chunks[0]] + [lax.ppermute(chunks[s], "member", swaps(s)) for s in range(1, chips)]


def swap_cores(array):
    return lax.ppermute(array, "member", [(i, i ^ 1) for i in range(lax.axis_size("member"))])


def place():
    block = lax.axis_index("member")
    core = lax.rem(block, 2)
    return block, (block - core) // 2, core


def share_body(*refs, region_rows):
    chunks, (own, other) = refs[:-3], refs[-2:]
    _, _, core = place()
    first = core == 0
    each = own.shape[0] // len(chunks)
    half = chunks[0].shape[0] - 2 * region_rows
    lines = half // 2
    for s, chunk in enumerate(chunks):
        low, high = chunk[0:region_rows, :], chunk[region_rows : 2 * region_rows, :]
        row = s * each
        own[row : row + region_rows, :] = jnp.where(first, low, high)
        other[row : row + region_rows, :] = jnp.where(first, high, low)
        if each == region_rows:
            continue
        seen = chunk[2 * region_rows :, :].astype(f32)
        west = jnp.concatenate([seen[0 : lines - 8], seen[lines : 2 * lines - 8]], axis=0)
        east = jnp.concatenate([seen[8:lines], seen[lines + 8 : 2 * lines]], axis=0)
        own[row + region_rows : row + each, :] = jnp.where(first, west, east).astype(bf16)
        other[row + region_rows : row + each, :] = jnp.where(first, east, west).astype(bf16)


def pack(forecast):
    members, levels, side, width = forecast.shape
    for q in range(width // LANES):
        parts = [
            forecast[:, :, r : r + BLOCK, q * LANES : (q + 1) * LANES].reshape(-1, LANES)
            for r in range(0, side, BLOCK)
        ]
        for i, part in enumerate(transpose_chunks(parts)):
            yield 4 * q + i, part.astype(bf16)


def observe(cell, table, observed, rows, levels, side, width, height):
    members = len(observed[0])
    hits = levels * BLOCK
    for c in range(cell.shape[0]):
        above_row, column = split(cell[c], width)
        level, grid_row = split(above_row, height)
        _, local_row = split(grid_row, side)
        _, local_column = split(column, side)
        band, sub_row = split(local_row, BLOCK)
        high = level * BLOCK + sub_row
        low = band * side + local_column
        for h in [l * BLOCK + r for l in range(levels) for r in rows]:
            here = high == h
            for b in range(members):
                line = table[c, b * hits + h : b * hits + h + 1, :]
                line = jnp.broadcast_to(line, (BLOCK, LANES))
                observed[c][b] = jnp.where(here, pick_lanes(line, low), observed[c][b])


def draft_body(tracer, courant, cell, _, forecast, seen, table, *, height):
    members, levels, side, width = tracer.shape
    for l in range(levels):
        factors = coefficients(courant[0, l], courant[1, l])
        for b in range(members):
            current = tracer[b, l]
            for step in range(2):
                lower = pltpu.roll(current, 1, 0)
                upper = pltpu.roll(current, side - 1, 0)
                current = stencil(current, lower, upper, factors)
            forecast[b, l] = current
    for c, rounded in pack(forecast):
        table[c] = rounded.astype(f32)
    blocks = cell.shape[0]
    observed = [[jnp.zeros((BLOCK, LANES), f32) for _ in range(members)] for _ in range(blocks)]
    observe(cell, table, observed, range(BLOCK), levels, side, width, height)
    for c in range(blocks):
        for b in range(members):
            seen[c, b] = observed[c][b]


def forecast_body(
    tracer, courant, draft, seen, first, second, cell, forecast, *rest, tiles, height
):
    *chunks, send, table = rest
    members, levels, side, width = tracer.shape
    blocks = width // side
    tile = lax.axis_index("tile")
    planes = members * levels
    region_rows = planes * BLOCK
    south, north = beside(first[0:24, :], second[0:24, :], tile)
    own = lambda at: jnp.concatenate(
        [tracer[b, l, at : at + 1, :] for b in range(members) for l in range(levels)], axis=0
    )
    rates = lambda part, at: jnp.concatenate(
        [courant[part, l, at : at + 1, :] for l in range(levels)] * members, axis=0
    )
    here = lambda at: coefficients(rates(0, at), rates(1, at))

    def there(source):
        twice = lambda at: jnp.concatenate([source[at : at + levels]] * members, axis=0)
        return coefficients(twice(16), twice(16 + levels))

    forecast[...] = draft[...]
    for other, inside, at, toward in (
        (south, tile > 0, 0, 1),
        (north, tile < tiles - 1, side - 1, -1),
    ):
        order = lambda outer, inner: (outer, inner) if toward == 1 else (inner, outer)
        rows = [own(at + toward * i) for i in range(4)]
        factors = [here(at + toward * i) for i in range(3)]
        near, far = other[0:planes], other[8 : 8 + planes]
        outside = jnp.where(inside, stencil(near, *order(far, rows[0]), there(other)), 0.0)
        outer = [near, rows[0], rows[1]]
        once = [stencil(rows[i], *order(outer[i], rows[i + 1]), factors[i]) for i in range(3)]
        final = (
            stencil(once[0], *order(outside, once[1]), factors[0]),
            stencil(once[1], *order(once[0], once[2]), factors[1]),
        )
        for i, values in enumerate(final):
            row = at + toward * i
            for b in range(members):
                for l in range(levels):
                    plane = b * levels + l
                    forecast[b, l, row : row + 1, :] = values[plane : plane + 1, :]

    for c, rounded in pack(forecast):
        send[c // 2, c % 2 * region_rows : (c % 2 + 1) * region_rows, :] = rounded
        table[c] = rounded.astype(f32)
    observed = [[seen[c, b] for b in range(members)] for c in range(blocks)]
    edge = (0, 1, BLOCK - 2, BLOCK - 1)
    observe(cell, table, observed, edge, levels, side, width, height)
    for chip in range(blocks // 2):
        lines = [
            observed[(2 * chip + r - 1) % blocks][b] for b in range(members) for r in range(4)
        ]
        for i in range(0, len(lines), 2):
            at = 2 * region_rows + i * BLOCK
            send[chip, at : at + 2 * BLOCK, :] = jnp.concatenate(lines[i : i + 2], axis=0).astype(
                bf16
            )
    _, chip, _ = place()
    for s, chunk in enumerate(chunks):
        chunk[...] = send[chip ^ turn(s, len(chunks))]


def weights_body(
    lists, first, second, cell, value, variance, weights, values, planes, *, tiles, blocks, height, width, side
):
    tile = lax.axis_index("tile")
    block = lax.axis_index("member")
    own_lists = slice(24, 24 + lists.shape[0] * lists.shape[1] * lists.shape[2] // width)
    south, north = beside(first[own_lists, :], second[own_lists, :], tile)
    per_side = side // PATCH
    patches = per_side * per_side
    slots = lists.shape[2]
    depth = 3 * BLOCK
    rows, columns, sizes = [], [], []
    for r in range(3):
        column_block = wrapped(block + (r - 1), blocks)
        first = pl.multiple_of((column_block * tiles + tile) * BLOCK, BLOCK)
        cells = cell[pl.ds(first, BLOCK), :]
        above_row, column = split(cells, width)
        _, grid_row = split(above_row, height)
        rows.append(grid_row)
        columns.append(column)
        sizes.append(variance[pl.ds(first, BLOCK), :])
        values[r * BLOCK : (r + 1) * BLOCK, :] = value[pl.ds(first, BLOCK), :]
    grid_row = jnp.concatenate(rows, axis=0)
    column = jnp.concatenate(columns, axis=0)
    size = jnp.concatenate(sizes, axis=0)

    def pieces(dt, p):
        if dt == 0:
            return [lists[p // per_side, p % per_side : p % per_side + 1, :]]
        source = south if dt < 0 else north
        each = slots // width
        return [
            source[p * each + i : p * each + i + 1].astype(jnp.int32) for i in range(each)
        ]

    index = 0
    for dt in (0, -1, 1):
        for p in range(patches):
            count = jnp.zeros((depth, LANES), f32)
            for part in pieces(dt, p):
                length = part.shape[1]
                region, within = split(part, BLOCK * LANES)
                region_column, region_row = split(region, tiles)
                line, lane = split(within, LANES)
                near = wrapped(region_column - block + 1, blocks)
                fits = (part >= 0) & (region_row == tile) & (near < 3)
                line = jnp.where(fits, near * BLOCK + line, -1)
                one = (iota((depth, length), 0) == line).astype(f32).astype(bf16)
                other = (iota((LANES, length), 0) == lane).astype(f32).astype(bf16)
                count += lax.dot_general(
                    one, other, (((1,), (1,)), ((), ())), preferred_element_type=f32
                )
            patch_row = (tile + dt) * per_side + p // per_side
            patch_column = block * per_side + p % per_side
            row_gap = (grid_row - patch_row * PATCH - PATCH // 2).astype(f32) + 0.5
            turned = column - patch_column * PATCH - PATCH // 2 + width // 2
            column_gap = (wrapped(turned, width) - width // 2).astype(f32) + 0.5
            near = jnp.exp(
                -(row_gap * row_gap + column_gap * column_gap) / (2.0 * LOC_LEN * LOC_LEN)
            )
            planes[index * depth : (index + 1) * depth, :] = count * (near / size)
            index += 1
    for extra in range(index, 16):
        planes[extra * depth : (extra + 1) * depth, :] = jnp.zeros((depth, LANES), f32)
    for i in range(depth):
        weights[:, i * LANES : (i + 1) * LANES] = planes[pl.ds(i, 16, stride=depth), :]


def halves(values):
    high = values.astype(bf16)
    return high, (values - high.astype(f32)).astype(bf16)


def dot_rows(left, right):
    return lax.dot_general(left, right, (((1,), (1,)), ((), ())), preferred_element_type=f32)


def scale(spread, weights, tall_high, tall_low, at, first):
    ensemble = spread.shape[0]
    for p in range(tall_high.shape[0] // ensemble):
        high, low = halves(spread * weights[first + p : first + p + 1, at])
        tall_high[p * ensemble : (p + 1) * ensemble, at] = high
        tall_low[p * ensemble : (p + 1) * ensemble, at] = low


def products(wide, tall_high, tall_low):
    rows = wide.shape[0] // 2
    both = dot_rows(wide[...], tall_high[...])
    result = both[0:rows] + both[rows:] + dot_rows(wide[0:rows, :], tall_low[...])
    count = result.shape[1] // 64
    if count % 2:
        result = jnp.concatenate([result, jnp.zeros((rows, 64), f32)], axis=1)
    found = []
    for n in range(count):
        piece = result[:, n // 2 * LANES : (n // 2 + 1) * LANES]
        if n % 2:
            piece = pltpu.roll(piece, 64, 1)
        found.append(jnp.where(iota(piece.shape, 1) < 64, piece, 0.0))
    return found


def neighbours_body(
    mine, theirs, weights, values, to_first, to_second, wide, planes, tall_high, tall_low, *, sources, members, region_rows
):
    depth = 3 * BLOCK
    each = 2 * mine.shape[0] // sources
    _, chip, core = place()
    ensemble = sources * members
    total = jnp.zeros((depth, LANES), f32)
    for s in range(sources):
        source, row = (mine, theirs)[s % 2], s // 2 * each
        both = source[row + region_rows : row + each, :].astype(f32)
        device = 2 * (chip ^ turn(s // 2, sources // 2)) + (core ^ (s % 2))
        at = pl.multiple_of(device * (members * depth), BLOCK)
        planes[pl.ds(at, members * depth), :] = both
        for b in range(members):
            total += both[b * depth : (b + 1) * depth, :]
    mean = total / ensemble
    for k in range(ensemble):
        planes[k * depth : (k + 1) * depth, :] -= mean
    planes[ensemble * depth : (ensemble + 1) * depth, :] = values[...] - mean
    for k in range(ensemble + 1, ensemble + 8):
        planes[k * depth : (k + 1) * depth, :] = jnp.zeros((depth, LANES), f32)
    rows = ensemble + 8
    patches = tall_high.shape[0] // (2 * ensemble)
    for i in range(depth):
        at = slice(i * LANES, (i + 1) * LANES)
        tile = planes[pl.ds(i, rows, stride=depth), :]
        high, low = halves(tile)
        wide[0:rows, at] = high
        wide[rows : 2 * rows, at] = low
        scale(tile[0:ensemble, :], weights, tall_high, tall_low, at, patches)
    found = products(wide, tall_high, tall_low)
    odd = lax.rem(lax.axis_index("tile"), 2) == 1
    count = len(found) // 2
    for i in range(count):
        at = slice(i * LANES, (i + 1) * LANES)
        for_south, for_north = found[i], found[count + i]
        to_first[:, at] = jnp.where(odd, for_south, for_north)
        to_second[:, at] = jnp.where(odd, for_north, for_south)


def own_body(
    mine, theirs, weights, wide, own, centred, tall_high, tall_low, *, sources, members, region_rows
):
    _, chip, core = place()
    each = 2 * mine.shape[0] // sources
    ensemble = sources * members
    hits = region_rows // members
    total = jnp.zeros((hits, LANES), f32)
    for s in range(sources):
        source, row = (mine, theirs)[s % 2], s // 2 * each
        device = 2 * (chip ^ turn(s // 2, sources // 2)) + (core ^ (s % 2))
        part = source[row : row + region_rows, :].astype(f32)
        for b in range(members):
            one = part[b * hits : (b + 1) * hits, :]
            centred[device * members + b] = one
            total += one
    mean = total / ensemble
    for k in range(ensemble):
        centred[k] -= mean
    rows = ensemble + 8
    for i in range(0, wide.shape[1], LANES):
        at = slice(i, i + LANES)
        spread = wide[0:ensemble, at].astype(f32) + wide[rows : rows + ensemble, at].astype(f32)
        scale(spread, weights, tall_high, tall_low, at, 0)
    for i, piece in enumerate(products(wide, tall_high, tall_low)):
        own[:, i * LANES : (i + 1) * LANES] = piece


def analysis_body(own, first, second, centred, *refs, patches, sources, members, region_rows):
    chunks, factors = refs[:-1], refs[-1]
    _, chip, _ = place()
    ensemble = sources * members
    hits = region_rows // members
    count = patches * ensemble // 64
    group = 64 // ensemble
    row = iota((ensemble + 8, LANES), 0)
    lane = iota((ensemble + 8, LANES), 1)
    within = lane & (ensemble - 1)
    start = jnp.where(
        (row == within) & (row < ensemble), jnp.where(lane < 64, ensemble - 1.0, 1.0), 0.0
    )
    lane8 = iota((BLOCK, LANES), 1)
    group_start = (lane8 & 63) & ~(ensemble - 1)
    transforms = []
    for i in range(count):
        at = slice(i * LANES, (i + 1) * LANES)
        state = own[:, at] + first[:, at] + second[:, at] + start
        columns = [pick_lanes(state, group_start + k) for k in range(ensemble)]
        pivots = jnp.ones((ensemble, LANES), f32)
        for k in range(ensemble):
            pivot = columns[k][k : k + 1, :]
            factor = jnp.where(row > k, columns[k], 0.0) * (1.0 / pivot)
            for j in range(k + 1, ensemble):
                columns[j] = columns[j] - factor * columns[j][k : k + 1, :]
            state = state - factor * state[k : k + 1, :]
            pivots = jnp.where(row[0:ensemble] == k, pivot, pivots)
        inverse = state[0:ensemble, :] * lax.rsqrt(pivots)
        mean_weight = -state[ensemble : ensemble + 1, :]
        unit = jnp.where(row[0:ensemble] == within[0:ensemble], 1.0, 0.0)
        transforms.append(mean_weight + (ensemble - 1.0) ** 0.5 * inverse - unit)

    side_lanes = 32
    patch = (lane8 // (2 * side_lanes)) * 2 + (lane8 & (side_lanes - 1)) // PATCH
    inside = 64 + (patch & (group - 1)) * ensemble if group > 1 else 64 + 0 * patch
    which = patch // group
    for j in range(ensemble):
        chosen = pick_lanes(transforms[0], inside + j)
        for i in range(1, count):
            other = pick_lanes(transforms[i], inside + j)
            chosen = jnp.where(jnp.broadcast_to(which[0:1] == i, chosen.shape), other, chosen)
        factors[j] = chosen

    for s, chunk in enumerate(chunks):
        for c in (0, 1):
            first_member = (2 * (chip ^ turn(s, len(chunks))) + c) * members
            totals = [jnp.zeros((hits, LANES), f32) for _ in range(members)]
            for j in range(ensemble):
                centred_j = centred[j]
                for b in range(members):
                    totals[b] += factors[j, pl.ds(first_member + b, 1), :] * centred_j
            at = slice(c * region_rows, (c + 1) * region_rows)
            chunk[at, :] = jnp.concatenate(totals, axis=0).astype(bf16)


def output_body(forecast, mine, theirs, analysis):
    members, levels, side, width = forecast.shape
    _, chip, core = place()
    rows = members * levels * BLOCK
    chips = mine.shape[0] // rows

    def block(device):
        s = lax.rem(chips - (chip ^ (device // 2)), chips)
        at = pl.ds(pl.multiple_of(s * rows, rows), rows)
        return jnp.where(core == device % 2, mine[at, :].astype(f32), theirs[at, :].astype(f32))

    for q in range(width // LANES):
        parts = [block(4 * q + c) for c in range(4)]
        at = slice(q * LANES, (q + 1) * LANES)
        for r, part in enumerate(transpose_chunks(parts)):
            lines = slice(r * BLOCK, (r + 1) * BLOCK)
            analysis[:, :, lines, at] = forecast[:, :, lines, at] + part.reshape(
                members, levels, BLOCK, LANES
            )


def shards(member_concentration, courant_pairs, obs_cell, obs_value, obs_error, obs_list):
    members, levels, side, width = member_concentration.shape
    blocks = lax.axis_size("member")
    tiles = lax.axis_size("tile")
    height = side * tiles
    ensemble = members * blocks
    per_side = side // PATCH
    patches = per_side * per_side
    slots = obs_list.shape[2]
    region_rows = members * levels * BLOCK
    depth = 3 * BLOCK
    all_rows = region_rows + members * depth
    chips = blocks // 2
    chip_rows = 2 * region_rows + members * 4 * BLOCK
    edge_rows = -(-(24 + patches * slots // width) // 8) * 8
    edge_shape = (members, levels, BLOCK, width)
    rate_shape = (2, levels, BLOCK, width)

    to_first, to_second = call(
        pack_edges,
        [((edge_rows, width), f32)] * 2,
        [
            pltpu.VMEM(edge_shape, f32),
            pltpu.VMEM(edge_shape, f32),
            pltpu.VMEM(rate_shape, f32),
            pltpu.VMEM(rate_shape, f32),
            pltpu.VMEM(obs_list.shape, jnp.int32),
            pltpu.SemaphoreType.DMA((5,)),
        ],
        specs=[pl.BlockSpec(memory_space=pltpu.HBM)] * 3,
        vmem=63,
    )(member_concentration, courant_pairs, obs_list)
    first, second = swap(to_first, to_second, tiles)

    whole = pl.BlockSpec(memory_space=pltpu.VMEM)
    flat = lambda array: array.reshape(-1, LANES)
    cell = flat(obs_cell)
    cell_row = lax.dynamic_index_in_dim(
        cell.reshape(blocks, tiles, BLOCK, LANES), lax.axis_index("tile"), 1, False
    )
    draft, seen = call(
        functools.partial(draft_body, height=height),
        [(member_concentration.shape, f32), ((blocks, members, BLOCK, LANES), f32)],
        [pltpu.VMEM((blocks, region_rows, LANES), f32)],
        flops=50_000_000,
        specs=[whole, whole, whole, pl.BlockSpec(memory_space=pltpu.HBM)],
    )(member_concentration, courant_pairs, cell_row, to_second)
    forecast, *chunks = call(
        functools.partial(forecast_body, tiles=tiles, height=height),
        [(member_concentration.shape, f32)] + [((chip_rows, LANES), bf16)] * chips,
        [
            pltpu.VMEM((chips, chip_rows, LANES), bf16),
            pltpu.VMEM((blocks, region_rows, LANES), f32),
        ],
    )(
        member_concentration,
        courant_pairs,
        draft,
        seen,
        first,
        second,
        cell_row,
    )
    received = exchange(chunks)
    weights, values = call(
        functools.partial(
            weights_body, tiles=tiles, blocks=blocks, height=height, width=width, side=side
        ),
        [((16, depth * LANES), f32), ((depth, LANES), f32)],
        [pltpu.VMEM((16 * depth, LANES), f32)],
        flops=100_000_000,
    )(obs_list, first, second, cell, flat(obs_value), flat(obs_error))

    sizes = dict(sources=blocks, members=members, region_rows=region_rows)
    tall = patches * ensemble
    length = depth * LANES
    system_shape = (ensemble + 8, tall // 64 * LANES)
    wide_shape = (2 * (ensemble + 8), length)
    centred_shape = (ensemble, levels * BLOCK, LANES)
    share = functools.partial(share_body, region_rows=region_rows)
    mine, theirs = call(share, [((chips * all_rows, LANES), bf16)] * 2)(*received, values)
    theirs = swap_cores(theirs)
    to_first, to_second, wide = call(
        functools.partial(neighbours_body, **sizes),
        [(system_shape, f32), (system_shape, f32), (wide_shape, bf16)],
        [
            pltpu.VMEM(((ensemble + 8) * depth, LANES), f32),
            pltpu.VMEM((2 * tall, length), bf16),
            pltpu.VMEM((2 * tall, length), bf16),
        ],
    )(mine, theirs, weights, values)
    first, second = swap(to_first, to_second, tiles)
    own, centred = call(
        functools.partial(own_body, **sizes),
        [(system_shape, f32), (centred_shape, f32)],
        [pltpu.VMEM((tall, length), bf16), pltpu.VMEM((tall, length), bf16)],
        flops=50_000_000,
    )(mine, theirs, weights, wide)

    changes = call(
        functools.partial(analysis_body, patches=patches, **sizes),
        [((2 * region_rows, LANES), bf16)] * chips,
        [pltpu.VMEM((ensemble, ensemble, LANES), f32)],
    )(own, first, second, centred)
    returned = exchange(changes)
    mine, theirs = call(share, [((chips * region_rows, LANES), bf16)] * 2)(*returned, forecast)
    theirs = swap_cores(theirs)
    (analysis,) = call(output_body, [(forecast.shape, f32)])(forecast, mine, theirs)
    return analysis


def solution(mesh):
    return jax.shard_map(
        shards,
        mesh=mesh,
        in_specs=(
            P("member", None, "tile", None),
            P(None, None, "tile", None),
            P(),
            P(),
            P(),
            P("tile", "member", None),
        ),
        out_specs=P("member", None, "tile", None),
        check_vma=False,
    )
```
